32 devices in a mesh: ep: 16 (over z, y, core), tp: 2 (over x).
Axes of the slice: x: 2, y: 2, z: 4, core: 2. Of those that a mesh axis runs over, the one named last changes fastest.
Arguments:
- tokens: bfloat16 [2048, 2048], P('ep'), may hold values from -6 to 6
- expert_ids: int32 [2048, 8], P('ep'), may hold values from 0 to 31, all different within a row; in each aligned block of 128 rows (0 to 127, 128 to 255, ...) at most 48 rows name the same one
- combine: float32 [2048, 8], P('ep'), may hold values from 0.05 to 0.5
- cotangent: bfloat16 [2048, 2048], P('ep'), may hold values from -6 to 6
- old_layout: int32 [32], replicated, may hold values from 0 to 31, each once
- pair_moves: int32 [16], replicated, may hold values from 0 to 1, as said below
- gate_w: bfloat16 [32, 2048, 768], P('ep', None, 'tp'), may hold values from -0.125 to 0.125
- up_w: bfloat16 [32, 2048, 768], P('ep', None, 'tp'), may hold values from -0.125 to 0.125
- down_w: bfloat16 [32, 768, 2048], P('ep', 'tp'), may hold values from -0.21875 to 0.21875
Outputs:
- mixed: bfloat16 [2048, 2048], P('ep', 'tp')
- d_tokens: bfloat16 [2048, 2048], P('ep', 'tp')
- d_combine: float32 [2048, 8], P('ep')
- grad_gate: bfloat16 [32, 2048, 768], P('ep', None, 'tp')
- grad_up: bfloat16 [32, 2048, 768], P('ep', None, 'tp')
- grad_down: bfloat16 [32, 768, 2048], P('ep', 'tp')
The draws below stay inside these ranges and needn't reach their ends.
Inputs may be any that keep to these rules, and one draw needn't show every extreme that they name: `expert_ids`: among the 128 tokens of one ep index no expert is named more than 48 times, a bound that some block reaches. `old_layout`: A permutation of the experts. pair_moves[q] = pair_moves[q + 8]; at least one pair moves.
All inputs are finite; a program needn't handle non-finite values.
Results may differ from the reference program's by a relative error of at most 0.008.
Values may be sent and summed in bfloat16 or wider, within the bound.
No kernel may reach another device: no remote copies, remote signals or barrier semaphores. Data moves between devices by JAX's collectives and lax.ppermute only.
A program may use at most 192 MiB of HBM per device.

```python
import math
import jax
import jax.numpy as jnp
import numpy as np
from jax import lax

D = 2048
FF = 768
TOP = 8
EXP_DEV = 2
TOK_DEV = 128
EXPERTS = 32
PAIRS = 8
CAP = 48
TOKENS = 2048
N_EP = 16


def draw_pair_moves(key, part):
    lower = jax.random.randint(key, (PAIRS,), 0, 2)
    chosen = jax.random.randint(jax.random.fold_in(key, 7), (), 0, PAIRS)
    lower = jnp.where(jnp.arange(PAIRS) == chosen, 1, lower)
    return jnp.concatenate([lower, lower]).astype(jnp.int32)


def block_scale(rng, dims, pieces, low, high):
    gain = 1.0
    for axis_at, parts in pieces:
        steps = jax.random.uniform(jax.random.fold_in(jax.random.fold_in(rng, 6), axis_at), (parts,), jnp.float32, low / len(pieces), high / len(pieces))
        gain = gain * jnp.repeat(jnp.exp(steps), dims[axis_at] // parts).reshape((-1,) + (1,) * (len(dims) - 1 - axis_at))
    return gain


def assign_block(key, own, number, rows, count, top, limit, slope):
    order = jax.random.permutation(key, count)
    packed, ordinary = portions_of(count, rows * top, limit, slope, True), portions_of(count, rows * top, limit, slope, False)
    places = jnp.arange(count)

    def named(sizes, offset_by):
        used = int((sizes > 0).sum())
        fixed = max(1, used // 4)
        shifted = fixed + (places - fixed + offset_by * (used - fixed)) % max(1, count - fixed)
        return jnp.zeros((count,), jnp.int32).at[order[jnp.where(places < fixed, places, shifted)]].set(jnp.asarray(sizes, jnp.int32))

    sizes = jnp.where(number % 4 == 0, named(packed, number // 4), named(ordinary, number - number // 4 - 1))
    mixed = jax.random.permutation(jax.random.fold_in(own, 3), count)
    giver, sink = mixed[0:count // 2 * 2:2], mixed[1:count // 2 * 2:2]
    margin = jnp.minimum(sizes[giver] - 1, limit - sizes[sink]) // 2
    margin = jnp.where((giver == order[0]) | (sink == order[0]) | (sizes[sink] == 0), 0, jnp.maximum(margin, 0))
    shifted = jax.random.randint(jax.random.fold_in(own, 4), (count // 2,), 0, 1 << 20) % (margin + 1)
    sizes = sizes.at[giver].add(-shifted).at[sink].add(shifted)
    items = jnp.searchsorted(jnp.cumsum(sizes), jnp.arange(rows * top), side="right").astype(jnp.int32)
    table = items.reshape(top, rows).T
    table = table[jax.random.permutation(jax.random.fold_in(own, 1), rows)]
    offset_by = jax.random.randint(jax.random.fold_in(own, 2), (rows, 1), 0, top)
    return jnp.take_along_axis(table, (jnp.arange(top)[None, :] + offset_by) % top, axis=1)


def portions_of(number_of, total, reach, skew, full):
    portions = [(1 << 20) // math.isqrt(rank ** skew) + 1 for rank in range(1, number_of + 1)]
    largest = reach if full else min(reach, max(-(-total // number_of), total * portions[0] // sum(portions)))
    least = 1 if total - largest >= number_of - 1 else 0
    counts, surplus = [largest] + [least] * (number_of - 1), total - largest - least * (number_of - 1)
    while surplus > 0:
        candidates = [i for i in range(1, number_of) if counts[i] < largest] or [i for i in range(1, number_of) if counts[i] < reach]
        whole, left = sum([portions[i] for i in candidates]), surplus
        for i in candidates:
            extra = min(reach - counts[i], max(1, left * portions[i] // whole), surplus)
            counts[i] = counts[i] + extra
            surplus = surplus - extra
    return np.array(counts)


def bell_draw(own_key, shape, deviation, bound, shards=(), kind=jnp.bfloat16):
    gain = block_scale(own_key, shape, shards, -0.22, 0.18) if shards else 1.0
    values = jax.random.normal(own_key, shape, jnp.float32) * deviation * gain
    return jnp.minimum(jnp.maximum(values, -bound), bound).astype(kind)


def setup_inputs(seed: int = 0) -> dict:
    key_of = jax.random.split(jax.random.key(seed), 10)
    tokens = bell_draw(key_of[0], (TOKENS, D), 1.0, 6.0, ((0, 16),))
    expert_ids_keys = jax.random.split(jax.random.fold_in(key_of[1], 1), TOKENS // TOK_DEV)
    expert_ids_turns = jax.random.permutation(jax.random.fold_in(key_of[1], 3), TOKENS // TOK_DEV)
    expert_ids = jax.vmap(lambda own, number: assign_block(jax.random.fold_in(key_of[1], 2), own, number, TOK_DEV, EXPERTS, TOP, CAP, 2))(expert_ids_keys, expert_ids_turns).reshape((TOKENS, TOP))
    combine = jnp.clip(jnp.exp(math.log(0.5) - 2.3025851 * jax.random.uniform(key_of[2], (TOKENS, TOP), jnp.float32) ** block_scale(key_of[2], (TOKENS, TOP), ((0, 16),), -0.2, 0.2)), 0.05, 0.5)
    cotangent = bell_draw(key_of[3], (TOKENS, D), 1.0, 6.0, ((0, 16),))
    old_layout = jax.random.permutation(key_of[4], EXPERTS).astype(jnp.int32)
    pair_moves = draw_pair_moves(jax.random.fold_in(key_of[9], 71), 0)
    gate_w = bell_draw(key_of[6], (EXPERTS, D, FF), D ** -0.5, 0.125, ((0, 16), (2, 2)))
    up_w = bell_draw(key_of[7], (EXPERTS, D, FF), D ** -0.5, 0.125, ((0, 16), (2, 2)))
    down_w = bell_draw(key_of[8], (EXPERTS, FF, D), FF ** -0.5, 0.21875, ((0, 16), (1, 2)))
    return {"tokens": tokens, "expert_ids": expert_ids, "combine": combine, "cotangent": cotangent, "old_layout": old_layout, "pair_moves": pair_moves, "gate_w": gate_w, "up_w": up_w, "down_w": down_w}


def expert_pass(rows_in, rows_grad, w_gate, w_up, w_down):
    gate = jnp.dot(rows_in, w_gate, preferred_element_type=jnp.float32)
    upper = jnp.dot(rows_in, w_up, preferred_element_type=jnp.float32)
    sigma = jax.nn.sigmoid(gate)
    active = gate * sigma
    hidden = (active * upper).astype(jnp.bfloat16)
    result = jnp.dot(hidden, w_down, preferred_element_type=jnp.float32).astype(jnp.bfloat16)
    d_hidden = jnp.dot(rows_grad, w_down.T, preferred_element_type=jnp.float32)
    d_gate = (d_hidden * upper * sigma * (1.0 + gate * (1.0 - sigma))).astype(jnp.bfloat16)
    d_up = (d_hidden * active).astype(jnp.bfloat16)
    d_rows = (jnp.dot(d_gate, w_gate.T, preferred_element_type=jnp.float32)
              + jnp.dot(d_up, w_up.T, preferred_element_type=jnp.float32)).astype(jnp.bfloat16)
    g_gate = jnp.dot(rows_in.T, d_gate, preferred_element_type=jnp.float32).astype(jnp.bfloat16)
    g_up = jnp.dot(rows_in.T, d_up, preferred_element_type=jnp.float32).astype(jnp.bfloat16)
    g_down = jnp.dot(hidden.T, rows_grad, preferred_element_type=jnp.float32).astype(jnp.bfloat16)
    return result, d_rows, g_gate, g_up, g_down


def reference(tokens, expert_ids, combine, cotangent, old_layout, pair_moves, gate_w, up_w, down_w):
    slot_ids = jnp.arange(EXPERTS, dtype=jnp.int32)
    slot_device = slot_ids // EXP_DEV
    slot_local = slot_ids % EXP_DEV
    moved = (slot_local == EXP_DEV - 1) & (pair_moves[slot_device] == 1)
    source_slot = jnp.where(moved, ((slot_device + PAIRS) % N_EP) * EXP_DEV + slot_local, slot_ids).astype(jnp.int32)
    new_layout = old_layout[source_slot]
    old_slot = jnp.zeros((EXPERTS,), jnp.int32).at[old_layout].set(slot_ids)
    blocks = expert_ids.reshape(N_EP, TOK_DEV * TOP)
    onehot = (blocks[..., None] == slot_ids[None, None, :]).astype(jnp.int32)
    before = jnp.cumsum(onehot, axis=1) - onehot
    position = jnp.sum(before * onehot, axis=-1).reshape(-1).astype(jnp.int32)
    flat_index = jnp.arange(TOKENS * TOP, dtype=jnp.int32)
    source_block = flat_index // (TOK_DEV * TOP)
    row_index = (source_block * CAP + position).astype(jnp.int32)
    token_of = flat_index // TOP
    expert_of = expert_ids.reshape(-1)
    rows_in = jnp.zeros((EXPERTS, N_EP * CAP, D), jnp.bfloat16).at[expert_of, row_index].set(tokens[token_of])
    grad_vals = (combine.reshape(-1)[:, None] * cotangent[token_of].astype(jnp.float32)).astype(jnp.bfloat16)
    rows_grad = jnp.zeros((EXPERTS, N_EP * CAP, D), jnp.bfloat16).at[expert_of, row_index].set(grad_vals)

    def one_expert(inputs):
        expert, x_rows, g_rows = inputs
        slot = old_slot[expert]
        return expert_pass(x_rows, g_rows, gate_w[slot], up_w[slot], down_w[slot])

    outputs, d_rows, g_gate, g_up, g_down = lax.map(one_expert, (slot_ids, rows_in, rows_grad))
    picked = outputs[expert_of, row_index].reshape(TOKENS, TOP, D)
    picked_grad = d_rows[expert_of, row_index].reshape(TOKENS, TOP, D)
    cot_float = cotangent.astype(jnp.float32)
    mixed = jnp.zeros((TOKENS, D), jnp.float32)
    d_tokens = jnp.zeros((TOKENS, D), jnp.float32)
    columns = []
    for choice_k in range(TOP):
        value_k = picked[:, choice_k].astype(jnp.float32)
        mixed = mixed + combine[:, choice_k][:, None] * value_k
        d_tokens = d_tokens + picked_grad[:, choice_k].astype(jnp.float32)
        columns.append(jnp.sum(cot_float * value_k, axis=-1))
    d_combine = jnp.stack(columns, axis=1)
    return (mixed.astype(jnp.bfloat16), d_tokens.astype(jnp.bfloat16), d_combine,
            g_gate[new_layout], g_up[new_layout], g_down[new_layout])
```

```python
import jax
import jax.numpy as jnp
import numpy as np
from jax import lax
from jax.sharding import PartitionSpec as P

F32 = jnp.float32
BF16 = jnp.bfloat16


def ring_order(chips):
    return list(range(0, chips, 2)) + list(range(chips - 1, 0, -2))


def ring_pairs(order, hop):
    chips = len(order)
    return [
        (chip * 2 + core, order[(place + hop) % chips] * 2 + core)
        for place, chip in enumerate(order)
        for core in range(2)
    ]


def block_tables(order):
    chips = len(order)
    half = chips // 2
    hops = [0] + [hop for step in range(1, half) for hop in (-step, step)] + [half]
    ep_count = 2 * chips
    arrival = np.zeros((ep_count, ep_count), np.int32)
    for place, chip in enumerate(order):
        for core in range(2):
            arrival[chip * 2 + core] = [
                order[(place + hop) % chips] * 2 + (core ^ side) for hop in hops for side in range(2)
            ]
    spot = np.argsort(arrival, axis=1).astype(np.int32)
    partner = np.arange(ep_count) ^ (ep_count // 2)
    from_partner = np.take_along_axis(spot[partner], arrival, axis=1).astype(np.int32)
    return arrival, spot, from_partner


def dot(a, b, ca, cb):
    return lax.dot_general(a, b, (((ca,), (cb,)), ((), ())), preferred_element_type=F32)


def gather_body(tokens, expert_ids, combine, cotangent, old_layout, pair_moves, gate_w, up_w, down_w):
    ep_count = lax.axis_size("ep")
    tp_count = lax.axis_size("tp")
    tok_count, top_k = expert_ids.shape
    expert_count = old_layout.shape[0]
    per_device, width, units = gate_w.shape
    share = width // tp_count
    capacity = 3 * tok_count * top_k // (2 * expert_count)
    chips = ep_count // 2
    half = chips // 2
    order = ring_order(chips)
    forward, backward = ring_pairs(order, 1), ring_pairs(order, -1)
    other_core = [(i, i ^ 1) for i in range(ep_count)]
    other_share = [(i, i ^ 1) for i in range(tp_count)]
    partners = [(i, i ^ (ep_count // 2)) for i in range(ep_count)]
    me = lax.axis_index("ep")
    my_share = lax.axis_index("tp")
    arrival, spot, from_partner = (jnp.asarray(table)[me] for table in block_tables(order))

    meta = lax.all_gather(
        jnp.concatenate([expert_ids.astype(F32), combine], axis=1), "ep", axis=0, tiled=False
    )
    meta = jnp.take(meta, arrival, axis=0)
    ids = meta[:, :, :top_k].astype(jnp.int32)
    weights = meta[:, :, top_k:]
    my_move = pair_moves[me] == 1
    last = per_device - 1
    experts = lax.dynamic_slice_in_dim(old_layout, me * per_device, per_device, 0)
    partner_last = old_layout[(me ^ (ep_count // 2)) * per_device + last]
    new_last = jnp.where(my_move, partner_last, experts[last])
    chosen = ids[:, :, None, :] == experts[None, None, :, None]
    scale = jnp.sum(jnp.where(chosen, weights[:, :, None, :], 0.0), axis=3)
    earlier = (jnp.arange(tok_count)[:, None] < jnp.arange(tok_count)[None, :]).astype(BF16)

    def rows_of(expert):
        named = jnp.any(ids == expert, axis=2)
        position = jnp.dot(named.astype(BF16), earlier, preferred_element_type=F32).astype(jnp.int32)
        wanted = jnp.arange(capacity, dtype=jnp.int32)[None, :, None]
        return ((position[:, None, :] == wanted) & named[:, None, :]).astype(BF16)

    both = per_device * units
    w_in = jnp.concatenate([gate_w[l] for l in range(per_device)] + [up_w[l] for l in range(per_device)], axis=1)
    w_out = down_w.reshape(both, width)
    mine_at, other_at = my_share * share, (1 - my_share) * share
    w_in_mine = lax.dynamic_slice_in_dim(w_in, mine_at, share, 0)
    w_in_other = lax.dynamic_slice_in_dim(w_in, other_at, share, 0)
    w_out_mine = lax.dynamic_slice_in_dim(w_out, mine_at, share, 1)
    w_out_other = lax.dynamic_slice_in_dim(w_out, other_at, share, 1)

    def group_pass(pieces, first):
        near = jnp.stack(pieces)
        far = lax.ppermute(near, "ep", other_core)
        count = len(pieces)
        group = jnp.stack([near, far], axis=1).reshape(count * 2 * tok_count, 2 * width)
        x, cot = group[:, :width], group[:, width:]
        gains = scale[first : first + 2 * count].reshape(-1, per_device)
        gains_wide = jnp.repeat(gains, units, axis=1)
        projected = dot(x, w_in, 1, 0)
        pulled = dot(cot, w_out, 1, 1)
        gate, upper = projected[:, :both], projected[:, both:]
        sigma = jax.nn.sigmoid(gate)
        active = gate * sigma
        hidden = active * upper
        d_combine_part = jnp.sum((hidden * pulled).reshape(-1, per_device, units), axis=2)
        d_hidden = pulled * gains_wide
        hidden = (hidden * gains_wide).astype(BF16)
        d_gate = (d_hidden * upper * sigma * (1.0 + gate * (1.0 - sigma))).astype(BF16)
        d_up = (d_hidden * active).astype(BF16)
        d_in = jnp.concatenate([d_gate, d_up], axis=1)

        def partial_sum(w_o, w_i):
            out = dot(hidden, w_o, 1, 0).astype(BF16)
            back = dot(d_in, w_i, 1, 1).astype(BF16)
            value = jnp.concatenate([out, back], axis=1).reshape(count, 2, tok_count, 2 * share)
            arrived = lax.ppermute(value[:, 1], "ep", other_core)
            return value[:, 0].astype(F32) + arrived.astype(F32)

        sent = partial_sum(w_out_other, w_in_other).astype(BF16)
        arrived = lax.ppermute(sent, "tp", other_share)
        total = partial_sum(w_out_mine, w_in_mine) + arrived.astype(F32)
        return x, cot, hidden, d_gate, d_up, d_combine_part, total.astype(BF16)

    both_in = jnp.concatenate([tokens, cotangent], axis=1)
    groups = [group_pass([both_in], 0)]
    right, left = both_in, both_in
    for step in range(1, half):
        right = lax.ppermute(right, "ep", forward)
        left = lax.ppermute(left, "ep", backward)
        groups.append(group_pass([right, left], 4 * step - 2))
    right = lax.ppermute(right[:, :width], "ep", forward)
    left = lax.ppermute(left[:, width:], "ep", backward)
    groups.append(group_pass([jnp.concatenate([right, left], axis=1)], 4 * half - 2))

    x, cot, hidden, d_gate, d_up, d_combine_part = (
        jnp.concatenate([group[i] for group in groups], axis=0) for i in range(6)
    )
    totals = {0: groups[0][6][0], half: groups[half][6][0]}
    for step in range(1, half):
        totals[-step], totals[step] = groups[step][6][0], groups[step][6][1]

    up_sum, down_sum = totals[half][:, :share], totals[half][:, share:]
    up_sum = jnp.pad(lax.ppermute(up_sum, "ep", forward).astype(F32), ((0, 0), (0, share)))
    down_sum = jnp.pad(lax.ppermute(down_sum, "ep", backward).astype(F32), ((0, 0), (share, 0)))
    for step in range(half - 1, 0, -1):
        up_sum = (totals[step].astype(F32) + up_sum).astype(BF16)
        down_sum = (totals[-step].astype(F32) + down_sum).astype(BF16)
        up_sum = lax.ppermute(up_sum, "ep", forward).astype(F32)
        down_sum = lax.ppermute(down_sum, "ep", backward).astype(F32)
    home = (totals[0].astype(F32) + up_sum + down_sum).astype(BF16)
    mixed, d_tokens = home[:, :share], home[:, share:]

    spread = jnp.sum(jnp.where(chosen, d_combine_part.reshape(ep_count, tok_count, per_device)[..., None], 0.0), axis=2)
    spread = jnp.take(spread, spot, axis=0).reshape(ep_count * tok_count, top_k)
    d_combine = lax.psum(lax.psum_scatter(spread, "ep", scatter_dimension=0, tiled=True), "tp")

    tail = slice(last * units, (last + 1) * units)
    packed = jnp.concatenate([hidden[:, tail], d_gate[:, tail], d_up[:, tail]], axis=1)
    packed = packed.reshape(ep_count, tok_count, 3 * units)
    packed = jnp.einsum("brt,btf->brf", rows_of(experts[last]), packed, preferred_element_type=F32).astype(BF16)
    swapped = jnp.take(lax.ppermute(packed, "ep", partners), from_partner, axis=0)
    packed = jnp.where(my_move, swapped, packed)
    spread_rows = jnp.einsum("brt,brf->btf", rows_of(new_last), packed, preferred_element_type=F32).astype(BF16)
    spread_rows = spread_rows.reshape(ep_count * tok_count, 3 * units)

    def grads(left_side, own, moved):
        parts = [left_side(own[:, l * units : (l + 1) * units]) for l in range(last)] + [left_side(moved)]
        return jnp.stack(parts)

    grad_gate = grads(lambda v: dot(x, v, 0, 0).astype(BF16), d_gate, spread_rows[:, units : 2 * units])
    grad_up = grads(lambda v: dot(x, v, 0, 0).astype(BF16), d_up, spread_rows[:, 2 * units :])
    grad_down = grads(lambda v: dot(v, cot, 0, 0).astype(BF16), hidden, spread_rows[:, :units])
    return (mixed, d_tokens, d_combine, grad_gate, grad_up, grad_down)


def exchange_halves(value, axis, distance):
    mask = 2**distance
    pairs = [(source, source ^ mask) for source in range(lax.axis_size(axis))]
    return lax.ppermute(value, axis, pairs)


def dispatch_body(tokens, expert_ids, combine, cotangent, old_layout, pair_moves, gate_w, up_w, down_w):
    ep_count = lax.axis_size("ep")
    tp_count = lax.axis_size("tp")
    tok_count, top_k = expert_ids.shape
    expert_count = old_layout.shape[0]
    per_device = gate_w.shape[0]
    model_width = tokens.shape[1]
    share_width = model_width // tp_count
    capacity = 3 * tok_count * top_k // (2 * expert_count)
    pair_count = ep_count // 2
    swap_bit = ep_count.bit_length() - 2
    my_index = lax.axis_index("ep")
    my_share = lax.axis_index("tp")
    my_move = pair_moves[my_index] == 1
    slot_ids = jnp.arange(expert_count, dtype=jnp.int32)
    slot_device = slot_ids // per_device
    slot_local = slot_ids % per_device
    moved = (slot_local == per_device - 1) & (pair_moves[slot_device] == 1)
    source_slot = jnp.where(
        moved, (slot_device + pair_count) % ep_count * per_device + slot_local, slot_ids
    )
    new_layout = jnp.sum(
        jnp.where(source_slot[:, None] == slot_ids[None, :], old_layout[None, :], 0), axis=1
    )
    w_gate, w_up, w_down = (gate_w, up_w, down_w)
    arrived = exchange_halves(
        (gate_w[per_device - 1], up_w[per_device - 1], down_w[per_device - 1]), "ep", swap_bit
    )
    w_gate = jnp.concatenate(
        [gate_w[:-1], jnp.where(my_move, arrived[0], gate_w[-1])[None]], axis=0
    )
    w_up = jnp.concatenate([up_w[:-1], jnp.where(my_move, arrived[1], up_w[-1])[None]], axis=0)
    w_down = jnp.concatenate(
        [down_w[:-1], jnp.where(my_move, arrived[2], down_w[-1])[None]], axis=0
    )
    slot_of = jnp.sum(
        jnp.where(new_layout[None, :] == slot_ids[:, None], slot_ids[None, :], 0), axis=1
    )
    flat_ids = expert_ids.reshape(-1)
    onehot = (flat_ids[:, None] == slot_ids[None, :]).astype(jnp.int32)
    before = jnp.cumsum(onehot, axis=0) - onehot
    position = jnp.sum(before * onehot, axis=1)
    target_slot = jnp.sum(onehot * slot_of[None, :], axis=1)
    target_device = target_slot // per_device
    target_local = target_slot % per_device
    row_index = target_local * (ep_count * capacity) + target_device * capacity + position
    rows_total = expert_count * capacity
    matches = jnp.arange(rows_total, dtype=jnp.int32)[:, None] == row_index[None, :]
    select = jnp.sum(
        matches.reshape(rows_total, tok_count, top_k).astype(jnp.int32), axis=2
    ).astype(jnp.bfloat16)
    row_weight = jnp.sum(jnp.where(matches, combine.reshape(-1)[None, :], 0.0), axis=1)

    def dispatch(source, scaling):
        portion = lax.dynamic_slice_in_dim(source, my_share * share_width, share_width, 1)
        picked = jnp.dot(select, portion, preferred_element_type=jnp.float32)
        if scaling is not None:
            picked = picked * scaling[:, None]
        buffer = picked.astype(jnp.bfloat16).reshape(per_device, ep_count * capacity, share_width)
        landed = lax.all_to_all(buffer, "ep", split_axis=1, concat_axis=1, tiled=True)
        return lax.all_gather(landed, "tp", axis=2, tiled=True)

    def send_back(partial_value):
        shares = lax.psum_scatter(partial_value, "tp", scatter_dimension=2, tiled=True).astype(
            jnp.bfloat16
        )
        returned = lax.all_to_all(shares, "ep", split_axis=1, concat_axis=1, tiled=True)
        return returned.reshape(rows_total, share_width)[row_index].reshape(
            tok_count, top_k, share_width
        )

    rows_in = dispatch(tokens, None)
    gate = jnp.einsum("erd,edf->erf", rows_in, w_gate, preferred_element_type=jnp.float32)
    upper = jnp.einsum("erd,edf->erf", rows_in, w_up, preferred_element_type=jnp.float32)
    sigma = jax.nn.sigmoid(gate)
    active = gate * sigma
    hidden = (active * upper).astype(jnp.bfloat16)
    out_part = jnp.einsum("erf,efd->erd", hidden, w_down, preferred_element_type=jnp.float32)
    out_rows = send_back(out_part).astype(jnp.float32)
    mixed = jnp.einsum("tk,tkd->td", combine, out_rows).astype(jnp.bfloat16)
    cot_share = lax.dynamic_slice_in_dim(cotangent, my_share * share_width, share_width, 1).astype(
        jnp.float32
    )
    combine_part = jnp.einsum("td,tkd->tk", cot_share, out_rows)
    d_combine = lax.psum(combine_part, "tp")
    rows_grad = dispatch(cotangent, row_weight)
    d_hidden = jnp.einsum("erd,efd->erf", rows_grad, w_down, preferred_element_type=jnp.float32)
    d_gate = (d_hidden * upper * sigma * (1.0 + gate * (1.0 - sigma))).astype(jnp.bfloat16)
    d_up = (d_hidden * active).astype(jnp.bfloat16)
    back_part = jnp.einsum(
        "erf,edf->erd", d_gate, w_gate, preferred_element_type=jnp.float32
    ) + jnp.einsum("erf,edf->erd", d_up, w_up, preferred_element_type=jnp.float32)
    back_rows = send_back(back_part)
    d_tokens = jnp.sum(back_rows.astype(jnp.float32), axis=1).astype(jnp.bfloat16)
    grad_gate = jnp.einsum(
        "erd,erf->edf", rows_in, d_gate, preferred_element_type=jnp.float32
    ).astype(jnp.bfloat16)
    grad_up = jnp.einsum("erd,erf->edf", rows_in, d_up, preferred_element_type=jnp.float32).astype(
        jnp.bfloat16
    )
    grad_down = jnp.einsum(
        "erf,erd->efd", hidden, rows_grad, preferred_element_type=jnp.float32
    ).astype(jnp.bfloat16)
    return (mixed, d_tokens, d_combine, grad_gate, grad_up, grad_down)


def body(*operands):
    expert_ids, old_layout = operands[1], operands[4]
    tok_count, top_k = expert_ids.shape
    ep_count = lax.axis_size("ep")
    rows = 3 * tok_count * top_k * ep_count // (2 * old_layout.shape[0]) * operands[6].shape[0]
    return (gather_body if ep_count * tok_count <= 2 * rows else dispatch_body)(*operands)


def solution(mesh):
    return jax.shard_map(
        body,
        mesh=mesh,
        in_specs=(
            P("ep", None),
            P("ep", None),
            P("ep", None),
            P("ep", None),
            P(),
            P(),
            P("ep", None, "tp"),
            P("ep", None, "tp"),
            P("ep", "tp", None),
        ),
        out_specs=(
            P("ep", "tp"),
            P("ep", "tp"),
            P("ep", None),
            P("ep", None, "tp"),
            P("ep", None, "tp"),
            P("ep", "tp", None),
        ),
        check_vma=False,
    )
```

```python
import jax
import jax.numpy as jnp
import numpy as np
from jax import lax
from jax.sharding import PartitionSpec as P

F32 = jnp.float32
BF16 = jnp.bfloat16


def ring_order(chips):
    return list(range(0, chips, 2)) + list(range(chips - 1, 0, -2))


def ring_pairs(order, hop):
    chips = len(order)
    return [
        (chip * 2 + core, order[(place + hop) % chips] * 2 + core)
        for place, chip in enumerate(order)
        for core in range(2)
    ]


def block_tables(order):
    chips = len(order)
    half = chips // 2
    hops = [0] + [hop for step in range(1, half) for hop in (-step, step)] + [half]
    ep_count = 2 * chips
    arrival = np.zeros((ep_count, ep_count), np.int32)
    for place, chip in enumerate(order):
        for core in range(2):
            arrival[chip * 2 + core] = [
                order[(place + hop) % chips] * 2 + (core ^ side) for hop in hops for side in range(2)
            ]
    spot = np.argsort(arrival, axis=1).astype(np.int32)
    partner = np.arange(ep_count) ^ (ep_count // 2)
    from_partner = np.take_along_axis(spot[partner], arrival, axis=1).astype(np.int32)
    return arrival, spot, from_partner


def dot(a, b, ca, cb):
    return lax.dot_general(a, b, (((ca,), (cb,)), ((), ())), preferred_element_type=F32)


def gather_body(tokens, expert_ids, combine, cotangent, old_layout, pair_moves, gate_w, up_w, down_w):
    ep_count = lax.axis_size("ep")
    tp_count = lax.axis_size("tp")
    tok_count, top_k = expert_ids.shape
    expert_count = old_layout.shape[0]
    per_device, width, units = gate_w.shape
    share = width // tp_count
    capacity = 3 * tok_count * top_k // (2 * expert_count)
    chips = ep_count // 2
    half = chips // 2
    order = ring_order(chips)
    forward, backward = ring_pairs(order, 1), ring_pairs(order, -1)
    other_core = [(i, i ^ 1) for i in range(ep_count)]
    other_share = [(i, i ^ 1) for i in range(tp_count)]
    partners = [(i, i ^ (ep_count // 2)) for i in range(ep_count)]
    me = lax.axis_index("ep")
    my_share = lax.axis_index("tp")
    arrival, spot, from_partner = (jnp.asarray(table)[me] for table in block_tables(order))

    my_move = pair_moves[me] == 1
    last = per_device - 1
    experts = lax.dynamic_slice_in_dim(old_layout, me * per_device, per_device, 0)
    partner_last = old_layout[(me ^ (ep_count // 2)) * per_device + last]
    new_last = jnp.where(my_move, partner_last, experts[last])
    earlier = (jnp.arange(tok_count)[:, None] < jnp.arange(tok_count)[None, :]).astype(BF16)

    def rows_of(expert, ids):
        named = jnp.any(ids == expert, axis=2)
        position = jnp.dot(named.astype(BF16), earlier, preferred_element_type=F32).astype(jnp.int32)
        wanted = jnp.arange(capacity, dtype=jnp.int32)[None, :, None]
        return ((position[:, None, :] == wanted) & named[:, None, :]).astype(BF16)

    both = per_device * units
    w_in = jnp.concatenate([gate_w[l] for l in range(per_device)] + [up_w[l] for l in range(per_device)], axis=1)
    w_out = down_w.reshape(both, width)
    mine_at, other_at = my_share * share, (1 - my_share) * share
    w_in_mine = lax.dynamic_slice_in_dim(w_in, mine_at, share, 0)
    w_in_other = lax.dynamic_slice_in_dim(w_in, other_at, share, 0)
    w_out_mine = lax.dynamic_slice_in_dim(w_out, mine_at, share, 1)
    w_out_other = lax.dynamic_slice_in_dim(w_out, other_at, share, 1)

    parts = []
    rest = combine
    for _ in range(3):
        parts.append(lax.reduce_precision(rest, 8, 7))
        rest = rest - parts[-1]
    id_parts = [expert_ids // 256, expert_ids % 256]
    notes = jnp.concatenate([part.astype(BF16) for part in id_parts + parts], axis=1)
    notes = jnp.pad(notes, ((0, 0), (0, -notes.shape[1] % 128)))
    payload = jnp.concatenate([tokens, cotangent, notes], axis=1)

    def compute(pieces):
        near = jnp.concatenate(pieces)
        far = lax.ppermute(near, "ep", other_core)
        count = len(pieces)
        near, far = near.reshape(count, tok_count, -1), far.reshape(count, tok_count, -1)
        group = jnp.stack([near, far], axis=1).reshape(count * 2 * tok_count, -1)
        x, cot, said = group[:, :width], group[:, width : 2 * width], group[:, 2 * width :].astype(F32)
        columns = [said[:, i * top_k : (i + 1) * top_k] for i in range(5)]
        ids = (columns[0] * 256 + columns[1]).astype(jnp.int32)
        weights = columns[2] + (columns[3] + columns[4])
        gains = [
            jnp.sum(jnp.where(ids == experts[l], weights, 0.0), axis=1, keepdims=True) for l in range(per_device)
        ]
        gains_wide = jnp.concatenate([jnp.broadcast_to(gain, (gain.shape[0], units)) for gain in gains], axis=1)
        projected = dot(x, w_in, 1, 0)
        pulled = dot(cot, w_out, 1, 1)
        gate, upper = projected[:, :both], projected[:, both:]
        sigma = jax.nn.sigmoid(gate)
        active = gate * sigma
        hidden = active * upper
        traded = hidden * pulled
        d_weights = sum(
            jnp.where(
                ids == experts[l], jnp.sum(traded[:, l * units : (l + 1) * units], axis=1, keepdims=True), 0.0
            )
            for l in range(per_device)
        )
        d_hidden = pulled * gains_wide
        hidden = (hidden * gains_wide).astype(BF16)
        d_gate = (d_hidden * upper * sigma * (1.0 + gate * (1.0 - sigma))).astype(BF16)
        d_up = (d_hidden * active).astype(BF16)
        d_in = jnp.concatenate([d_gate, d_up], axis=1)

        def partial_sum(w_o, w_i):
            out = dot(hidden, w_o, 1, 0).astype(BF16)
            back = dot(d_in, w_i, 1, 1).astype(BF16)
            value = jnp.concatenate([out, back], axis=1).reshape(count, 2, tok_count, 2 * share)
            arrived = lax.ppermute(value[:, 1], "ep", other_core)
            return value[:, 0].astype(F32) + arrived.astype(F32)

        sent = partial_sum(w_out_other, w_in_other).astype(BF16)
        kept = partial_sum(w_out_mine, w_in_mine).astype(BF16)
        ids = ids.reshape(2 * count, tok_count, top_k)
        tail = slice(last * units, (last + 1) * units)
        packed = jnp.concatenate([hidden[:, tail], d_gate[:, tail], d_up[:, tail]], axis=1)
        packed = packed.reshape(2 * count, tok_count, 3 * units)
        packed = jnp.einsum("brt,btf->brf", rows_of(experts[last], ids), packed, preferred_element_type=F32)
        return (x, cot, hidden, d_gate, d_up, d_weights, ids, packed.astype(BF16)), sent, kept

    kept_groups, totals = [], []
    right = left = payload
    pending = None
    for step in range(half + 1):
        pieces = [payload] if step == 0 else [right, left] if step < half else [jnp.concatenate([right, left], axis=1)]
        if step < half - 1:
            right = lax.ppermute(right, "ep", forward)
            left = lax.ppermute(left, "ep", backward)
        elif step == half - 1:
            right = lax.ppermute(right[:, :width], "ep", forward)
            left = lax.ppermute(left[:, width:], "ep", backward)
        if pending is not None:
            arrived = lax.ppermute(pending[0], "tp", other_share)
            totals.append((pending[1].astype(F32) + arrived.astype(F32)).astype(BF16))
        group, sent, kept = compute(pieces)
        right, left, sent, kept, group, totals = lax.optimization_barrier((right, left, sent, kept, group, totals))
        kept_groups.append(group)
        pending = (sent, kept)
    arrived = lax.ppermute(pending[0], "tp", other_share)
    totals.append((pending[1].astype(F32) + arrived.astype(F32)).astype(BF16))

    x, cot, hidden, d_gate, d_up, d_weights, ids, packed = (
        jnp.concatenate([group[i] for group in kept_groups], axis=0) for i in range(8)
    )
    by_hop = {0: totals[0][0], half: totals[half][0]}
    for step in range(1, half):
        by_hop[-step], by_hop[step] = totals[step][0], totals[step][1]

    up_sum, down_sum = by_hop[half][:, :share], by_hop[half][:, share:]
    up_sum = jnp.pad(lax.ppermute(up_sum, "ep", forward).astype(F32), ((0, 0), (0, share)))
    down_sum = jnp.pad(lax.ppermute(down_sum, "ep", backward).astype(F32), ((0, 0), (share, 0)))
    for step in range(half - 1, 0, -1):
        up_sum = (by_hop[step].astype(F32) + up_sum).astype(BF16)
        down_sum = (by_hop[-step].astype(F32) + down_sum).astype(BF16)
        up_sum = lax.ppermute(up_sum, "ep", forward).astype(F32)
        down_sum = lax.ppermute(down_sum, "ep", backward).astype(F32)
    home = (by_hop[0].astype(F32) + up_sum + down_sum).astype(BF16)
    mixed, d_tokens = home[:, :share], home[:, share:]

    d_weights = d_weights + lax.ppermute(d_weights, "tp", other_share)
    d_weights = jnp.take(d_weights.reshape(ep_count, tok_count, top_k), spot, axis=0)
    d_combine = lax.psum_scatter(
        d_weights.reshape(ep_count * tok_count, top_k), "ep", scatter_dimension=0, tiled=True
    )

    swapped = jnp.take(lax.ppermute(packed, "ep", partners), from_partner, axis=0)
    packed = jnp.where(my_move, swapped, packed)
    spread_rows = jnp.einsum("brt,brf->btf", rows_of(new_last, ids), packed, preferred_element_type=F32).astype(BF16)
    spread_rows = spread_rows.reshape(ep_count * tok_count, 3 * units)

    def grads(left_side, own, moved):
        parts = [left_side(own[:, l * units : (l + 1) * units]) for l in range(last)] + [left_side(moved)]
        return jnp.stack(parts)

    grad_gate = grads(lambda v: dot(x, v, 0, 0).astype(BF16), d_gate, spread_rows[:, units : 2 * units])
    grad_up = grads(lambda v: dot(x, v, 0, 0).astype(BF16), d_up, spread_rows[:, 2 * units :])
    grad_down = grads(lambda v: dot(v, cot, 0, 0).astype(BF16), hidden, spread_rows[:, :units])
    return (mixed, d_tokens, d_combine, grad_gate, grad_up, grad_down)


def exchange_halves(value, axis, distance):
    mask = 2**distance
    pairs = [(source, source ^ mask) for source in range(lax.axis_size(axis))]
    return lax.ppermute(value, axis, pairs)


def dispatch_body(tokens, expert_ids, combine, cotangent, old_layout, pair_moves, gate_w, up_w, down_w):
    ep_count = lax.axis_size("ep")
    tp_count = lax.axis_size("tp")
    tok_count, top_k = expert_ids.shape
    expert_count = old_layout.shape[0]
    per_device = gate_w.shape[0]
    model_width = tokens.shape[1]
    share_width = model_width // tp_count
    capacity = 3 * tok_count * top_k // (2 * expert_count)
    pair_count = ep_count // 2
    swap_bit = ep_count.bit_length() - 2
    my_index = lax.axis_index("ep")
    my_share = lax.axis_index("tp")
    my_move = pair_moves[my_index] == 1
    slot_ids = jnp.arange(expert_count, dtype=jnp.int32)
    slot_device = slot_ids // per_device
    slot_local = slot_ids % per_device
    moved = (slot_local == per_device - 1) & (pair_moves[slot_device] == 1)
    source_slot = jnp.where(
        moved, (slot_device + pair_count) % ep_count * per_device + slot_local, slot_ids
    )
    new_layout = jnp.sum(
        jnp.where(source_slot[:, None] == slot_ids[None, :], old_layout[None, :], 0), axis=1
    )
    w_gate, w_up, w_down = (gate_w, up_w, down_w)
    arrived = exchange_halves(
        (gate_w[per_device - 1], up_w[per_device - 1], down_w[per_device - 1]), "ep", swap_bit
    )
    w_gate = jnp.concatenate(
        [gate_w[:-1], jnp.where(my_move, arrived[0], gate_w[-1])[None]], axis=0
    )
    w_up = jnp.concatenate([up_w[:-1], jnp.where(my_move, arrived[1], up_w[-1])[None]], axis=0)
    w_down = jnp.concatenate(
        [down_w[:-1], jnp.where(my_move, arrived[2], down_w[-1])[None]], axis=0
    )
    slot_of = jnp.sum(
        jnp.where(new_layout[None, :] == slot_ids[:, None], slot_ids[None, :], 0), axis=1
    )
    flat_ids = expert_ids.reshape(-1)
    onehot = (flat_ids[:, None] == slot_ids[None, :]).astype(jnp.int32)
    before = jnp.cumsum(onehot, axis=0) - onehot
    position = jnp.sum(before * onehot, axis=1)
    target_slot = jnp.sum(onehot * slot_of[None, :], axis=1)
    target_device = target_slot // per_device
    target_local = target_slot % per_device
    row_index = target_local * (ep_count * capacity) + target_device * capacity + position
    rows_total = expert_count * capacity
    matches = jnp.arange(rows_total, dtype=jnp.int32)[:, None] == row_index[None, :]
    select = jnp.sum(
        matches.reshape(rows_total, tok_count, top_k).astype(jnp.int32), axis=2
    ).astype(jnp.bfloat16)
    row_weight = jnp.sum(jnp.where(matches, combine.reshape(-1)[None, :], 0.0), axis=1)

    def dispatch(source, scaling):
        portion = lax.dynamic_slice_in_dim(source, my_share * share_width, share_width, 1)
        picked = jnp.dot(select, portion, preferred_element_type=jnp.float32)
        if scaling is not None:
            picked = picked * scaling[:, None]
        buffer = picked.astype(jnp.bfloat16).reshape(per_device, ep_count * capacity, share_width)
        landed = lax.all_to_all(buffer, "ep", split_axis=1, concat_axis=1, tiled=True)
        return lax.all_gather(landed, "tp", axis=2, tiled=True)

    def send_back(partial_value):
        shares = lax.psum_scatter(partial_value, "tp", scatter_dimension=2, tiled=True).astype(
            jnp.bfloat16
        )
        returned = lax.all_to_all(shares, "ep", split_axis=1, concat_axis=1, tiled=True)
        return returned.reshape(rows_total, share_width)[row_index].reshape(
            tok_count, top_k, share_width
        )

    rows_in = dispatch(tokens, None)
    gate = jnp.einsum("erd,edf->erf", rows_in, w_gate, preferred_element_type=jnp.float32)
    upper = jnp.einsum("erd,edf->erf", rows_in, w_up, preferred_element_type=jnp.float32)
    sigma = jax.nn.sigmoid(gate)
    active = gate * sigma
    hidden = (active * upper).astype(jnp.bfloat16)
    out_part = jnp.einsum("erf,efd->erd", hidden, w_down, preferred_element_type=jnp.float32)
    out_rows = send_back(out_part).astype(jnp.float32)
    mixed = jnp.einsum("tk,tkd->td", combine, out_rows).astype(jnp.bfloat16)
    cot_share = lax.dynamic_slice_in_dim(cotangent, my_share * share_width, share_width, 1).astype(
        jnp.float32
    )
    combine_part = jnp.einsum("td,tkd->tk", cot_share, out_rows)
    d_combine = lax.psum(combine_part, "tp")
    rows_grad = dispatch(cotangent, row_weight)
    d_hidden = jnp.einsum("erd,efd->erf", rows_grad, w_down, preferred_element_type=jnp.float32)
    d_gate = (d_hidden * upper * sigma * (1.0 + gate * (1.0 - sigma))).astype(jnp.bfloat16)
    d_up = (d_hidden * active).astype(jnp.bfloat16)
    back_part = jnp.einsum(
        "erf,edf->erd", d_gate, w_gate, preferred_element_type=jnp.float32
    ) + jnp.einsum("erf,edf->erd", d_up, w_up, preferred_element_type=jnp.float32)
    back_rows = send_back(back_part)
    d_tokens = jnp.sum(back_rows.astype(jnp.float32), axis=1).astype(jnp.bfloat16)
    grad_gate = jnp.einsum(
        "erd,erf->edf", rows_in, d_gate, preferred_element_type=jnp.float32
    ).astype(jnp.bfloat16)
    grad_up = jnp.einsum("erd,erf->edf", rows_in, d_up, preferred_element_type=jnp.float32).astype(
        jnp.bfloat16
    )
    grad_down = jnp.einsum(
        "erf,erd->efd", hidden, rows_grad, preferred_element_type=jnp.float32
    ).astype(jnp.bfloat16)
    return (mixed, d_tokens, d_combine, grad_gate, grad_up, grad_down)


def body(*operands):
    expert_ids, old_layout = operands[1], operands[4]
    tok_count, top_k = expert_ids.shape
    ep_count = lax.axis_size("ep")
    rows = 3 * tok_count * top_k * ep_count // (2 * old_layout.shape[0]) * operands[6].shape[0]
    return (gather_body if ep_count * tok_count <= 2 * rows else dispatch_body)(*operands)


def solution(mesh):
    return jax.shard_map(
        body,
        mesh=mesh,
        in_specs=(
            P("ep", None),
            P("ep", None),
            P("ep", None),
            P("ep", None),
            P(),
            P(),
            P("ep", None, "tp"),
            P("ep", None, "tp"),
            P("ep", "tp", None),
        ),
        out_specs=(
            P("ep", "tp"),
            P("ep", "tp"),
            P("ep", None),
            P("ep", None, "tp"),
            P("ep", None, "tp"),
            P("ep", "tp", None),
        ),
        check_vma=False,
    )
```

```python
import functools

import jax
import jax.numpy as jnp
import numpy as np
from jax import lax
from jax.experimental import pallas as pl
from jax.experimental.pallas import tpu as pltpu
from jax.sharding import PartitionSpec as P

F32 = jnp.float32
BF16 = jnp.bfloat16


def ring_order(chips):
    return list(range(0, chips, 2)) + list(range(chips - 1, 0, -2))


def ring_pairs(order, hop):
    chips = len(order)
    return [
        (chip * 2 + core, order[(place + hop) % chips] * 2 + core)
        for place, chip in enumerate(order)
        for core in range(2)
    ]


def block_tables(order):
    chips = len(order)
    half = chips // 2
    groups = [[0]] + [[-step, step] for step in range(1, half)] + [[half]]
    ep_count = 2 * chips
    arrival = np.zeros((ep_count, ep_count), np.int32)
    for place, chip in enumerate(order):
        for core in range(2):
            arrival[chip * 2 + core] = [
                order[(place + hop) % chips] * 2 + (core ^ side)
                for hops in groups
                for side in range(2)
                for hop in hops
            ]
    spot = np.argsort(arrival, axis=1).astype(np.int32)
    partner = np.arange(ep_count) ^ (ep_count // 2)
    from_partner = np.take_along_axis(spot[partner], arrival, axis=1).astype(np.int32)
    return arrival, spot, from_partner


def dot(a, b, ca, cb):
    return lax.dot_general(a, b, (((ca,), (cb,)), ((), ())), preferred_element_type=F32)


def group_kernel(pieces, top_k, capacity, share, facts, *refs):
    x_refs, cot_refs, note_refs = refs[:pieces], refs[pieces : 2 * pieces], refs[2 * pieces : 3 * pieces]
    gate_ref, up_ref, down_ref = refs[3 * pieces : 3 * pieces + 3]
    acts, near_other, near_mine, far_other, far_mine, d_weights, packed, out_sum, back_sum = refs[3 * pieces + 3 :]
    slot, last = pl.program_id(0), pl.num_programs(0) - 1
    x = jnp.concatenate([ref[...] for ref in x_refs], axis=0)
    cot = jnp.concatenate([ref[...] for ref in cot_refs], axis=0)
    said = jnp.concatenate([ref[...] for ref in note_refs], axis=0).astype(F32)
    tok_count = note_refs[0].shape[0]
    lanes = said.shape[1]
    lane = lax.broadcasted_iota(jnp.int32, said.shape, 1)
    chosen = (said.astype(jnp.int32) == facts[1 + slot]) & (lane < top_k)
    weight = pltpu.roll(said, lanes - top_k, 1) + (
        pltpu.roll(said, lanes - 2 * top_k, 1) + pltpu.roll(said, lanes - 3 * top_k, 1)
    )
    gain = jnp.sum(jnp.where(chosen, weight, 0.0), axis=1, keepdims=True)
    w_gate, w_up, w_down = gate_ref[0], up_ref[0], down_ref[0]
    gate, upper = dot(x, w_gate, 1, 0), dot(x, w_up, 1, 0)
    pulled = dot(cot, w_down, 1, 1)
    sigma = jax.nn.sigmoid(gate)
    active = gate * sigma
    hidden = active * upper
    traded = jnp.where(chosen, jnp.sum(hidden * pulled, axis=1, keepdims=True), 0.0)
    d_hidden = pulled * gain
    hidden = (hidden * gain).astype(BF16)
    d_gate = (d_hidden * upper * sigma * (1.0 + gate * (1.0 - sigma))).astype(BF16)
    d_up = (d_hidden * active).astype(BF16)
    act = jnp.concatenate([hidden, d_gate, d_up], axis=1)
    acts[0] = act
    out = dot(hidden, w_down, 1, 0)
    back = dot(d_gate, w_gate, 1, 1) + dot(d_up, w_up, 1, 1)

    @pl.when(slot == 0)
    def _():
        out_sum[...] = out
        back_sum[...] = back
        d_weights[...] = traded

    @pl.when(slot > 0)
    def _():
        out_sum[...] += out
        back_sum[...] += back
        d_weights[...] += traded

    @pl.when(slot == last)
    def _():
        near = pieces // 2 * tok_count
        for value, at in ((out_sum, 0), (back_sum, share)):
            low, high = value[:, :share].astype(BF16), value[:, share:].astype(BF16)
            mine = jnp.where(facts[0] == 0, low, high)
            other = jnp.where(facts[0] == 0, high, low)
            near_other[:, at : at + share] = other[:near]
            near_mine[:, at : at + share] = mine[:near]
            far_other[:, at : at + share] = other[near:]
            far_mine[:, at : at + share] = mine[near:]
        named = jnp.max(jnp.where(chosen, 1.0, 0.0), axis=1, keepdims=True)
        row = lax.broadcasted_iota(jnp.int32, (tok_count, tok_count), 0)
        column = lax.broadcasted_iota(jnp.int32, (tok_count, tok_count), 1)
        earlier = jnp.where(column < row, 1.0, 0.0).astype(BF16)
        for piece in range(pieces):
            rows = slice(piece * tok_count, (piece + 1) * tok_count)
            mask = jnp.broadcast_to(named[rows], (tok_count, tok_count))
            position = dot(earlier, mask.astype(BF16), 1, 0).astype(jnp.int32)
            pick = jnp.where((position == column) & (mask > 0.0), 1.0, 0.0).astype(BF16)
            packed[piece] = dot(pick, act[rows], 0, 0).astype(BF16)[:capacity]


def group_call(x_pieces, cot_pieces, note_pieces, facts, weights, top_k, capacity, share):
    pieces = len(x_pieces)
    gate_w, up_w, down_w = weights
    per_device, width, units = gate_w.shape
    tok_count = x_pieces[0][0].shape[0]
    rows = pieces * tok_count
    lanes = 128

    def columns(piece, size):
        return pl.BlockSpec((tok_count, size), lambda slot, at=piece[1]: (0, at))

    half = rows // 2
    wide = jax.ShapeDtypeStruct((half, 2 * share), BF16)
    whole = pl.BlockSpec((half, 2 * share), lambda slot: (0, 0))
    return pl.pallas_call(
        functools.partial(group_kernel, pieces, top_k, capacity, share),
        grid=(per_device,),
        in_specs=[pl.BlockSpec(memory_space=pltpu.SMEM)]
        + [columns(piece, width) for piece in x_pieces + cot_pieces]
        + [columns(piece, lanes) for piece in note_pieces]
        + [pl.BlockSpec((1,) + w.shape[1:], lambda slot: (slot, 0, 0)) for w in weights],
        out_specs=[pl.BlockSpec((1, rows, 3 * units), lambda slot: (slot, 0, 0))]
        + [whole] * 4
        + [
            pl.BlockSpec((rows, lanes), lambda slot: (0, 0)),
            pl.BlockSpec((pieces, capacity, 3 * units), lambda slot: (0, 0, 0)),
        ],
        out_shape=[jax.ShapeDtypeStruct((per_device, rows, 3 * units), BF16)]
        + [wide] * 4
        + [
            jax.ShapeDtypeStruct((rows, lanes), F32),
            jax.ShapeDtypeStruct((pieces, capacity, 3 * units), BF16),
        ],
        scratch_shapes=[pltpu.VMEM((rows, width), F32)] * 2,
        compiler_params=pltpu.CompilerParams(vmem_limit_bytes=60 * 1024 * 1024),
        cost_estimate=pl.CostEstimate(
            flops=12 * rows * width * units * per_device,
            bytes_accessed=12 * width * units * per_device // 2 + 12 * rows * width,
            transcendentals=rows * units * per_device,
        ),
    )(facts, *[p[0] for p in x_pieces], *[p[0] for p in cot_pieces], *[p[0] for p in note_pieces], *weights)


def gather_body(tokens, expert_ids, combine, cotangent, old_layout, pair_moves, gate_w, up_w, down_w):
    ep_count = lax.axis_size("ep")
    tp_count = lax.axis_size("tp")
    tok_count, top_k = expert_ids.shape
    expert_count = old_layout.shape[0]
    per_device, width, units = gate_w.shape
    share = width // tp_count
    capacity = 3 * tok_count * top_k // (2 * expert_count)
    chips = ep_count // 2
    half = chips // 2
    order = ring_order(chips)
    forward, backward = ring_pairs(order, 1), ring_pairs(order, -1)
    other_core = [(i, i ^ 1) for i in range(ep_count)]
    other_share = [(i, i ^ 1) for i in range(tp_count)]
    partners = [(i, i ^ (ep_count // 2)) for i in range(ep_count)]
    me = lax.axis_index("ep")
    my_share = lax.axis_index("tp")
    arrival, spot, from_partner = (jnp.asarray(table)[me] for table in block_tables(order))

    my_move = pair_moves[me] == 1
    last = per_device - 1
    experts = lax.dynamic_slice_in_dim(old_layout, me * per_device, per_device, 0)
    partner_last = old_layout[(me ^ (ep_count // 2)) * per_device + last]
    new_last = jnp.where(my_move, partner_last, experts[last])
    earlier = (jnp.arange(tok_count)[:, None] < jnp.arange(tok_count)[None, :]).astype(BF16)

    def rows_of(expert, ids):
        named = jnp.any(ids == expert, axis=2)
        position = jnp.dot(named.astype(BF16), earlier, preferred_element_type=F32).astype(jnp.int32)
        wanted = jnp.arange(capacity, dtype=jnp.int32)[None, :, None]
        return ((position[:, None, :] == wanted) & named[:, None, :]).astype(BF16)

    facts = jnp.concatenate([my_share[None], experts]).astype(jnp.int32)

    parts = [expert_ids.astype(F32)]
    rest = combine
    for _ in range(3):
        parts.append(lax.reduce_precision(rest, 8, 7))
        rest = rest - parts[-1]
    notes = jnp.concatenate(parts, axis=1)
    notes = jnp.pad(notes, ((0, 0), (0, -notes.shape[1] % 128))).astype(BF16)
    payload = jnp.concatenate([tokens, cotangent, notes], axis=1)
    note_at = 2 * width // notes.shape[1]

    def add_pair(a, b):
        return (a.astype(F32) + b.astype(F32)).astype(BF16)

    def whole(piece):
        return ((piece, 0), (piece, 1), (piece, note_at))

    def halves(first, second):
        return ((first, 0), (second, 0), (second, width // notes.shape[1]))

    kept_groups, totals = [], []
    right = left = payload
    pending = crossing = None
    for step in range(half + 1):
        near = [payload] if step == 0 else [right, left]
        far = [lax.ppermute(piece, "ep", other_core) for piece in near]
        if step == half:
            pieces = [halves(*near), halves(*far)]
        else:
            pieces = [whole(piece) for piece in near + far]
        if step < half - 1:
            right = lax.ppermute(right, "ep", forward)
            left = lax.ppermute(left, "ep", backward)
        elif step == half - 1:
            right = lax.ppermute(right[:, :width], "ep", forward)
            left = lax.ppermute(left[:, width:], "ep", backward)
        if crossing is not None:
            totals.append(add_pair(*crossing))
            crossing = None
        if pending is not None:
            near_other, near_mine, far_other, far_mine = pending
            sent = add_pair(near_other, lax.ppermute(far_other, "ep", other_core))
            kept = add_pair(near_mine, lax.ppermute(far_mine, "ep", other_core))
            crossing = (kept, lax.ppermute(sent, "tp", other_share))
        acts, *pending, d_part, packed = group_call(
            *[list(part) for part in zip(*pieces)], facts, (gate_w, up_w, down_w), top_k, capacity, share
        )
        group = (acts, d_part, packed)
        right, left, pending, crossing, group, totals = lax.optimization_barrier(
            (right, left, pending, crossing, group, totals)
        )
        kept_groups.append((pieces, *group))
    totals.append(add_pair(*crossing))
    near_other, near_mine, far_other, far_mine = pending
    sent = add_pair(near_other, lax.ppermute(far_other, "ep", other_core))
    kept = add_pair(near_mine, lax.ppermute(far_mine, "ep", other_core))
    totals.append(add_pair(kept, lax.ppermute(sent, "tp", other_share)))

    every = [piece for group in kept_groups for piece in group[0]]
    x = jnp.concatenate([array[:, at * width : (at + 1) * width] for (array, at), _, _ in every])
    cot = jnp.concatenate([array[:, at * width : (at + 1) * width] for _, (array, at), _ in every])
    ids = jnp.concatenate([array[:, at * 128 : at * 128 + top_k] for _, _, (array, at) in every])
    ids = ids.astype(jnp.int32).reshape(ep_count, tok_count, top_k)
    acts = jnp.concatenate([group[1] for group in kept_groups], axis=1)
    d_weights = jnp.concatenate([group[2] for group in kept_groups])[:, :top_k]
    packed = jnp.concatenate([group[3] for group in kept_groups])
    by_hop = {0: totals[0], half: totals[half]}
    for step in range(1, half):
        by_hop[-step], by_hop[step] = totals[step][:tok_count], totals[step][tok_count:]

    up_sum, down_sum = by_hop[half][:, :share], by_hop[half][:, share:]
    up_sum = jnp.pad(lax.ppermute(up_sum, "ep", forward).astype(F32), ((0, 0), (0, share)))
    down_sum = jnp.pad(lax.ppermute(down_sum, "ep", backward).astype(F32), ((0, 0), (share, 0)))
    for step in range(half - 1, 0, -1):
        up_sum = (by_hop[step].astype(F32) + up_sum).astype(BF16)
        down_sum = (by_hop[-step].astype(F32) + down_sum).astype(BF16)
        up_sum = lax.ppermute(up_sum, "ep", forward).astype(F32)
        down_sum = lax.ppermute(down_sum, "ep", backward).astype(F32)
    home = (by_hop[0].astype(F32) + up_sum + down_sum).astype(BF16)
    mixed, d_tokens = home[:, :share], home[:, share:]

    d_weights = d_weights + lax.ppermute(d_weights, "tp", other_share)
    d_weights = jnp.take(d_weights.reshape(ep_count, tok_count, top_k), spot, axis=0)
    d_combine = lax.psum_scatter(
        d_weights.reshape(ep_count * tok_count, top_k), "ep", scatter_dimension=0, tiled=True
    )

    swapped = jnp.take(lax.ppermute(packed, "ep", partners), from_partner, axis=0)
    packed = jnp.where(my_move, swapped, packed)
    spread_rows = jnp.einsum("brt,brf->btf", rows_of(new_last, ids), packed, preferred_element_type=F32).astype(BF16)
    spread_rows = spread_rows.reshape(ep_count * tok_count, 3 * units)

    def grads(multiply, at):
        columns = slice(at * units, (at + 1) * units)
        own = [multiply(acts[l, :, columns]) for l in range(last)]
        return jnp.stack(own + [multiply(spread_rows[:, columns])])

    grad_down = grads(lambda v: dot(v, cot, 0, 0).astype(BF16), 0)
    grad_gate = grads(lambda v: dot(x, v, 0, 0).astype(BF16), 1)
    grad_up = grads(lambda v: dot(x, v, 0, 0).astype(BF16), 2)
    return (mixed, d_tokens, d_combine, grad_gate, grad_up, grad_down)


def exchange_halves(value, axis, distance):
    mask = 2**distance
    pairs = [(source, source ^ mask) for source in range(lax.axis_size(axis))]
    return lax.ppermute(value, axis, pairs)


def dispatch_body(tokens, expert_ids, combine, cotangent, old_layout, pair_moves, gate_w, up_w, down_w):
    ep_count = lax.axis_size("ep")
    tp_count = lax.axis_size("tp")
    tok_count, top_k = expert_ids.shape
    expert_count = old_layout.shape[0]
    per_device = gate_w.shape[0]
    model_width = tokens.shape[1]
    share_width = model_width // tp_count
    capacity = 3 * tok_count * top_k // (2 * expert_count)
    pair_count = ep_count // 2
    swap_bit = ep_count.bit_length() - 2
    my_index = lax.axis_index("ep")
    my_share = lax.axis_index("tp")
    my_move = pair_moves[my_index] == 1
    slot_ids = jnp.arange(expert_count, dtype=jnp.int32)
    slot_device = slot_ids // per_device
    slot_local = slot_ids % per_device
    moved = (slot_local == per_device - 1) & (pair_moves[slot_device] == 1)
    source_slot = jnp.where(
        moved, (slot_device + pair_count) % ep_count * per_device + slot_local, slot_ids
    )
    new_layout = jnp.sum(
        jnp.where(source_slot[:, None] == slot_ids[None, :], old_layout[None, :], 0), axis=1
    )
    w_gate, w_up, w_down = (gate_w, up_w, down_w)
    arrived = exchange_halves(
        (gate_w[per_device - 1], up_w[per_device - 1], down_w[per_device - 1]), "ep", swap_bit
    )
    w_gate = jnp.concatenate(
        [gate_w[:-1], jnp.where(my_move, arrived[0], gate_w[-1])[None]], axis=0
    )
    w_up = jnp.concatenate([up_w[:-1], jnp.where(my_move, arrived[1], up_w[-1])[None]], axis=0)
    w_down = jnp.concatenate(
        [down_w[:-1], jnp.where(my_move, arrived[2], down_w[-1])[None]], axis=0
    )
    slot_of = jnp.sum(
        jnp.where(new_layout[None, :] == slot_ids[:, None], slot_ids[None, :], 0), axis=1
    )
    flat_ids = expert_ids.reshape(-1)
    onehot = (flat_ids[:, None] == slot_ids[None, :]).astype(jnp.int32)
    before = jnp.cumsum(onehot, axis=0) - onehot
    position = jnp.sum(before * onehot, axis=1)
    target_slot = jnp.sum(onehot * slot_of[None, :], axis=1)
    target_device = target_slot // per_device
    target_local = target_slot % per_device
    row_index = target_local * (ep_count * capacity) + target_device * capacity + position
    rows_total = expert_count * capacity
    matches = jnp.arange(rows_total, dtype=jnp.int32)[:, None] == row_index[None, :]
    select = jnp.sum(
        matches.reshape(rows_total, tok_count, top_k).astype(jnp.int32), axis=2
    ).astype(jnp.bfloat16)
    row_weight = jnp.sum(jnp.where(matches, combine.reshape(-1)[None, :], 0.0), axis=1)

    def dispatch(source, scaling):
        portion = lax.dynamic_slice_in_dim(source, my_share * share_width, share_width, 1)
        picked = jnp.dot(select, portion, preferred_element_type=jnp.float32)
        if scaling is not None:
            picked = picked * scaling[:, None]
        buffer = picked.astype(jnp.bfloat16).reshape(per_device, ep_count * capacity, share_width)
        landed = lax.all_to_all(buffer, "ep", split_axis=1, concat_axis=1, tiled=True)
        return lax.all_gather(landed, "tp", axis=2, tiled=True)

    def send_back(partial_value):
        shares = lax.psum_scatter(partial_value, "tp", scatter_dimension=2, tiled=True).astype(
            jnp.bfloat16
        )
        returned = lax.all_to_all(shares, "ep", split_axis=1, concat_axis=1, tiled=True)
        return returned.reshape(rows_total, share_width)[row_index].reshape(
            tok_count, top_k, share_width
        )

    rows_in = dispatch(tokens, None)
    gate = jnp.einsum("erd,edf->erf", rows_in, w_gate, preferred_element_type=jnp.float32)
    upper = jnp.einsum("erd,edf->erf", rows_in, w_up, preferred_element_type=jnp.float32)
    sigma = jax.nn.sigmoid(gate)
    active = gate * sigma
    hidden = (active * upper).astype(jnp.bfloat16)
    out_part = jnp.einsum("erf,efd->erd", hidden, w_down, preferred_element_type=jnp.float32)
    out_rows = send_back(out_part).astype(jnp.float32)
    mixed = jnp.einsum("tk,tkd->td", combine, out_rows).astype(jnp.bfloat16)
    cot_share = lax.dynamic_slice_in_dim(cotangent, my_share * share_width, share_width, 1).astype(
        jnp.float32
    )
    combine_part = jnp.einsum("td,tkd->tk", cot_share, out_rows)
    d_combine = lax.psum(combine_part, "tp")
    rows_grad = dispatch(cotangent, row_weight)
    d_hidden = jnp.einsum("erd,efd->erf", rows_grad, w_down, preferred_element_type=jnp.float32)
    d_gate = (d_hidden * upper * sigma * (1.0 + gate * (1.0 - sigma))).astype(jnp.bfloat16)
    d_up = (d_hidden * active).astype(jnp.bfloat16)
    back_part = jnp.einsum(
        "erf,edf->erd", d_gate, w_gate, preferred_element_type=jnp.float32
    ) + jnp.einsum("erf,edf->erd", d_up, w_up, preferred_element_type=jnp.float32)
    back_rows = send_back(back_part)
    d_tokens = jnp.sum(back_rows.astype(jnp.float32), axis=1).astype(jnp.bfloat16)
    grad_gate = jnp.einsum(
        "erd,erf->edf", rows_in, d_gate, preferred_element_type=jnp.float32
    ).astype(jnp.bfloat16)
    grad_up = jnp.einsum("erd,erf->edf", rows_in, d_up, preferred_element_type=jnp.float32).astype(
        jnp.bfloat16
    )
    grad_down = jnp.einsum(
        "erf,erd->efd", hidden, rows_grad, preferred_element_type=jnp.float32
    ).astype(jnp.bfloat16)
    return (mixed, d_tokens, d_combine, grad_gate, grad_up, grad_down)


def body(*operands):
    expert_ids, old_layout = operands[1], operands[4]
    tok_count, top_k = expert_ids.shape
    ep_count = lax.axis_size("ep")
    rows = 3 * tok_count * top_k * ep_count // (2 * old_layout.shape[0]) * operands[6].shape[0]
    gather = ep_count * tok_count <= 2 * rows and old_layout.shape[0] <= 256
    return (gather_body if gather else dispatch_body)(*operands)


def solution(mesh):
    return jax.shard_map(
        body,
        mesh=mesh,
        in_specs=(
            P("ep", None),
            P("ep", None),
            P("ep", None),
            P("ep", None),
            P(),
            P(),
            P("ep", None, "tp"),
            P("ep", None, "tp"),
            P("ep", "tp", None),
        ),
        out_specs=(
            P("ep", "tp"),
            P("ep", "tp"),
            P("ep", None),
            P("ep", None, "tp"),
            P("ep", None, "tp"),
            P("ep", "tp", None),
        ),
        check_vma=False,
    )
```

```python
import functools

import jax
import jax.numpy as jnp
import numpy as np
from jax import lax
from jax.experimental import pallas as pl
from jax.experimental.pallas import tpu as pltpu
from jax.sharding import PartitionSpec as P

F32 = jnp.float32
BF16 = jnp.bfloat16


def ring_order(chips):
    return list(range(0, chips, 2)) + list(range(chips - 1, 0, -2))


def ring_pairs(order, hop):
    chips = len(order)
    return [
        (chip * 2 + core, order[(place + hop) % chips] * 2 + core)
        for place, chip in enumerate(order)
        for core in range(2)
    ]


def block_tables(order):
    chips = len(order)
    half = chips // 2
    groups = [[0]] + [[-step, step] for step in range(1, half)] + [[half]]
    ep_count = 2 * chips
    arrival = np.zeros((ep_count, ep_count), np.int32)
    for place, chip in enumerate(order):
        for core in range(2):
            arrival[chip * 2 + core] = [
                order[(place + hop) % chips] * 2 + (core ^ side)
                for hops in groups
                for side in range(2)
                for hop in hops
            ]
    spot = np.argsort(arrival, axis=1).astype(np.int32)
    partner = np.arange(ep_count) ^ (ep_count // 2)
    from_partner = np.take_along_axis(spot[partner], arrival, axis=1).astype(np.int32)
    return arrival, spot, from_partner


def dot(a, b, ca, cb):
    return lax.dot_general(a, b, (((ca,), (cb,)), ((), ())), preferred_element_type=F32)


def group_kernel(pieces, top_k, capacity, units, steps_in, tile_count, facts, *refs):
    x_refs, cot_refs, note_refs = refs[:pieces], refs[pieces : 2 * pieces], refs[2 * pieces : 3 * pieces]
    gate_in, up_in, down_in, gate_out, up_out, down_out = refs[3 * pieces : 3 * pieces + 6]
    hidden_ref, d_gate_ref, d_up_ref, *sums, d_weights, packed, picks = refs[3 * pieces + 6 : 3 * pieces + 16]
    x_all, cot_all, gains = refs[3 * pieces + 16 :]
    step = pl.program_id(0)
    tok_count = note_refs[0].shape[0]
    per_device = gains.shape[0]
    tile = gate_in.shape[1]
    lanes = note_refs[0].shape[1]

    def notes():
        said = jnp.concatenate([ref[...] for ref in note_refs], axis=0).astype(F32)
        lane = lax.broadcasted_iota(jnp.int32, said.shape, 1)
        return said, jnp.where(lane < top_k, said, -1.0).astype(jnp.int32)

    @pl.when(step == 0)
    def _():
        for piece in range(pieces):
            rows = slice(piece * tok_count, (piece + 1) * tok_count)
            x_all[rows] = x_refs[piece][...]
            cot_all[rows] = cot_refs[piece][...]
        said, ids = notes()
        weight = pltpu.roll(said, lanes - top_k, 1) + (
            pltpu.roll(said, lanes - 2 * top_k, 1) + pltpu.roll(said, lanes - 3 * top_k, 1)
        )
        for slot in range(per_device):
            gain = jnp.sum(jnp.where(ids == facts[1 + slot], weight, 0.0), axis=1, keepdims=True)
            gains[slot] = jnp.broadcast_to(gain, said.shape)
        d_weights[...] = jnp.zeros_like(d_weights)

    @pl.when(step < steps_in)
    def _():
        x, cot = x_all[...], cot_all[...]
        gate = dot(x, gate_in[...], 1, 0)
        upper = dot(x, up_in[...], 1, 0)
        pulled = dot(cot, down_in[...], 1, 1)
        sigma = jax.nn.sigmoid(gate)
        active = gate * sigma
        hidden = active * upper
        slots = [(step * (tile // lanes) + part) * lanes // units for part in range(tile // lanes)]
        gain = jnp.concatenate([gains[slot] for slot in slots], axis=1)
        _, ids = notes()
        traded = hidden * pulled
        for part, slot in enumerate(slots):
            value = jnp.sum(traded[:, part * lanes : (part + 1) * lanes], axis=1, keepdims=True)
            d_weights[...] += jnp.where(ids == facts[1 + slot], value, 0.0)
        d_hidden = pulled * gain
        at = pl.ds(pl.multiple_of(step * tile, tile), tile)
        hidden_ref[:, at] = (hidden * gain).astype(BF16)
        d_gate_ref[:, at] = (d_hidden * upper * sigma * (1.0 + gate * (1.0 - sigma))).astype(BF16)
        d_up_ref[:, at] = (d_hidden * active).astype(BF16)

    @pl.when(step >= steps_in)
    def _():
        out = dot(hidden_ref[...], down_out[...], 1, 0).astype(BF16)
        back = (dot(d_gate_ref[...], gate_out[...], 1, 1) + dot(d_up_ref[...], up_out[...], 1, 1)).astype(BF16)
        near = pieces // 2 * tok_count
        for which in range(2):

            @pl.when((step - steps_in) // tile_count == which)
            def _(near_ref=sums[2 * which], far_ref=sums[2 * which + 1]):
                near_ref[0], far_ref[0] = out[:near], out[near:]
                near_ref[1], far_ref[1] = back[:near], back[near:]

    @pl.when(step == steps_in)
    def _():
        _, ids = notes()
        row = lax.broadcasted_iota(jnp.int32, (tok_count, tok_count), 0)
        column = lax.broadcasted_iota(jnp.int32, (tok_count, tok_count), 1)
        earlier = jnp.where(column < row, 1.0, 0.0).astype(BF16)
        tail = slice((per_device - 1) * units, per_device * units)

        def pick_of(rows, expert):
            named = jnp.max(jnp.where(ids[rows] == expert, 1.0, 0.0), axis=1, keepdims=True)
            mask = jnp.broadcast_to(named, (tok_count, tok_count))
            position = dot(earlier, mask.astype(BF16), 1, 0).astype(jnp.int32)
            return jnp.where((position == column) & (mask > 0.0), 1.0, 0.0).astype(BF16)

        for piece in range(pieces):
            rows = slice(piece * tok_count, (piece + 1) * tok_count)
            pick = pick_of(rows, facts[per_device])
            for at, ref in enumerate((hidden_ref, d_gate_ref, d_up_ref)):
                packed[piece, :, at * units : (at + 1) * units] = dot(pick, ref[rows, tail], 0, 0).astype(BF16)[:capacity]
            picks[piece] = pick_of(rows, facts[1 + per_device])


def group_call(x_pieces, cot_pieces, note_pieces, facts, weights, top_k, capacity, per_device, share):
    pieces = len(x_pieces)
    w_gate, w_up, w_down = weights
    width, both = w_gate.shape
    units = both // per_device
    tok_count = x_pieces[0][0].shape[0]
    rows = pieces * tok_count
    lanes = 128
    tile, tile_out = 256, 512
    steps_in, tile_count = both // tile, share // tile_out

    def columns(piece, size):
        return pl.BlockSpec((tok_count, size), lambda step, facts, at=piece[1]: (0, at))

    def unit_tile(step):
        return jnp.minimum(step, steps_in - 1)

    def feature_tile(step, facts):
        place = jnp.maximum(step - steps_in, 0)
        mine = jnp.where(place < tile_count, 1 - facts[0], facts[0])
        return mine * tile_count + place % tile_count

    def sums(which):
        def at(step, facts):
            return (0, 0, jnp.clip(step - steps_in - which * tile_count, 0, tile_count - 1))

        return pl.BlockSpec((2, rows // 2, tile_out), at)

    full = pl.BlockSpec((rows, both), lambda step, facts: (0, 0))
    return pl.pallas_call(
        functools.partial(group_kernel, pieces, top_k, capacity, units, steps_in, tile_count),
        grid_spec=pltpu.PrefetchScalarGridSpec(
            num_scalar_prefetch=1,
            grid=(steps_in + 2 * tile_count,),
            in_specs=[columns(piece, width) for piece in x_pieces + cot_pieces]
            + [columns(piece, lanes) for piece in note_pieces]
            + [pl.BlockSpec((width, tile), lambda step, facts: (0, unit_tile(step)))] * 2
            + [pl.BlockSpec((tile, width), lambda step, facts: (unit_tile(step), 0))]
            + [pl.BlockSpec((tile_out, both), lambda step, facts: (feature_tile(step, facts), 0))] * 2
            + [pl.BlockSpec((both, tile_out), lambda step, facts: (0, feature_tile(step, facts)))],
            out_specs=[full] * 3
            + [sums(0), sums(0), sums(1), sums(1)]
            + [
                pl.BlockSpec((rows, lanes), lambda step, facts: (0, 0)),
                pl.BlockSpec((pieces, capacity, 3 * units), lambda step, facts: (0, 0, 0)),
                pl.BlockSpec((pieces, tok_count, tok_count), lambda step, facts: (0, 0, 0)),
            ],
            scratch_shapes=[pltpu.VMEM((rows, width), BF16)] * 2 + [pltpu.VMEM((per_device, rows, lanes), F32)],
        ),
        out_shape=[jax.ShapeDtypeStruct((rows, both), BF16)] * 3
        + [jax.ShapeDtypeStruct((2, rows // 2, share), BF16)] * 4
        + [
            jax.ShapeDtypeStruct((rows, lanes), F32),
            jax.ShapeDtypeStruct((pieces, capacity, 3 * units), BF16),
            jax.ShapeDtypeStruct((pieces, tok_count, tok_count), BF16),
        ],
        compiler_params=pltpu.CompilerParams(vmem_limit_bytes=56 * 1024 * 1024),
        cost_estimate=pl.CostEstimate(
            flops=12 * rows * width * both,
            bytes_accessed=12 * width * both + 12 * rows * width,
            transcendentals=rows * both,
        ),
    )(facts, *[p[0] for p in x_pieces + cot_pieces + note_pieces], *weights, *weights)


def grad_kernel(counts, moved, units, facts, *refs):
    blocks, act_count = counts
    x_refs, cot_refs = refs[:blocks], refs[blocks : 2 * blocks]
    act_refs = refs[2 * blocks : 2 * blocks + act_count]
    grad_gate, grad_up, grad_down, hidden, d_both = refs[-5:]

    @pl.when(pl.program_id(0) == 0)
    def _():
        if moved:
            picks, own, swapped = act_refs[:-2], act_refs[-2], act_refs[-1]
            block = 0
            for ref in picks:
                for piece in range(ref.shape[0]):
                    tok_count, capacity = ref.shape[1], own.shape[1]
                    packed = jnp.where(facts[0] == 1, swapped[facts[1 + block]], own[block])
                    spread = dot(ref[piece][:, :capacity], packed, 1, 0).astype(BF16)
                    rows = slice(block * tok_count, (block + 1) * tok_count)
                    hidden[rows] = spread[:, :units]
                    d_both[rows] = spread[:, units:]
                    block += 1
        else:
            third = act_count // 3
            at = 0
            for ref, gate, up in zip(act_refs[:third], act_refs[third : 2 * third], act_refs[2 * third :]):
                rows = slice(at, at + ref.shape[0])
                hidden[rows] = ref[...]
                d_both[rows, :units] = gate[...]
                d_both[rows, units:] = up[...]
                at += ref.shape[0]

    x = jnp.concatenate([ref[...] for ref in x_refs], axis=0)
    cot = jnp.concatenate([ref[...] for ref in cot_refs], axis=0)
    pair = dot(x, d_both[...], 0, 0).astype(BF16)
    grad_gate[0], grad_up[0] = pair[:, :units], pair[:, units:]
    grad_down[0] = dot(hidden[...], cot, 0, 0).astype(BF16)


def grad_call(x_pieces, cot_pieces, acts, facts, slot, units, per_device, width, before=None):
    moved = before is not None
    tok_count = x_pieces[0][0].shape[0]
    total = len(x_pieces) * tok_count
    tile = 256

    def tiles(piece):
        first = piece[1] * (width // tile)
        return pl.BlockSpec((tok_count, tile), lambda step, facts: (0, first + step))

    if moved:
        act_specs = [pl.BlockSpec(array.shape, lambda step, facts: (0, 0, 0)) for array in acts]
        act_arrays = list(acts)
    else:
        act_specs = [
            pl.BlockSpec((array.shape[0], units), lambda step, facts, at=at: (0, at)) for array, at in acts
        ]
        act_arrays = [array for array, _ in acts]
    arrays = [p[0] for p in x_pieces + cot_pieces] + act_arrays + list(before or ())
    shapes = [(per_device, width, units)] * 2 + [(per_device, units, width)]
    return pl.pallas_call(
        functools.partial(grad_kernel, (len(x_pieces), len(acts)), moved, units),
        grid_spec=pltpu.PrefetchScalarGridSpec(
            num_scalar_prefetch=1,
            grid=(width // tile,),
            in_specs=[tiles(piece) for piece in x_pieces + cot_pieces]
            + act_specs
            + [pl.BlockSpec(memory_space=pl.ANY)] * len(before or ()),
            out_specs=[pl.BlockSpec((1, tile, units), lambda step, facts: (slot, step, 0))] * 2
            + [pl.BlockSpec((1, units, tile), lambda step, facts: (slot, 0, step))],
            scratch_shapes=[pltpu.VMEM((total, units), BF16), pltpu.VMEM((total, 2 * units), BF16)],
        ),
        out_shape=[jax.ShapeDtypeStruct(shape, BF16) for shape in shapes],
        input_output_aliases={1 + len(arrays) - 3 + i: i for i in range(3)} if moved else {},
        compiler_params=pltpu.CompilerParams(vmem_limit_bytes=48 * 1024 * 1024),
        cost_estimate=pl.CostEstimate(
            flops=6 * total * width * units, bytes_accessed=4 * total * width, transcendentals=0
        ),
    )(facts, *arrays)


def gather_body(tokens, expert_ids, combine, cotangent, old_layout, pair_moves, gate_w, up_w, down_w):
    ep_count = lax.axis_size("ep")
    tp_count = lax.axis_size("tp")
    tok_count, top_k = expert_ids.shape
    expert_count = old_layout.shape[0]
    per_device, width, units = gate_w.shape
    share = width // tp_count
    capacity = 3 * tok_count * top_k // (2 * expert_count)
    chips = ep_count // 2
    half = chips // 2
    order = ring_order(chips)
    forward, backward = ring_pairs(order, 1), ring_pairs(order, -1)
    other_core = [(i, i ^ 1) for i in range(ep_count)]
    other_share = [(i, i ^ 1) for i in range(tp_count)]
    partners = [(i, i ^ (ep_count // 2)) for i in range(ep_count)]
    me = lax.axis_index("ep")
    my_share = lax.axis_index("tp")
    arrival, spot, from_partner = (jnp.asarray(table)[me] for table in block_tables(order))

    my_move = pair_moves[me] == 1
    last = per_device - 1
    experts = lax.dynamic_slice_in_dim(old_layout, me * per_device, per_device, 0)
    partner_last = old_layout[(me ^ (ep_count // 2)) * per_device + last]
    new_last = jnp.where(my_move, partner_last, experts[last])
    facts = jnp.concatenate([my_share[None], experts, new_last[None]]).astype(jnp.int32)
    weights = (
        jnp.concatenate([gate_w[l] for l in range(per_device)], axis=1),
        jnp.concatenate([up_w[l] for l in range(per_device)], axis=1),
        down_w.reshape(per_device * units, width),
    )

    parts = [expert_ids.astype(F32)]
    rest = combine
    for _ in range(3):
        parts.append(lax.reduce_precision(rest, 8, 7))
        rest = rest - parts[-1]
    notes = jnp.concatenate(parts, axis=1)
    notes = jnp.pad(notes, ((0, 0), (0, -notes.shape[1] % 128))).astype(BF16)
    payload = jnp.concatenate([tokens, cotangent, notes], axis=1)
    note_at = 2 * width // notes.shape[1]

    def add_pair(a, b):
        return (a.astype(F32) + b.astype(F32)).astype(BF16)

    def whole(piece):
        return ((piece, 0), (piece, 1), (piece, note_at))

    def halves(first, second):
        return ((first, 0), (second, 0), (second, width // notes.shape[1]))

    kept_groups, totals = [], []
    right = left = payload
    pending = crossing = None
    for step in range(half + 1):
        near = [payload] if step == 0 else [right, left]
        far = [lax.ppermute(piece, "ep", other_core) for piece in near]
        if step == half:
            pieces = [halves(*near), halves(*far)]
        else:
            pieces = [whole(piece) for piece in near + far]
        if step < half - 1:
            right = lax.ppermute(right, "ep", forward)
            left = lax.ppermute(left, "ep", backward)
        elif step == half - 1:
            right = lax.ppermute(right[:, :width], "ep", forward)
            left = lax.ppermute(left[:, width:], "ep", backward)
        if crossing is not None:
            totals.append(add_pair(*crossing))
            crossing = None
        if pending is not None:
            near_other, near_mine, far_other, far_mine = pending
            sent = add_pair(near_other, lax.ppermute(far_other, "ep", other_core))
            kept = add_pair(near_mine, lax.ppermute(far_mine, "ep", other_core))
            crossing = (kept, lax.ppermute(sent, "tp", other_share))
        result = group_call(
            *[list(part) for part in zip(*pieces)], facts, weights, top_k, capacity, per_device, share
        )
        acts, (near_other, far_other, near_mine, far_mine), rest = result[:3], result[3:7], result[7:]
        pending = (near_other, near_mine, far_other, far_mine)
        group = (acts, rest)
        right, left, pending, crossing, group, totals = lax.optimization_barrier(
            (right, left, pending, crossing, group, totals)
        )
        kept_groups.append((pieces, *group))
    totals.append(add_pair(*crossing))
    near_other, near_mine, far_other, far_mine = pending
    sent = add_pair(near_other, lax.ppermute(far_other, "ep", other_core))
    kept = add_pair(near_mine, lax.ppermute(far_mine, "ep", other_core))
    totals.append(add_pair(kept, lax.ppermute(sent, "tp", other_share)))

    every = [piece for group in kept_groups for piece in group[0]]
    x_pieces, cot_pieces = [piece[0] for piece in every], [piece[1] for piece in every]
    d_weights = jnp.concatenate([group[2][0] for group in kept_groups])[:, :top_k]
    by_hop = {0: totals[0], half: totals[half]}
    for step in range(1, half):
        by_hop[-step], by_hop[step] = totals[step][:, :tok_count], totals[step][:, tok_count:]

    own_rows = jnp.concatenate([group[2][1] for group in kept_groups])
    swapped = [
        lax.ppermute(jnp.concatenate([group[2][1] for group in part]), "ep", partners)
        for part in (kept_groups[: half - 1], kept_groups[half - 1 :])
    ]

    d_weights = d_weights + lax.ppermute(d_weights, "tp", other_share)
    d_weights = jnp.take(d_weights.reshape(ep_count, tok_count, top_k), spot, axis=0)
    d_combine = lax.psum_scatter(
        d_weights.reshape(ep_count * tok_count, top_k), "ep", scatter_dimension=0, tiled=True
    )

    up_sum = lax.ppermute(by_hop[half][0], "ep", forward)
    down_sum = lax.ppermute(by_hop[half][1], "ep", backward)
    for step in range(half - 1, 0, -1):
        if step == half - 1:
            up_sum = jnp.stack([add_pair(by_hop[step][0], up_sum), by_hop[step][1]])
            down_sum = jnp.stack([by_hop[-step][0], add_pair(by_hop[-step][1], down_sum)])
        else:
            up_sum = add_pair(by_hop[step], up_sum)
            down_sum = add_pair(by_hop[-step], down_sum)
        if step == 1:
            up_sum, down_sum, d_combine = lax.optimization_barrier((up_sum, down_sum, d_combine))
        up_sum = lax.ppermute(up_sum, "ep", forward)
        down_sum = lax.ppermute(down_sum, "ep", backward)
    home = (by_hop[0].astype(F32) + up_sum.astype(F32) + down_sum.astype(F32)).astype(BF16)
    mixed, d_tokens = home[0], home[1]

    acts = [(group[1][i], 0) for i in range(3) for group in kept_groups]
    first_facts = jnp.zeros((1,), jnp.int32)
    grads = None
    for slot in range(last):
        own_acts = [(array, slot) for array, _ in acts]
        grads = grad_call(x_pieces, cot_pieces, own_acts, first_facts, slot, units, per_device, width)
    move_facts = jnp.concatenate([my_move.astype(jnp.int32)[None], from_partner])
    moved_acts = [group[2][2] for group in kept_groups] + [own_rows, jnp.concatenate(swapped)]
    grad_gate, grad_up, grad_down = grad_call(
        x_pieces, cot_pieces, moved_acts, move_facts, last, units, per_device, width, before=grads
    )
    return (mixed, d_tokens, d_combine, grad_gate, grad_up, grad_down)


def exchange_halves(value, axis, distance):
    mask = 2**distance
    pairs = [(source, source ^ mask) for source in range(lax.axis_size(axis))]
    return lax.ppermute(value, axis, pairs)


def dispatch_body(tokens, expert_ids, combine, cotangent, old_layout, pair_moves, gate_w, up_w, down_w):
    ep_count = lax.axis_size("ep")
    tp_count = lax.axis_size("tp")
    tok_count, top_k = expert_ids.shape
    expert_count = old_layout.shape[0]
    per_device = gate_w.shape[0]
    model_width = tokens.shape[1]
    share_width = model_width // tp_count
    capacity = 3 * tok_count * top_k // (2 * expert_count)
    pair_count = ep_count // 2
    swap_bit = ep_count.bit_length() - 2
    my_index = lax.axis_index("ep")
    my_share = lax.axis_index("tp")
    my_move = pair_moves[my_index] == 1
    slot_ids = jnp.arange(expert_count, dtype=jnp.int32)
    slot_device = slot_ids // per_device
    slot_local = slot_ids % per_device
    moved = (slot_local == per_device - 1) & (pair_moves[slot_device] == 1)
    source_slot = jnp.where(
        moved, (slot_device + pair_count) % ep_count * per_device + slot_local, slot_ids
    )
    new_layout = jnp.sum(
        jnp.where(source_slot[:, None] == slot_ids[None, :], old_layout[None, :], 0), axis=1
    )
    w_gate, w_up, w_down = (gate_w, up_w, down_w)
    arrived = exchange_halves(
        (gate_w[per_device - 1], up_w[per_device - 1], down_w[per_device - 1]), "ep", swap_bit
    )
    w_gate = jnp.concatenate(
        [gate_w[:-1], jnp.where(my_move, arrived[0], gate_w[-1])[None]], axis=0
    )
    w_up = jnp.concatenate([up_w[:-1], jnp.where(my_move, arrived[1], up_w[-1])[None]], axis=0)
    w_down = jnp.concatenate(
        [down_w[:-1], jnp.where(my_move, arrived[2], down_w[-1])[None]], axis=0
    )
    slot_of = jnp.sum(
        jnp.where(new_layout[None, :] == slot_ids[:, None], slot_ids[None, :], 0), axis=1
    )
    flat_ids = expert_ids.reshape(-1)
    onehot = (flat_ids[:, None] == slot_ids[None, :]).astype(jnp.int32)
    before = jnp.cumsum(onehot, axis=0) - onehot
    position = jnp.sum(before * onehot, axis=1)
    target_slot = jnp.sum(onehot * slot_of[None, :], axis=1)
    target_device = target_slot // per_device
    target_local = target_slot % per_device
    row_index = target_local * (ep_count * capacity) + target_device * capacity + position
    rows_total = expert_count * capacity
    matches = jnp.arange(rows_total, dtype=jnp.int32)[:, None] == row_index[None, :]
    select = jnp.sum(
        matches.reshape(rows_total, tok_count, top_k).astype(jnp.int32), axis=2
    ).astype(jnp.bfloat16)
    row_weight = jnp.sum(jnp.where(matches, combine.reshape(-1)[None, :], 0.0), axis=1)

    def dispatch(source, scaling):
        portion = lax.dynamic_slice_in_dim(source, my_share * share_width, share_width, 1)
        picked = jnp.dot(select, portion, preferred_element_type=jnp.float32)
        if scaling is not None:
            picked = picked * scaling[:, None]
        buffer = picked.astype(jnp.bfloat16).reshape(per_device, ep_count * capacity, share_width)
        landed = lax.all_to_all(buffer, "ep", split_axis=1, concat_axis=1, tiled=True)
        return lax.all_gather(landed, "tp", axis=2, tiled=True)

    def send_back(partial_value):
        shares = lax.psum_scatter(partial_value, "tp", scatter_dimension=2, tiled=True).astype(
            jnp.bfloat16
        )
        returned = lax.all_to_all(shares, "ep", split_axis=1, concat_axis=1, tiled=True)
        return returned.reshape(rows_total, share_width)[row_index].reshape(
            tok_count, top_k, share_width
        )

    rows_in = dispatch(tokens, None)
    gate = jnp.einsum("erd,edf->erf", rows_in, w_gate, preferred_element_type=jnp.float32)
    upper = jnp.einsum("erd,edf->erf", rows_in, w_up, preferred_element_type=jnp.float32)
    sigma = jax.nn.sigmoid(gate)
    active = gate * sigma
    hidden = (active * upper).astype(jnp.bfloat16)
    out_part = jnp.einsum("erf,efd->erd", hidden, w_down, preferred_element_type=jnp.float32)
    out_rows = send_back(out_part).astype(jnp.float32)
    mixed = jnp.einsum("tk,tkd->td", combine, out_rows).astype(jnp.bfloat16)
    cot_share = lax.dynamic_slice_in_dim(cotangent, my_share * share_width, share_width, 1).astype(
        jnp.float32
    )
    combine_part = jnp.einsum("td,tkd->tk", cot_share, out_rows)
    d_combine = lax.psum(combine_part, "tp")
    rows_grad = dispatch(cotangent, row_weight)
    d_hidden = jnp.einsum("erd,efd->erf", rows_grad, w_down, preferred_element_type=jnp.float32)
    d_gate = (d_hidden * upper * sigma * (1.0 + gate * (1.0 - sigma))).astype(jnp.bfloat16)
    d_up = (d_hidden * active).astype(jnp.bfloat16)
    back_part = jnp.einsum(
        "erf,edf->erd", d_gate, w_gate, preferred_element_type=jnp.float32
    ) + jnp.einsum("erf,edf->erd", d_up, w_up, preferred_element_type=jnp.float32)
    back_rows = send_back(back_part)
    d_tokens = jnp.sum(back_rows.astype(jnp.float32), axis=1).astype(jnp.bfloat16)
    grad_gate = jnp.einsum(
        "erd,erf->edf", rows_in, d_gate, preferred_element_type=jnp.float32
    ).astype(jnp.bfloat16)
    grad_up = jnp.einsum("erd,erf->edf", rows_in, d_up, preferred_element_type=jnp.float32).astype(
        jnp.bfloat16
    )
    grad_down = jnp.einsum(
        "erf,erd->efd", hidden, rows_grad, preferred_element_type=jnp.float32
    ).astype(jnp.bfloat16)
    return (mixed, d_tokens, d_combine, grad_gate, grad_up, grad_down)


def body(*operands):
    expert_ids, old_layout = operands[1], operands[4]
    tok_count, top_k = expert_ids.shape
    ep_count = lax.axis_size("ep")
    rows = 3 * tok_count * top_k * ep_count // (2 * old_layout.shape[0]) * operands[6].shape[0]
    gather = ep_count * tok_count <= 2 * rows and old_layout.shape[0] <= 256
    return (gather_body if gather else dispatch_body)(*operands)


def solution(mesh):
    return jax.shard_map(
        body,
        mesh=mesh,
        in_specs=(
            P("ep", None),
            P("ep", None),
            P("ep", None),
            P("ep", None),
            P(),
            P(),
            P("ep", None, "tp"),
            P("ep", None, "tp"),
            P("ep", "tp", None),
        ),
        out_specs=(
            P("ep", "tp"),
            P("ep", "tp"),
            P("ep", None),
            P("ep", None, "tp"),
            P("ep", None, "tp"),
            P("ep", "tp", None),
        ),
        check_vma=False,
    )
```

```python
import functools

import jax
import jax.numpy as jnp
import numpy as np
from jax import lax
from jax.experimental import pallas as pl
from jax.experimental.pallas import tpu as pltpu
from jax.sharding import PartitionSpec as P

F32 = jnp.float32
BF16 = jnp.bfloat16


def ring_order(chips):
    return list(range(0, chips, 2)) + list(range(chips - 1, 0, -2))


def ring_pairs(order, hop):
    chips = len(order)
    return [
        (chip * 2 + core, order[(place + hop) % chips] * 2 + core)
        for place, chip in enumerate(order)
        for core in range(2)
    ]


def block_tables(order):
    chips = len(order)
    half = chips // 2
    groups = [[0]] + [[-step, step] for step in range(1, half)] + [[half]]
    ep_count = 2 * chips
    arrival = np.zeros((ep_count, ep_count), np.int32)
    for place, chip in enumerate(order):
        for core in range(2):
            arrival[chip * 2 + core] = [
                order[(place + hop) % chips] * 2 + (core ^ side)
                for hops in groups
                for side in range(2)
                for hop in hops
            ]
    spot = np.argsort(arrival, axis=1).astype(np.int32)
    partner = np.arange(ep_count) ^ (ep_count // 2)
    from_partner = np.take_along_axis(spot[partner], arrival, axis=1).astype(np.int32)
    return arrival, spot, from_partner


def dot(a, b, ca, cb):
    return lax.dot_general(a, b, (((ca,), (cb,)), ((), ())), preferred_element_type=F32)


def group_kernel(pieces, top_k, capacity, units, steps_in, tile_count, facts, *refs):
    x_refs, cot_refs, note_refs = refs[:pieces], refs[pieces : 2 * pieces], refs[2 * pieces : 3 * pieces]
    x_all, cot_all, gains = refs[-3:]
    hidden_ref, d_gate_ref, d_up_ref, *sums, d_weights, packed, picks = refs[-13:-3]
    w_refs = refs[3 * pieces : -13]
    per_device = gains.shape[0]
    chunks = (len(w_refs) - 2 - 2 * per_device) // 2
    gate_in, up_in, down_in = w_refs[:chunks], w_refs[chunks : 2 * chunks], w_refs[2 * chunks]
    gate_out, up_out = w_refs[2 * chunks + 1 : -1 - per_device], w_refs[-1 - per_device : -1]
    down_out = w_refs[-1]
    step = pl.program_id(0)
    tok_count = note_refs[0].shape[0]
    tile = down_in.shape[0]
    lanes = note_refs[0].shape[1]

    def notes():
        said = jnp.concatenate([ref[...] for ref in note_refs], axis=0).astype(F32)
        lane = lax.broadcasted_iota(jnp.int32, said.shape, 1)
        return said, jnp.where(lane < top_k, said, -1.0).astype(jnp.int32)

    @pl.when(step == 0)
    def _():
        for piece in range(pieces):
            rows = slice(piece * tok_count, (piece + 1) * tok_count)
            x_all[rows] = x_refs[piece][...]
            cot_all[rows] = cot_refs[piece][...]
        said, ids = notes()
        weight = pltpu.roll(said, lanes - top_k, 1) + (
            pltpu.roll(said, lanes - 2 * top_k, 1) + pltpu.roll(said, lanes - 3 * top_k, 1)
        )
        for slot in range(per_device):
            gain = jnp.sum(jnp.where(ids == facts[1 + slot], weight, 0.0), axis=1, keepdims=True)
            gains[slot] = jnp.broadcast_to(gain, said.shape)
        d_weights[...] = jnp.zeros_like(d_weights)

    @pl.when(step < steps_in)
    def _():
        x, cot = x_all[...], cot_all[...]
        gate = dot(x, jnp.concatenate([ref[0] for ref in gate_in], axis=1), 1, 0)
        upper = dot(x, jnp.concatenate([ref[0] for ref in up_in], axis=1), 1, 0)
        pulled = dot(cot, down_in[...], 1, 1)
        sigma = jax.nn.sigmoid(gate)
        active = gate * sigma
        hidden = active * upper
        slots = [(step * (tile // lanes) + part) * lanes // units for part in range(tile // lanes)]
        gain = jnp.concatenate([gains[slot] for slot in slots], axis=1)
        _, ids = notes()
        traded = hidden * pulled
        for part, slot in enumerate(slots):
            value = jnp.sum(traded[:, part * lanes : (part + 1) * lanes], axis=1, keepdims=True)
            d_weights[...] += jnp.where(ids == facts[1 + slot], value, 0.0)
        d_hidden = pulled * gain
        at = pl.ds(pl.multiple_of(step * tile, tile), tile)
        hidden_ref[:, at] = (hidden * gain).astype(BF16)
        d_gate_ref[:, at] = (d_hidden * upper * sigma * (1.0 + gate * (1.0 - sigma))).astype(BF16)
        d_up_ref[:, at] = (d_hidden * active).astype(BF16)

    @pl.when(step >= steps_in)
    def _():
        out = dot(hidden_ref[...], down_out[...], 1, 0).astype(BF16)
        back = dot(d_gate_ref[...], jnp.concatenate([ref[0] for ref in gate_out], axis=1), 1, 1)
        back += dot(d_up_ref[...], jnp.concatenate([ref[0] for ref in up_out], axis=1), 1, 1)
        back = back.astype(BF16)
        near = pieces // 2 * tok_count
        for which in range(2):

            @pl.when((step - steps_in) // tile_count == which)
            def _(near_ref=sums[2 * which], far_ref=sums[2 * which + 1]):
                near_ref[0], far_ref[0] = out[:near], out[near:]
                near_ref[1], far_ref[1] = back[:near], back[near:]

    @pl.when(step == steps_in)
    def _():
        _, ids = notes()
        row = lax.broadcasted_iota(jnp.int32, (tok_count, tok_count), 0)
        column = lax.broadcasted_iota(jnp.int32, (tok_count, tok_count), 1)
        earlier = jnp.where(column < row, 1.0, 0.0).astype(BF16)
        tail = slice((per_device - 1) * units, per_device * units)

        def pick_of(rows, expert):
            named = jnp.max(jnp.where(ids[rows] == expert, 1.0, 0.0), axis=1, keepdims=True)
            mask = jnp.broadcast_to(named, (tok_count, tok_count))
            position = dot(earlier, mask.astype(BF16), 1, 0).astype(jnp.int32)
            return jnp.where((position == column) & (mask > 0.0), 1.0, 0.0).astype(BF16)

        for piece in range(pieces):
            rows = slice(piece * tok_count, (piece + 1) * tok_count)
            pick = pick_of(rows, facts[per_device])
            for at, ref in enumerate((hidden_ref, d_gate_ref, d_up_ref)):
                packed[piece, :, at * units : (at + 1) * units] = dot(pick, ref[rows, tail], 0, 0).astype(BF16)[:capacity]
            picks[piece] = pick_of(rows, facts[1 + per_device])


def group_call(x_pieces, cot_pieces, note_pieces, facts, weights, top_k, capacity, per_device, share):
    pieces = len(x_pieces)
    w_gate, w_up, w_down = weights
    _, width, units = w_gate.shape
    both = per_device * units
    tok_count = x_pieces[0][0].shape[0]
    rows = pieces * tok_count
    lanes = 128
    tile, tile_out = 256, 512
    steps_in, tile_count = both // tile, share // tile_out

    def columns(piece, size):
        return pl.BlockSpec((tok_count, size), lambda step, facts, at=piece[1]: (0, at))

    def unit_tile(step):
        return jnp.minimum(step, steps_in - 1)

    def feature_tile(step, facts):
        place = jnp.maximum(step - steps_in, 0)
        mine = jnp.where(place < tile_count, 1 - facts[0], facts[0])
        return mine * tile_count + place % tile_count

    def sums(which):
        def at(step, facts):
            return (0, 0, jnp.clip(step - steps_in - which * tile_count, 0, tile_count - 1))

        return pl.BlockSpec((2, rows // 2, tile_out), at)

    def in_chunk(chunk):
        def at(step, facts):
            place = unit_tile(step) * (tile // lanes) + chunk
            return (place * lanes // units, 0, place % (units // lanes))

        return pl.BlockSpec((1, width, lanes), at)

    def out_slot(slot):
        return pl.BlockSpec((1, tile_out, units), lambda step, facts: (slot, feature_tile(step, facts), 0))

    chunks = [in_chunk(chunk) for chunk in range(tile // lanes)]
    slots = [out_slot(slot) for slot in range(per_device)]
    full = pl.BlockSpec((rows, both), lambda step, facts: (0, 0))
    return pl.pallas_call(
        functools.partial(group_kernel, pieces, top_k, capacity, units, steps_in, tile_count),
        grid_spec=pltpu.PrefetchScalarGridSpec(
            num_scalar_prefetch=1,
            grid=(steps_in + 2 * tile_count,),
            in_specs=[columns(piece, width) for piece in x_pieces + cot_pieces]
            + [columns(piece, lanes) for piece in note_pieces]
            + chunks * 2
            + [pl.BlockSpec((tile, width), lambda step, facts: (unit_tile(step), 0))]
            + slots * 2
            + [pl.BlockSpec((both, tile_out), lambda step, facts: (0, feature_tile(step, facts)))],
            out_specs=[full] * 3
            + [sums(0), sums(0), sums(1), sums(1)]
            + [
                pl.BlockSpec((rows, lanes), lambda step, facts: (0, 0)),
                pl.BlockSpec((pieces, capacity, 3 * units), lambda step, facts: (0, 0, 0)),
                pl.BlockSpec((pieces, tok_count, tok_count), lambda step, facts: (0, 0, 0)),
            ],
            scratch_shapes=[pltpu.VMEM((rows, width), BF16)] * 2 + [pltpu.VMEM((per_device, rows, lanes), F32)],
        ),
        out_shape=[jax.ShapeDtypeStruct((rows, both), BF16)] * 3
        + [jax.ShapeDtypeStruct((2, rows // 2, share), BF16)] * 4
        + [
            jax.ShapeDtypeStruct((rows, lanes), F32),
            jax.ShapeDtypeStruct((pieces, capacity, 3 * units), BF16),
            jax.ShapeDtypeStruct((pieces, tok_count, tok_count), BF16),
        ],
        compiler_params=pltpu.CompilerParams(vmem_limit_bytes=56 * 1024 * 1024),
        cost_estimate=pl.CostEstimate(
            flops=12 * rows * width * both,
            bytes_accessed=12 * width * both + 12 * rows * width,
            transcendentals=rows * both,
        ),
    )(
        facts,
        *[p[0] for p in x_pieces + cot_pieces + note_pieces],
        *[w_gate] * len(chunks),
        *[w_up] * len(chunks),
        w_down,
        *[w_gate] * per_device,
        *[w_up] * per_device,
        w_down,
    )


def grad_kernel(counts, moved, units, facts, *refs):
    blocks, act_count = counts
    x_refs, cot_refs = refs[:blocks], refs[blocks : 2 * blocks]
    act_refs = refs[2 * blocks : 2 * blocks + act_count]
    grad_gate, grad_up, grad_down, hidden, d_both = refs[-5:]

    @pl.when(pl.program_id(0) == 0)
    def _():
        if moved:
            picks, own, swapped = act_refs[:-2], act_refs[-2], act_refs[-1]
            block = 0
            for ref in picks:
                for piece in range(ref.shape[0]):
                    tok_count, capacity = ref.shape[1], own.shape[1]
                    packed = jnp.where(facts[0] == 1, swapped[facts[1 + block]], own[block])
                    spread = dot(ref[piece][:, :capacity], packed, 1, 0).astype(BF16)
                    rows = slice(block * tok_count, (block + 1) * tok_count)
                    hidden[rows] = spread[:, :units]
                    d_both[rows] = spread[:, units:]
                    block += 1
        else:
            third = act_count // 3
            at = 0
            for ref, gate, up in zip(act_refs[:third], act_refs[third : 2 * third], act_refs[2 * third :]):
                rows = slice(at, at + ref.shape[0])
                hidden[rows] = ref[...]
                d_both[rows, :units] = gate[...]
                d_both[rows, units:] = up[...]
                at += ref.shape[0]

    x = jnp.concatenate([ref[...] for ref in x_refs], axis=0)
    cot = jnp.concatenate([ref[...] for ref in cot_refs], axis=0)
    pair = dot(x, d_both[...], 0, 0).astype(BF16)
    grad_gate[0], grad_up[0] = pair[:, :units], pair[:, units:]
    grad_down[0] = dot(hidden[...], cot, 0, 0).astype(BF16)


def grad_call(x_pieces, cot_pieces, acts, facts, slot, units, per_device, width, before=None):
    moved = before is not None
    tok_count = x_pieces[0][0].shape[0]
    total = len(x_pieces) * tok_count
    tile = 256

    def tiles(piece):
        first = piece[1] * (width // tile)
        return pl.BlockSpec((tok_count, tile), lambda step, facts: (0, first + step))

    if moved:
        act_specs = [pl.BlockSpec(array.shape, lambda step, facts: (0, 0, 0)) for array in acts]
        act_arrays = list(acts)
    else:
        act_specs = [
            pl.BlockSpec((array.shape[0], units), lambda step, facts, at=at: (0, at)) for array, at in acts
        ]
        act_arrays = [array for array, _ in acts]
    arrays = [p[0] for p in x_pieces + cot_pieces] + act_arrays + list(before or ())
    shapes = [(per_device, width, units)] * 2 + [(per_device, units, width)]
    return pl.pallas_call(
        functools.partial(grad_kernel, (len(x_pieces), len(acts)), moved, units),
        grid_spec=pltpu.PrefetchScalarGridSpec(
            num_scalar_prefetch=1,
            grid=(width // tile,),
            in_specs=[tiles(piece) for piece in x_pieces + cot_pieces]
            + act_specs
            + [pl.BlockSpec(memory_space=pl.ANY)] * len(before or ()),
            out_specs=[pl.BlockSpec((1, tile, units), lambda step, facts: (slot, step, 0))] * 2
            + [pl.BlockSpec((1, units, tile), lambda step, facts: (slot, 0, step))],
            scratch_shapes=[pltpu.VMEM((total, units), BF16), pltpu.VMEM((total, 2 * units), BF16)],
        ),
        out_shape=[jax.ShapeDtypeStruct(shape, BF16) for shape in shapes],
        input_output_aliases={1 + len(arrays) - 3 + i: i for i in range(3)} if moved else {},
        compiler_params=pltpu.CompilerParams(vmem_limit_bytes=48 * 1024 * 1024),
        cost_estimate=pl.CostEstimate(
            flops=6 * total * width * units, bytes_accessed=4 * total * width, transcendentals=0
        ),
    )(facts, *arrays)


def gather_body(tokens, expert_ids, combine, cotangent, old_layout, pair_moves, gate_w, up_w, down_w):
    ep_count = lax.axis_size("ep")
    tp_count = lax.axis_size("tp")
    tok_count, top_k = expert_ids.shape
    expert_count = old_layout.shape[0]
    per_device, width, units = gate_w.shape
    share = width // tp_count
    capacity = 3 * tok_count * top_k // (2 * expert_count)
    chips = ep_count // 2
    half = chips // 2
    order = ring_order(chips)
    forward, backward = ring_pairs(order, 1), ring_pairs(order, -1)
    by_core = [(forward if pair[0] % 2 == 0 else backward)[i] for i, pair in enumerate(forward)]
    other_core = [(i, i ^ 1) for i in range(ep_count)]
    other_share = [(i, i ^ 1) for i in range(tp_count)]
    partners = [(i, i ^ (ep_count // 2)) for i in range(ep_count)]
    me = lax.axis_index("ep")
    my_share = lax.axis_index("tp")
    core = me % 2
    spot, from_partner = (jnp.asarray(table)[me] for table in block_tables(order)[1:])

    my_move = pair_moves[me] == 1
    last = per_device - 1
    experts = lax.dynamic_slice_in_dim(old_layout, me * per_device, per_device, 0)
    partner_last = old_layout[(me ^ (ep_count // 2)) * per_device + last]
    new_last = jnp.where(my_move, partner_last, experts[last])
    facts = jnp.concatenate([my_share[None], experts, new_last[None]]).astype(jnp.int32)
    weights = (gate_w, up_w, down_w.reshape(per_device * units, width))

    parts = [expert_ids.astype(F32)]
    rest = combine
    for _ in range(3):
        parts.append(lax.reduce_precision(rest, 8, 7))
        rest = rest - parts[-1]
    notes = jnp.concatenate(parts, axis=1)
    notes = jnp.pad(notes, ((0, 0), (0, -notes.shape[1] % 128))).astype(BF16)
    payload = jnp.concatenate([tokens, cotangent, notes], axis=1)
    note_at = 2 * width // notes.shape[1]

    def add_pair(a, b):
        return (a.astype(F32) + b.astype(F32)).astype(BF16)

    def whole(piece):
        return ((piece, 0), (piece, 1), (piece, note_at))

    move_facts = jnp.concatenate([my_move.astype(jnp.int32)[None], from_partner])
    kept_groups, totals, swapped = [], [], []
    right = left = payload
    pending = crossing = None
    for step in range(half + 1):
        near = [payload] if step == 0 else [right, left] if step < half else [right]
        far = [lax.ppermute(piece, "ep", other_core) for piece in near]
        pieces = [whole(piece) for piece in near + far]
        if step < half - 1:
            right = lax.ppermute(right, "ep", forward)
            left = lax.ppermute(left, "ep", backward)
        elif step == half - 1:
            right = lax.ppermute(jnp.where(core == 0, right, left), "ep", by_core)
        if crossing is not None:
            totals.append(add_pair(*crossing))
            crossing = None
        if pending is not None:
            near_other, near_mine, far_other, far_mine = pending
            sent = add_pair(near_other, lax.ppermute(far_other, "ep", other_core))
            kept = add_pair(near_mine, lax.ppermute(far_mine, "ep", other_core))
            crossing = (kept, lax.ppermute(sent, "tp", other_share))
        result = group_call(
            *[list(part) for part in zip(*pieces)], facts, weights, top_k, capacity, per_device, share
        )
        acts, (near_other, far_other, near_mine, far_mine), rest = result[:3], result[3:7], result[7:]
        pending = (near_other, near_mine, far_other, far_mine)
        group = (acts, rest)
        part = {half - 1: kept_groups[:2], half: kept_groups[2:half - 1]}.get(step)
        if part:
            swapped.append(lax.ppermute(jnp.concatenate([g[2][1] for g in part]), "ep", partners))
        right, left, pending, crossing, group, totals, move_facts, swapped = lax.optimization_barrier(
            (right, left, pending, crossing, group, totals, move_facts, swapped)
        )
        kept_groups.append((pieces, *group))
    totals.append(add_pair(*crossing))
    near_other, near_mine, far_other, far_mine = pending
    sent = add_pair(near_other, lax.ppermute(far_other, "ep", other_core))
    kept = add_pair(near_mine, lax.ppermute(far_mine, "ep", other_core))
    totals.append(add_pair(kept, lax.ppermute(sent, "tp", other_share)))

    every = [piece for group in kept_groups for piece in group[0]]
    x_pieces, cot_pieces = [piece[0] for piece in every], [piece[1] for piece in every]
    d_weights = jnp.concatenate([group[2][0] for group in kept_groups])[:, :top_k]
    by_hop = {0: totals[0], half: totals[half]}
    for step in range(1, half):
        by_hop[-step], by_hop[step] = totals[step][:, :tok_count], totals[step][:, tok_count:]

    own_rows = jnp.concatenate([group[2][1] for group in kept_groups])
    rest_of_rows = kept_groups[half - 1 :]
    swapped.append(lax.ppermute(jnp.concatenate([group[2][1] for group in rest_of_rows]), "ep", partners))

    d_weights = d_weights + lax.ppermute(d_weights, "tp", other_share)
    d_weights = jnp.take(d_weights.reshape(ep_count, tok_count, top_k), spot, axis=0)
    d_weights = lax.all_to_all(d_weights.transpose(0, 2, 1), "ep", split_axis=0, concat_axis=0, tiled=True)
    d_combine = jnp.sum(d_weights, axis=0).T

    met = lax.ppermute(by_hop[half], "ep", by_core)
    none = jnp.zeros_like(met)
    up_sum, down_sum = jnp.where(core == 0, met, none), jnp.where(core == 0, none, met)
    for step in range(half - 1, 0, -1):
        up_sum = lax.ppermute(add_pair(by_hop[step], up_sum), "ep", forward)
        down_sum = lax.ppermute(add_pair(by_hop[-step], down_sum), "ep", backward)
    home = (by_hop[0].astype(F32) + up_sum.astype(F32) + down_sum.astype(F32)).astype(BF16)
    mixed, d_tokens = home[0], home[1]

    acts = [(group[1][i], 0) for i in range(3) for group in kept_groups]
    first_facts = jnp.zeros((1,), jnp.int32)
    grads = None
    for slot in range(last):
        own_acts = [(array, slot) for array, _ in acts]
        grads = grad_call(x_pieces, cot_pieces, own_acts, first_facts, slot, units, per_device, width)
    moved_acts = [group[2][2] for group in kept_groups] + [own_rows, jnp.concatenate(swapped)]
    grad_gate, grad_up, grad_down = grad_call(
        x_pieces, cot_pieces, moved_acts, move_facts, last, units, per_device, width, before=grads
    )
    return (mixed, d_tokens, d_combine, grad_gate, grad_up, grad_down)


def exchange_halves(value, axis, distance):
    mask = 2**distance
    pairs = [(source, source ^ mask) for source in range(lax.axis_size(axis))]
    return lax.ppermute(value, axis, pairs)


def dispatch_body(tokens, expert_ids, combine, cotangent, old_layout, pair_moves, gate_w, up_w, down_w):
    ep_count = lax.axis_size("ep")
    tp_count = lax.axis_size("tp")
    tok_count, top_k = expert_ids.shape
    expert_count = old_layout.shape[0]
    per_device = gate_w.shape[0]
    model_width = tokens.shape[1]
    share_width = model_width // tp_count
    capacity = 3 * tok_count * top_k // (2 * expert_count)
    pair_count = ep_count // 2
    swap_bit = ep_count.bit_length() - 2
    my_index = lax.axis_index("ep")
    my_share = lax.axis_index("tp")
    my_move = pair_moves[my_index] == 1
    slot_ids = jnp.arange(expert_count, dtype=jnp.int32)
    slot_device = slot_ids // per_device
    slot_local = slot_ids % per_device
    moved = (slot_local == per_device - 1) & (pair_moves[slot_device] == 1)
    source_slot = jnp.where(
        moved, (slot_device + pair_count) % ep_count * per_device + slot_local, slot_ids
    )
    new_layout = jnp.sum(
        jnp.where(source_slot[:, None] == slot_ids[None, :], old_layout[None, :], 0), axis=1
    )
    w_gate, w_up, w_down = (gate_w, up_w, down_w)
    arrived = exchange_halves(
        (gate_w[per_device - 1], up_w[per_device - 1], down_w[per_device - 1]), "ep", swap_bit
    )
    w_gate = jnp.concatenate(
        [gate_w[:-1], jnp.where(my_move, arrived[0], gate_w[-1])[None]], axis=0
    )
    w_up = jnp.concatenate([up_w[:-1], jnp.where(my_move, arrived[1], up_w[-1])[None]], axis=0)
    w_down = jnp.concatenate(
        [down_w[:-1], jnp.where(my_move, arrived[2], down_w[-1])[None]], axis=0
    )
    slot_of = jnp.sum(
        jnp.where(new_layout[None, :] == slot_ids[:, None], slot_ids[None, :], 0), axis=1
    )
    flat_ids = expert_ids.reshape(-1)
    onehot = (flat_ids[:, None] == slot_ids[None, :]).astype(jnp.int32)
    before = jnp.cumsum(onehot, axis=0) - onehot
    position = jnp.sum(before * onehot, axis=1)
    target_slot = jnp.sum(onehot * slot_of[None, :], axis=1)
    target_device = target_slot // per_device
    target_local = target_slot % per_device
    row_index = target_local * (ep_count * capacity) + target_device * capacity + position
    rows_total = expert_count * capacity
    matches = jnp.arange(rows_total, dtype=jnp.int32)[:, None] == row_index[None, :]
    select = jnp.sum(
        matches.reshape(rows_total, tok_count, top_k).astype(jnp.int32), axis=2
    ).astype(jnp.bfloat16)
    row_weight = jnp.sum(jnp.where(matches, combine.reshape(-1)[None, :], 0.0), axis=1)

    def dispatch(source, scaling):
        portion = lax.dynamic_slice_in_dim(source, my_share * share_width, share_width, 1)
        picked = jnp.dot(select, portion, preferred_element_type=jnp.float32)
        if scaling is not None:
            picked = picked * scaling[:, None]
        buffer = picked.astype(jnp.bfloat16).reshape(per_device, ep_count * capacity, share_width)
        landed = lax.all_to_all(buffer, "ep", split_axis=1, concat_axis=1, tiled=True)
        return lax.all_gather(landed, "tp", axis=2, tiled=True)

    def send_back(partial_value):
        shares = lax.psum_scatter(partial_value, "tp", scatter_dimension=2, tiled=True).astype(
            jnp.bfloat16
        )
        returned = lax.all_to_all(shares, "ep", split_axis=1, concat_axis=1, tiled=True)
        return returned.reshape(rows_total, share_width)[row_index].reshape(
            tok_count, top_k, share_width
        )

    rows_in = dispatch(tokens, None)
    gate = jnp.einsum("erd,edf->erf", rows_in, w_gate, preferred_element_type=jnp.float32)
    upper = jnp.einsum("erd,edf->erf", rows_in, w_up, preferred_element_type=jnp.float32)
    sigma = jax.nn.sigmoid(gate)
    active = gate * sigma
    hidden = (active * upper).astype(jnp.bfloat16)
    out_part = jnp.einsum("erf,efd->erd", hidden, w_down, preferred_element_type=jnp.float32)
    out_rows = send_back(out_part).astype(jnp.float32)
    mixed = jnp.einsum("tk,tkd->td", combine, out_rows).astype(jnp.bfloat16)
    cot_share = lax.dynamic_slice_in_dim(cotangent, my_share * share_width, share_width, 1).astype(
        jnp.float32
    )
    combine_part = jnp.einsum("td,tkd->tk", cot_share, out_rows)
    d_combine = lax.psum(combine_part, "tp")
    rows_grad = dispatch(cotangent, row_weight)
    d_hidden = jnp.einsum("erd,efd->erf", rows_grad, w_down, preferred_element_type=jnp.float32)
    d_gate = (d_hidden * upper * sigma * (1.0 + gate * (1.0 - sigma))).astype(jnp.bfloat16)
    d_up = (d_hidden * active).astype(jnp.bfloat16)
    back_part = jnp.einsum(
        "erf,edf->erd", d_gate, w_gate, preferred_element_type=jnp.float32
    ) + jnp.einsum("erf,edf->erd", d_up, w_up, preferred_element_type=jnp.float32)
    back_rows = send_back(back_part)
    d_tokens = jnp.sum(back_rows.astype(jnp.float32), axis=1).astype(jnp.bfloat16)
    grad_gate = jnp.einsum(
        "erd,erf->edf", rows_in, d_gate, preferred_element_type=jnp.float32
    ).astype(jnp.bfloat16)
    grad_up = jnp.einsum("erd,erf->edf", rows_in, d_up, preferred_element_type=jnp.float32).astype(
        jnp.bfloat16
    )
    grad_down = jnp.einsum(
        "erf,erd->efd", hidden, rows_grad, preferred_element_type=jnp.float32
    ).astype(jnp.bfloat16)
    return (mixed, d_tokens, d_combine, grad_gate, grad_up, grad_down)


def body(*operands):
    expert_ids, old_layout = operands[1], operands[4]
    tok_count, top_k = expert_ids.shape
    ep_count = lax.axis_size("ep")
    rows = 3 * tok_count * top_k * ep_count // (2 * old_layout.shape[0]) * operands[6].shape[0]
    gather = ep_count * tok_count <= 2 * rows and old_layout.shape[0] <= 256
    return (gather_body if gather else dispatch_body)(*operands)


def solution(mesh):
    return jax.shard_map(
        body,
        mesh=mesh,
        in_specs=(
            P("ep", None),
            P("ep", None),
            P("ep", None),
            P("ep", None),
            P(),
            P(),
            P("ep", None, "tp"),
            P("ep", None, "tp"),
            P("ep", "tp", None),
        ),
        out_specs=(
            P("ep", "tp"),
            P("ep", "tp"),
            P("ep", None),
            P("ep", None, "tp"),
            P("ep", None, "tp"),
            P("ep", "tp", None),
        ),
        check_vma=False,
    )
```

```python
import functools

import jax
import jax.numpy as jnp
import numpy as np
from jax import lax
from jax.experimental import pallas as pl
from jax.experimental.pallas import tpu as pltpu
from jax.sharding import PartitionSpec as P

F32 = jnp.float32
BF16 = jnp.bfloat16


def ring_order(chips):
    return list(range(0, chips, 2)) + list(range(chips - 1, 0, -2))


def ring_pairs(order, hop):
    chips = len(order)
    return [
        (chip * 2 + core, order[(place + hop) % chips] * 2 + core)
        for place, chip in enumerate(order)
        for core in range(2)
    ]


def block_tables(order):
    chips = len(order)
    half = chips // 2
    groups = [[0]] + [[-step, step] for step in range(1, half)] + [[half]]
    ep_count = 2 * chips
    arrival = np.zeros((ep_count, ep_count), np.int32)
    for place, chip in enumerate(order):
        for core in range(2):
            arrival[chip * 2 + core] = [
                order[(place + hop) % chips] * 2 + (core ^ side)
                for hops in groups
                for side in range(2)
                for hop in hops
            ]
    spot = np.argsort(arrival, axis=1).astype(np.int32)
    partner = np.arange(ep_count) ^ (ep_count // 2)
    from_partner = np.take_along_axis(spot[partner], arrival, axis=1).astype(np.int32)
    return arrival, spot, from_partner


def dot(a, b, ca, cb):
    return lax.dot_general(a, b, (((ca,), (cb,)), ((), ())), preferred_element_type=F32)


def group_kernel(pieces, top_k, capacity, tile, tile_out, facts, *refs):
    blocks, (gate_w, up_w, down_w) = refs[:pieces], refs[pieces : pieces + 3]
    act_outs, sum_outs, (d_weights, packed, picks) = refs[pieces + 3 : pieces + 6], refs[pieces + 6 : pieces + 10], refs[pieces + 10 : pieces + 13]
    x_all, cot_all, notes_all, gate_v, up_v, down_v, hidden_v, d_gate_v, d_up_v = refs[pieces + 13 : pieces + 22]
    sums, (fetched, loaded, stored) = refs[pieces + 22 : pieces + 26], refs[pieces + 26 :]
    per_device, width, units = gate_w.shape
    both = per_device * units
    tok_count, lanes = blocks[0].shape[0], notes_all.shape[1]
    share = sums[0].shape[2]

    def fetches(part):
        target = (x_all, cot_all, notes_all)[part]
        return [
            pltpu.make_async_copy(
                ref.at[:, pl.ds(part * width, target.shape[1])],
                target.at[pl.ds(piece * tok_count, tok_count), :],
                fetched.at[part, piece],
            )
            for piece, ref in enumerate(blocks)
        ]

    def load(which, slot):
        if which == 2:
            rows = pl.ds(slot * units, units)
            return pltpu.make_async_copy(down_w.at[rows, :], down_v.at[rows, :], loaded.at[which, slot])
        source, target = ((gate_w, gate_v), (up_w, up_v))[which]
        return pltpu.make_async_copy(
            source.at[slot], target.at[:, pl.ds(slot * units, units)], loaded.at[which, slot]
        )

    for fetch in fetches(2) + fetches(0):
        fetch.start()
    load(0, 0).start()
    load(1, 0).start()
    for fetch in fetches(1):
        fetch.start()
    load(2, 0).start()
    for slot in range(1, per_device):
        for which in range(3):
            load(which, slot).start()
    for fetch in fetches(2):
        fetch.wait()
    said = notes_all[...].astype(F32)
    lane = lax.broadcasted_iota(jnp.int32, said.shape, 1)
    ids = jnp.where(lane < top_k, said, -1.0).astype(jnp.int32)
    weight = pltpu.roll(said, lanes - top_k, 1) + (
        pltpu.roll(said, lanes - 2 * top_k, 1) + pltpu.roll(said, lanes - 3 * top_k, 1)
    )
    gains = [
        jnp.sum(jnp.where(ids == facts[1 + slot], weight, 0.0), axis=1, keepdims=True) for slot in range(per_device)
    ]
    traded_sums = [0.0] * per_device
    for fetch in fetches(0):
        fetch.wait()
    slots_in = 0
    for at in range(0, both, tile):
        columns = slice(at, at + tile)
        fresh = range(slots_in, (at + tile - 1) // units + 1)
        slots_in = (at + tile - 1) // units + 1
        for slot in fresh:
            load(0, slot).wait()
            load(1, slot).wait()
        gate = dot(x_all[...], gate_v[:, columns], 1, 0)
        upper = dot(x_all[...], up_v[:, columns], 1, 0)
        if at == 0:
            for fetch in fetches(1):
                fetch.wait()
        for slot in fresh:
            load(2, slot).wait()
        pulled = dot(cot_all[...], down_v[columns, :], 1, 1)
        sigma = jax.nn.sigmoid(gate)
        active = gate * sigma
        hidden = active * upper
        traded = hidden * pulled
        parts = [(part // units, part - at) for part in range(at, at + tile, lanes)]
        for slot, part in parts:
            traded_sums[slot] += jnp.sum(traded[:, part : part + lanes], axis=1, keepdims=True)
        gain = jnp.concatenate([jnp.broadcast_to(gains[slot], said.shape) for slot, _ in parts], axis=1)
        d_hidden = pulled * gain
        hidden_v[:, columns] = (hidden * gain).astype(BF16)
        d_gate_v[:, columns] = (d_hidden * upper * sigma * (1.0 + gate * (1.0 - sigma))).astype(BF16)
        d_up_v[:, columns] = (d_hidden * active).astype(BF16)

    stores = [
        pltpu.make_async_copy(source, target, stored.at[i])
        for i, (source, target) in enumerate(zip((hidden_v, d_gate_v, d_up_v, *sums), (*act_outs, *sum_outs)))
    ]
    for store in stores[:3]:
        store.start()
    d_weights[...] = sum(
        jnp.where(ids == facts[1 + slot], traded_sums[slot], 0.0) for slot in range(per_device)
    )

    near = pieces // 2 * tok_count
    for which in range(2):
        first = jnp.where(which == 0, 1 - facts[0], facts[0]) * share
        for at in range(0, share, tile_out):
            features = pl.ds(pl.multiple_of(first + at, tile_out), tile_out)
            out = dot(hidden_v[...], down_v[:, features], 1, 0).astype(BF16)
            back = dot(d_gate_v[...], gate_v[features, :], 1, 1) + dot(d_up_v[...], up_v[features, :], 1, 1)
            back = back.astype(BF16)
            columns = slice(at, at + tile_out)
            for kind, value in enumerate((out, back)):
                sums[2 * which][kind, :, columns] = value[:near]
                sums[2 * which + 1][kind, :, columns] = value[near:]
        for store in stores[3 + 2 * which : 5 + 2 * which]:
            store.start()

    row = lax.broadcasted_iota(jnp.int32, (tok_count, tok_count), 0)
    column = lax.broadcasted_iota(jnp.int32, (tok_count, tok_count), 1)
    earlier = jnp.where(column < row, 1.0, 0.0).astype(BF16)
    tail = slice((per_device - 1) * units, per_device * units)

    def pick_of(rows, expert):
        named = jnp.max(jnp.where(ids[rows] == expert, 1.0, 0.0), axis=1, keepdims=True)
        mask = jnp.broadcast_to(named, (tok_count, tok_count))
        position = dot(earlier, mask.astype(BF16), 1, 0).astype(jnp.int32)
        return jnp.where((position == column) & (mask > 0.0), 1.0, 0.0).astype(BF16)

    for piece in range(pieces):
        rows = slice(piece * tok_count, (piece + 1) * tok_count)
        pick = pick_of(rows, facts[per_device])
        for at, ref in enumerate((hidden_v, d_gate_v, d_up_v)):
            packed[piece, :, at * units : (at + 1) * units] = dot(pick, ref[rows, tail], 0, 0).astype(BF16)[:capacity]
        picks[piece] = pick_of(rows, facts[1 + per_device])
    for store in stores:
        store.wait()


def group_call(blocks, facts, weights, top_k, capacity, share):
    pieces = len(blocks)
    per_device, width, units = weights[0].shape
    both = per_device * units
    tok_count = blocks[0].shape[0]
    rows = pieces * tok_count
    lanes = 128
    anywhere, vmem = pl.BlockSpec(memory_space=pl.ANY), pl.BlockSpec(memory_space=pltpu.VMEM)
    act, total = (rows, both), (2, rows // 2, share)
    return pl.pallas_call(
        functools.partial(group_kernel, pieces, top_k, capacity, 256, 512),
        in_specs=[pl.BlockSpec(memory_space=pltpu.SMEM)] + [anywhere] * (pieces + 3),
        out_specs=[anywhere] * 7 + [vmem] * 3,
        out_shape=[jax.ShapeDtypeStruct(act, BF16)] * 3
        + [jax.ShapeDtypeStruct(total, BF16)] * 4
        + [
            jax.ShapeDtypeStruct((rows, lanes), F32),
            jax.ShapeDtypeStruct((pieces, capacity, 3 * units), BF16),
            jax.ShapeDtypeStruct((pieces, tok_count, tok_count), BF16),
        ],
        scratch_shapes=[pltpu.VMEM((rows, width), BF16)] * 2
        + [pltpu.VMEM((rows, lanes), BF16)]
        + [pltpu.VMEM((width, both), BF16)] * 2
        + [pltpu.VMEM((both, width), BF16)]
        + [pltpu.VMEM(act, BF16)] * 3
        + [pltpu.VMEM(total, BF16)] * 4
        + [
            pltpu.SemaphoreType.DMA((3, pieces)),
            pltpu.SemaphoreType.DMA((3, per_device)),
            pltpu.SemaphoreType.DMA((7,)),
        ],
        compiler_params=pltpu.CompilerParams(vmem_limit_bytes=56 * 1024 * 1024),
        cost_estimate=pl.CostEstimate(
            flops=12 * rows * width * both,
            bytes_accessed=6 * width * both + 12 * rows * width,
            transcendentals=rows * both,
        ),
    )(facts, *blocks, *weights)


def grad_kernel(blocks, moved, sides, slot, tile, facts, *refs):
    pieces, refs = refs[:blocks], refs[blocks:]
    out_count = 2 * sides[0] + sides[1]
    outs, (x_all, cot_all, hidden, d_both, gate_v, up_v, down_v, gathered) = refs[-11 - out_count : -11], refs[-11:-3]
    fetched, taken, stored = refs[-3:]
    acts = refs[: -11 - out_count * (2 if moved else 1)]
    tok_count, (width, units) = pieces[0].shape[0], gate_v.shape

    def fetches(part):
        return [
            pltpu.make_async_copy(
                ref.at[:, pl.ds(part * width, width)],
                (x_all, cot_all)[part].at[pl.ds(piece * tok_count, tok_count), :],
                fetched.at[part, piece],
            )
            for piece, ref in enumerate(pieces)
        ]

    takes = []
    if not moved:
        third = len(acts) // 3
        for which in range(3):
            at = 0
            for group, ref in enumerate(acts[which * third : (which + 1) * third]):
                rows = pl.ds(at, ref.shape[0])
                target = hidden.at[rows, :] if which == 0 else d_both.at[rows, pl.ds((which - 1) * units, units)]
                source = ref.at[:, pl.ds(slot * units, units)]
                takes.append(pltpu.make_async_copy(source, target, taken.at[which, group]))
                at += ref.shape[0]
    for copy in takes + [copy for part in range(2) if sides[part] for copy in fetches(part)]:
        copy.start()
    if moved:
        groups = len(acts) // 3
        picks, own = acts[:groups], acts[groups : 2 * groups]
        block = 0
        for ref in acts[2 * groups :]:
            gathered[block : block + ref.shape[0]] = ref[...]
            block += ref.shape[0]
        block = 0
        for ref, mine in zip(picks, own):
            for piece in range(ref.shape[0]):
                packed = jnp.where(facts[0] == 1, gathered[facts[1 + block]], mine[piece])
                spread = dot(ref[piece][:, : mine.shape[1]], packed, 1, 0).astype(BF16)
                rows = slice(block * tok_count, (block + 1) * tok_count)
                hidden[rows] = spread[:, :units]
                d_both[rows] = spread[:, units:]
                block += 1
    for copy in takes + (fetches(0) if sides[0] else []):
        copy.wait()

    def each(body):
        lax.fori_loop(0, width // tile, lambda i, _: body(pl.ds(pl.multiple_of(i * tile, tile), tile)), None)

    def into_columns(features):
        pair = dot(x_all[:, features], d_both[...], 0, 0).astype(BF16)
        gate_v[features, :] = pair[:, :units]
        up_v[features, :] = pair[:, units:]

    def into_rows(features):
        down_v[:, features] = dot(hidden[...], cot_all[:, features], 0, 0).astype(BF16)

    sources = (gate_v, up_v) * sides[0] + (down_v,) * sides[1]
    stores = [
        pltpu.make_async_copy(source, target.at[slot], stored.at[i])
        for i, (source, target) in enumerate(zip(sources, outs))
    ]
    if sides[0]:
        each(into_columns)
        for store in stores[:2]:
            store.start()
    if sides[1]:
        for copy in fetches(1):
            copy.wait()
        each(into_rows)
        stores[-1].start()
    for store in stores:
        store.wait()


def grad_call(pieces, acts, facts, slot, units, per_device, width, sides=(1, 1), before=None):
    moved = before is not None
    tok_count = pieces[0].shape[0]
    total = len(pieces) * tok_count
    anywhere, vmem = pl.BlockSpec(memory_space=pl.ANY), pl.BlockSpec(memory_space=pltpu.VMEM)
    arrays = list(pieces) + list(acts) + list(before or ())
    shapes = [(per_device, width, units)] * (2 * sides[0]) + [(per_device, units, width)] * sides[1]
    row_blocks = (len(pieces),) + acts[-1].shape[1:] if moved else (1, 16, 128)
    return pl.pallas_call(
        functools.partial(grad_kernel, len(pieces), moved, sides, slot, 512),
        in_specs=[pl.BlockSpec(memory_space=pltpu.SMEM)]
        + [anywhere] * len(pieces)
        + [vmem if moved else anywhere] * len(acts)
        + [anywhere] * len(before or ()),
        out_specs=[anywhere] * len(shapes),
        out_shape=[jax.ShapeDtypeStruct(shape, BF16) for shape in shapes],
        scratch_shapes=[pltpu.VMEM((total, width), BF16)] * 2
        + [pltpu.VMEM((total, units), BF16), pltpu.VMEM((total, 2 * units), BF16)]
        + [pltpu.VMEM((width, units), BF16)] * 2
        + [pltpu.VMEM((units, width), BF16), pltpu.VMEM(row_blocks, BF16)]
        + [
            pltpu.SemaphoreType.DMA((2, len(pieces))),
            pltpu.SemaphoreType.DMA((3, len(acts))),
            pltpu.SemaphoreType.DMA((3,)),
        ],
        input_output_aliases={1 + len(arrays) - len(shapes) + i: i for i in range(len(shapes))} if moved else {},
        compiler_params=pltpu.CompilerParams(vmem_limit_bytes=56 * 1024 * 1024),
        cost_estimate=pl.CostEstimate(
            flops=6 * total * width * units, bytes_accessed=4 * total * width, transcendentals=0
        ),
    )(facts, *arrays)


def gather_body(tokens, expert_ids, combine, cotangent, old_layout, pair_moves, gate_w, up_w, down_w):
    ep_count = lax.axis_size("ep")
    tp_count = lax.axis_size("tp")
    tok_count, top_k = expert_ids.shape
    expert_count = old_layout.shape[0]
    per_device, width, units = gate_w.shape
    share = width // tp_count
    capacity = 3 * tok_count * top_k // (2 * expert_count)
    chips = ep_count // 2
    half = chips // 2
    order = ring_order(chips)
    forward, backward = ring_pairs(order, 1), ring_pairs(order, -1)
    by_core = [(forward if pair[0] % 2 == 0 else backward)[i] for i, pair in enumerate(forward)]
    other_core = [(i, i ^ 1) for i in range(ep_count)]
    other_share = [(i, i ^ 1) for i in range(tp_count)]
    partners = [(i, i ^ (ep_count // 2)) for i in range(ep_count)]
    me = lax.axis_index("ep")
    my_share = lax.axis_index("tp")
    core = me % 2
    spot, from_partner = (jnp.asarray(table)[me] for table in block_tables(order)[1:])

    my_move = pair_moves[me] == 1
    last = per_device - 1
    experts = lax.dynamic_slice_in_dim(old_layout, me * per_device, per_device, 0)
    partner_last = old_layout[(me ^ (ep_count // 2)) * per_device + last]
    new_last = jnp.where(my_move, partner_last, experts[last])
    facts = jnp.concatenate([my_share[None], experts, new_last[None]]).astype(jnp.int32)
    weights = (gate_w, up_w, down_w.reshape(per_device * units, width))

    parts = [expert_ids.astype(F32)]
    rest = combine
    for _ in range(3):
        parts.append(lax.reduce_precision(rest, 8, 7))
        rest = rest - parts[-1]
    notes = jnp.concatenate(parts, axis=1)
    notes = jnp.pad(notes, ((0, 0), (0, -notes.shape[1] % 128))).astype(BF16)
    payload = jnp.concatenate([tokens, cotangent, notes], axis=1)

    def add(*values):
        return sum(value.astype(F32) for value in values).astype(BF16)

    def exchange(near_other, near_mine, far_other, far_mine):
        sent = add(near_other, lax.ppermute(far_other, "ep", other_core))
        return near_mine, lax.ppermute(far_mine, "ep", other_core), lax.ppermute(sent, "tp", other_share)

    move_facts = jnp.concatenate([my_move.astype(jnp.int32)[None], from_partner])
    kept_groups, totals, swapped = [], [], {}
    right = left = payload
    pending = crossing = None
    for step in range(half + 1):
        near = [payload] if step == 0 else [right, left] if step < half else [right]
        far = [lax.ppermute(piece, "ep", other_core) for piece in near]
        pieces = near + far
        if step < half - 1:
            right = lax.ppermute(right, "ep", forward)
            left = lax.ppermute(left, "ep", backward)
        elif step == half - 1:
            right = lax.ppermute(jnp.where(core == 0, right, left), "ep", by_core)
        crossing = pending and exchange(*pending)
        result = group_call(pieces, facts, weights, top_k, capacity, share)
        acts, (near_other, far_other, near_mine, far_mine), rest = result[:3], result[3:7], result[7:]
        pending = (near_other, near_mine, far_other, far_mine)
        group = (acts, rest)
        if step == half - 1:
            swapped[1] = lax.ppermute(kept_groups[1][2][1], "ep", partners)
        right, left, pending, crossing, group, move_facts, swapped = lax.optimization_barrier(
            (right, left, pending, crossing, group, move_facts, swapped)
        )
        if crossing:
            totals.append(crossing)
        kept_groups.append((pieces, *group))
    near_other, near_mine, far_other, far_mine = pending
    sent = add(near_other, lax.ppermute(far_other, "ep", other_core))
    stay_facts = jnp.zeros((1,), jnp.int32)
    for number in (0, *range(2, half - 1)):
        swapped[number] = lax.ppermute(kept_groups[number][2][1], "ep", partners)
    sent, stay_facts, swapped = lax.optimization_barrier((sent, stay_facts, swapped))
    last_three = near_mine, lax.ppermute(far_mine, "ep", other_core), lax.ppermute(sent, "tp", other_share)

    for number in (half - 1, half):
        swapped[number] = lax.ppermute(kept_groups[number][2][1], "ep", partners)

    every = [piece for group in kept_groups for piece in group[0]]
    grads = None
    for slot in range(last):
        own_acts = [group[1][i] for i in range(3) for group in kept_groups]
        grads = grad_call(every, own_acts, stay_facts, slot, units, per_device, width)

    d_weights = jnp.concatenate([group[2][0] for group in kept_groups])[:, :top_k]
    d_weights = d_weights + lax.ppermute(d_weights, "tp", other_share)
    totals = [add(*parts) for parts in totals]
    last_three, grads, d_weights, swapped, totals = lax.optimization_barrier(
        (last_three, grads, d_weights, swapped, totals)
    )

    farthest = add(*last_three)
    met = [lax.ppermute(farthest[kind], "ep", by_core) for kind in range(2)]
    met, move_facts = lax.optimization_barrier((met, move_facts))
    by_hop = {0: totals[0]}
    for step in range(1, half):
        by_hop[-step], by_hop[step] = totals[step][:, :tok_count], totals[step][:, tok_count:]
    moved_acts = [group[2][2] for group in kept_groups] + [group[2][1] for group in kept_groups]
    moved_acts += [swapped[number] for number in range(half + 1)]

    def moved_grads(sides, before):
        return grad_call(every, moved_acts, move_facts, last, units, per_device, width, sides, before)

    (grad_down,) = moved_grads((0, 1), grads[2:])
    none = jnp.zeros_like(met[0])
    sums = [(jnp.where(core == 0, value, none), jnp.where(core == 0, none, value)) for value in met]
    for step in range(half - 1, 0, -1):
        sums = [
            (
                lax.ppermute(add(by_hop[step][kind], sums[kind][0]), "ep", forward),
                lax.ppermute(add(by_hop[-step][kind], sums[kind][1]), "ep", backward),
            )
            for kind in range(2)
        ]
        if step == half - 1:
            sums, grad_down, d_weights = lax.optimization_barrier((sums, grad_down, d_weights))
            d_weights = jnp.take(d_weights.reshape(ep_count, tok_count, top_k), spot, axis=0)
            d_weights = lax.all_to_all(d_weights.transpose(0, 2, 1), "ep", split_axis=0, concat_axis=0, tiled=True)
            d_combine = jnp.sum(d_weights, axis=0).T
        elif step == 2:
            sums, move_facts, d_combine = lax.optimization_barrier((sums, move_facts, d_combine))
    grad_gate, grad_up = moved_grads((1, 0), grads[:2])
    mixed, d_tokens = (add(by_hop[0][kind], *sums[kind]) for kind in range(2))

    return (mixed, d_tokens, d_combine, grad_gate, grad_up, grad_down)


def exchange_halves(value, axis, distance):
    mask = 2**distance
    pairs = [(source, source ^ mask) for source in range(lax.axis_size(axis))]
    return lax.ppermute(value, axis, pairs)


def dispatch_body(tokens, expert_ids, combine, cotangent, old_layout, pair_moves, gate_w, up_w, down_w):
    ep_count = lax.axis_size("ep")
    tp_count = lax.axis_size("tp")
    tok_count, top_k = expert_ids.shape
    expert_count = old_layout.shape[0]
    per_device = gate_w.shape[0]
    model_width = tokens.shape[1]
    share_width = model_width // tp_count
    capacity = 3 * tok_count * top_k // (2 * expert_count)
    pair_count = ep_count // 2
    swap_bit = ep_count.bit_length() - 2
    my_index = lax.axis_index("ep")
    my_share = lax.axis_index("tp")
    my_move = pair_moves[my_index] == 1
    slot_ids = jnp.arange(expert_count, dtype=jnp.int32)
    slot_device = slot_ids // per_device
    slot_local = slot_ids % per_device
    moved = (slot_local == per_device - 1) & (pair_moves[slot_device] == 1)
    source_slot = jnp.where(
        moved, (slot_device + pair_count) % ep_count * per_device + slot_local, slot_ids
    )
    new_layout = jnp.sum(
        jnp.where(source_slot[:, None] == slot_ids[None, :], old_layout[None, :], 0), axis=1
    )
    w_gate, w_up, w_down = (gate_w, up_w, down_w)
    arrived = exchange_halves(
        (gate_w[per_device - 1], up_w[per_device - 1], down_w[per_device - 1]), "ep", swap_bit
    )
    w_gate = jnp.concatenate(
        [gate_w[:-1], jnp.where(my_move, arrived[0], gate_w[-1])[None]], axis=0
    )
    w_up = jnp.concatenate([up_w[:-1], jnp.where(my_move, arrived[1], up_w[-1])[None]], axis=0)
    w_down = jnp.concatenate(
        [down_w[:-1], jnp.where(my_move, arrived[2], down_w[-1])[None]], axis=0
    )
    slot_of = jnp.sum(
        jnp.where(new_layout[None, :] == slot_ids[:, None], slot_ids[None, :], 0), axis=1
    )
    flat_ids = expert_ids.reshape(-1)
    onehot = (flat_ids[:, None] == slot_ids[None, :]).astype(jnp.int32)
    before = jnp.cumsum(onehot, axis=0) - onehot
    position = jnp.sum(before * onehot, axis=1)
    target_slot = jnp.sum(onehot * slot_of[None, :], axis=1)
    target_device = target_slot // per_device
    target_local = target_slot % per_device
    row_index = target_local * (ep_count * capacity) + target_device * capacity + position
    rows_total = expert_count * capacity
    matches = jnp.arange(rows_total, dtype=jnp.int32)[:, None] == row_index[None, :]
    select = jnp.sum(
        matches.reshape(rows_total, tok_count, top_k).astype(jnp.int32), axis=2
    ).astype(jnp.bfloat16)
    row_weight = jnp.sum(jnp.where(matches, combine.reshape(-1)[None, :], 0.0), axis=1)

    def dispatch(source, scaling):
        portion = lax.dynamic_slice_in_dim(source, my_share * share_width, share_width, 1)
        picked = jnp.dot(select, portion, preferred_element_type=jnp.float32)
        if scaling is not None:
            picked = picked * scaling[:, None]
        buffer = picked.astype(jnp.bfloat16).reshape(per_device, ep_count * capacity, share_width)
        landed = lax.all_to_all(buffer, "ep", split_axis=1, concat_axis=1, tiled=True)
        return lax.all_gather(landed, "tp", axis=2, tiled=True)

    def send_back(partial_value):
        shares = lax.psum_scatter(partial_value, "tp", scatter_dimension=2, tiled=True).astype(
            jnp.bfloat16
        )
        returned = lax.all_to_all(shares, "ep", split_axis=1, concat_axis=1, tiled=True)
        return returned.reshape(rows_total, share_width)[row_index].reshape(
            tok_count, top_k, share_width
        )

    rows_in = dispatch(tokens, None)
    gate = jnp.einsum("erd,edf->erf", rows_in, w_gate, preferred_element_type=jnp.float32)
    upper = jnp.einsum("erd,edf->erf", rows_in, w_up, preferred_element_type=jnp.float32)
    sigma = jax.nn.sigmoid(gate)
    active = gate * sigma
    hidden = (active * upper).astype(jnp.bfloat16)
    out_part = jnp.einsum("erf,efd->erd", hidden, w_down, preferred_element_type=jnp.float32)
    out_rows = send_back(out_part).astype(jnp.float32)
    mixed = jnp.einsum("tk,tkd->td", combine, out_rows).astype(jnp.bfloat16)
    cot_share = lax.dynamic_slice_in_dim(cotangent, my_share * share_width, share_width, 1).astype(
        jnp.float32
    )
    combine_part = jnp.einsum("td,tkd->tk", cot_share, out_rows)
    d_combine = lax.psum(combine_part, "tp")
    rows_grad = dispatch(cotangent, row_weight)
    d_hidden = jnp.einsum("erd,efd->erf", rows_grad, w_down, preferred_element_type=jnp.float32)
    d_gate = (d_hidden * upper * sigma * (1.0 + gate * (1.0 - sigma))).astype(jnp.bfloat16)
    d_up = (d_hidden * active).astype(jnp.bfloat16)
    back_part = jnp.einsum(
        "erf,edf->erd", d_gate, w_gate, preferred_element_type=jnp.float32
    ) + jnp.einsum("erf,edf->erd", d_up, w_up, preferred_element_type=jnp.float32)
    back_rows = send_back(back_part)
    d_tokens = jnp.sum(back_rows.astype(jnp.float32), axis=1).astype(jnp.bfloat16)
    grad_gate = jnp.einsum(
        "erd,erf->edf", rows_in, d_gate, preferred_element_type=jnp.float32
    ).astype(jnp.bfloat16)
    grad_up = jnp.einsum("erd,erf->edf", rows_in, d_up, preferred_element_type=jnp.float32).astype(
        jnp.bfloat16
    )
    grad_down = jnp.einsum(
        "erf,erd->efd", hidden, rows_grad, preferred_element_type=jnp.float32
    ).astype(jnp.bfloat16)
    return (mixed, d_tokens, d_combine, grad_gate, grad_up, grad_down)


def body(*operands):
    expert_ids, old_layout = operands[1], operands[4]
    tok_count, top_k = expert_ids.shape
    ep_count = lax.axis_size("ep")
    rows = 3 * tok_count * top_k * ep_count // (2 * old_layout.shape[0]) * operands[6].shape[0]
    gather = ep_count * tok_count <= 2 * rows and old_layout.shape[0] <= 256
    return (gather_body if gather else dispatch_body)(*operands)


def solution(mesh):
    return jax.shard_map(
        body,
        mesh=mesh,
        in_specs=(
            P("ep", None),
            P("ep", None),
            P("ep", None),
            P("ep", None),
            P(),
            P(),
            P("ep", None, "tp"),
            P("ep", None, "tp"),
            P("ep", "tp", None),
        ),
        out_specs=(
            P("ep", "tp"),
            P("ep", "tp"),
            P("ep", None),
            P("ep", None, "tp"),
            P("ep", None, "tp"),
            P("ep", "tp", None),
        ),
        check_vma=False,
    )
```

```python
import functools

import jax
import jax.numpy as jnp
import numpy as np
from jax import lax
from jax.experimental import pallas as pl
from jax.experimental.pallas import tpu as pltpu
from jax.sharding import PartitionSpec as P

F32 = jnp.float32
BF16 = jnp.bfloat16


def ring_order(chips):
    return list(range(0, chips, 2)) + list(range(chips - 1, 0, -2))


def ring_pairs(order, hop):
    chips = len(order)
    return [
        (chip * 2 + core, order[(place + hop) % chips] * 2 + core)
        for place, chip in enumerate(order)
        for core in range(2)
    ]


def block_tables(order):
    chips = len(order)
    half = chips // 2
    groups = [[0]] + [[-step, step] for step in range(1, half)] + [[half]]
    ep_count = 2 * chips
    arrival = np.zeros((ep_count, ep_count), np.int32)
    for place, chip in enumerate(order):
        for core in range(2):
            arrival[chip * 2 + core] = [
                order[(place + hop) % chips] * 2 + (core ^ side)
                for hops in groups
                for side in range(2)
                for hop in hops
            ]
    spot = np.argsort(arrival, axis=1).astype(np.int32)
    partner = np.arange(ep_count) ^ (ep_count // 2)
    from_partner = np.take_along_axis(spot[partner], arrival, axis=1).astype(np.int32)
    return arrival, spot, from_partner


def dot(a, b, ca, cb):
    return lax.dot_general(a, b, (((ca,), (cb,)), ((), ())), preferred_element_type=F32)


def group_kernel(pieces, top_k, capacity, tile, tile_out, facts, *refs):
    blocks, (gate_w, up_w, down_w) = refs[:pieces], refs[pieces : pieces + 3]
    act_outs, sum_outs, (d_weights, packed, picks) = refs[pieces + 3 : pieces + 6], refs[pieces + 6 : pieces + 10], refs[pieces + 10 : pieces + 13]
    x_all, cot_all, notes_all, gate_v, up_v, down_v, hidden_v, d_gate_v, d_up_v = refs[pieces + 13 : pieces + 22]
    sums, (fetched, loaded, stored) = refs[pieces + 22 : pieces + 26], refs[pieces + 26 :]
    per_device, width, units = gate_w.shape
    both = per_device * units
    tok_count, lanes = blocks[0].shape[0], notes_all.shape[1]
    share = sums[0].shape[2]

    def fetches(part):
        target = (x_all, cot_all, notes_all)[part]
        return [
            pltpu.make_async_copy(
                ref.at[:, pl.ds(part * width, target.shape[1])],
                target.at[pl.ds(piece * tok_count, tok_count), :],
                fetched.at[part, piece],
            )
            for piece, ref in enumerate(blocks)
        ]

    def load(which, slot):
        if which == 2:
            rows = pl.ds(slot * units, units)
            return pltpu.make_async_copy(down_w.at[rows, :], down_v.at[rows, :], loaded.at[which, slot])
        source, target = ((gate_w, gate_v), (up_w, up_v))[which]
        return pltpu.make_async_copy(
            source.at[slot], target.at[:, pl.ds(slot * units, units)], loaded.at[which, slot]
        )

    for fetch in fetches(2) + fetches(0):
        fetch.start()
    load(0, 0).start()
    load(1, 0).start()
    for fetch in fetches(1):
        fetch.start()
    load(2, 0).start()
    for slot in range(1, per_device):
        for which in range(3):
            load(which, slot).start()
    for fetch in fetches(2):
        fetch.wait()
    said = notes_all[...].astype(F32)
    lane = lax.broadcasted_iota(jnp.int32, said.shape, 1)
    ids = jnp.where(lane < top_k, said, -1.0).astype(jnp.int32)
    weight = pltpu.roll(said, lanes - top_k, 1) + (
        pltpu.roll(said, lanes - 2 * top_k, 1) + pltpu.roll(said, lanes - 3 * top_k, 1)
    )
    gains = [
        jnp.sum(jnp.where(ids == facts[1 + slot], weight, 0.0), axis=1, keepdims=True) for slot in range(per_device)
    ]
    traded_sums = [0.0] * per_device
    for fetch in fetches(0):
        fetch.wait()
    slots_in = 0
    for at in range(0, both, tile):
        columns = slice(at, at + tile)
        fresh = range(slots_in, (at + tile - 1) // units + 1)
        slots_in = (at + tile - 1) // units + 1
        for slot in fresh:
            load(0, slot).wait()
            load(1, slot).wait()
        gate = dot(x_all[...], gate_v[:, columns], 1, 0)
        upper = dot(x_all[...], up_v[:, columns], 1, 0)
        if at == 0:
            for fetch in fetches(1):
                fetch.wait()
        for slot in fresh:
            load(2, slot).wait()
        pulled = dot(cot_all[...], down_v[columns, :], 1, 1)
        sigma = jax.nn.sigmoid(gate)
        active = gate * sigma
        hidden = active * upper
        traded = hidden * pulled
        parts = [(part // units, part - at) for part in range(at, at + tile, lanes)]
        for slot, part in parts:
            traded_sums[slot] += jnp.sum(traded[:, part : part + lanes], axis=1, keepdims=True)
        gain = jnp.concatenate([jnp.broadcast_to(gains[slot], said.shape) for slot, _ in parts], axis=1)
        d_hidden = pulled * gain
        hidden_v[:, columns] = (hidden * gain).astype(BF16)
        d_gate_v[:, columns] = (d_hidden * upper * sigma * (1.0 + gate * (1.0 - sigma))).astype(BF16)
        d_up_v[:, columns] = (d_hidden * active).astype(BF16)

    stores = [
        pltpu.make_async_copy(source, target, stored.at[i])
        for i, (source, target) in enumerate(zip((hidden_v, d_gate_v, d_up_v, *sums), (*act_outs, *sum_outs)))
    ]
    for store in stores[:3]:
        store.start()
    d_weights[...] = sum(
        jnp.where(ids == facts[1 + slot], traded_sums[slot], 0.0) for slot in range(per_device)
    )

    near = pieces // 2 * tok_count
    for which in range(2):
        first = jnp.where(which == 0, 1 - facts[0], facts[0]) * share
        for at in range(0, share, tile_out):
            features = pl.ds(pl.multiple_of(first + at, tile_out), tile_out)
            out = dot(hidden_v[...], down_v[:, features], 1, 0).astype(BF16)
            back = dot(d_gate_v[...], gate_v[features, :], 1, 1) + dot(d_up_v[...], up_v[features, :], 1, 1)
            back = back.astype(BF16)
            columns = slice(at, at + tile_out)
            for kind, value in enumerate((out, back)):
                sums[2 * which][kind, :, columns] = value[:near]
                sums[2 * which + 1][kind, :, columns] = value[near:]
        for store in stores[3 + 2 * which : 5 + 2 * which]:
            store.start()

    row = lax.broadcasted_iota(jnp.int32, (tok_count, tok_count), 0)
    column = lax.broadcasted_iota(jnp.int32, (tok_count, tok_count), 1)
    earlier = jnp.where(column < row, 1.0, 0.0).astype(BF16)
    tail = slice((per_device - 1) * units, per_device * units)

    def pick_of(rows, expert):
        named = jnp.max(jnp.where(ids[rows] == expert, 1.0, 0.0), axis=1, keepdims=True)
        mask = jnp.broadcast_to(named, (tok_count, tok_count))
        position = dot(earlier, mask.astype(BF16), 1, 0).astype(jnp.int32)
        return jnp.where((position == column) & (mask > 0.0), 1.0, 0.0).astype(BF16)

    for piece in range(pieces):
        rows = slice(piece * tok_count, (piece + 1) * tok_count)
        pick = pick_of(rows, facts[per_device])
        for at, ref in enumerate((hidden_v, d_gate_v, d_up_v)):
            packed[piece, :, at * units : (at + 1) * units] = dot(pick, ref[rows, tail], 0, 0).astype(BF16)[:capacity]
        picks[piece] = pick_of(rows, facts[1 + per_device])
    for store in stores:
        store.wait()


def group_call(blocks, facts, weights, top_k, capacity, share):
    pieces = len(blocks)
    per_device, width, units = weights[0].shape
    both = per_device * units
    tok_count = blocks[0].shape[0]
    rows = pieces * tok_count
    lanes = 128
    anywhere, vmem = pl.BlockSpec(memory_space=pl.ANY), pl.BlockSpec(memory_space=pltpu.VMEM)
    act, total = (rows, both), (2, rows // 2, share)
    return pl.pallas_call(
        functools.partial(group_kernel, pieces, top_k, capacity, 256, 512),
        in_specs=[pl.BlockSpec(memory_space=pltpu.SMEM)] + [anywhere] * (pieces + 3),
        out_specs=[anywhere] * 7 + [vmem] * 3,
        out_shape=[jax.ShapeDtypeStruct(act, BF16)] * 3
        + [jax.ShapeDtypeStruct(total, BF16)] * 4
        + [
            jax.ShapeDtypeStruct((rows, lanes), F32),
            jax.ShapeDtypeStruct((pieces, capacity, 3 * units), BF16),
            jax.ShapeDtypeStruct((pieces, tok_count, tok_count), BF16),
        ],
        scratch_shapes=[pltpu.VMEM((rows, width), BF16)] * 2
        + [pltpu.VMEM((rows, lanes), BF16)]
        + [pltpu.VMEM((width, both), BF16)] * 2
        + [pltpu.VMEM((both, width), BF16)]
        + [pltpu.VMEM(act, BF16)] * 3
        + [pltpu.VMEM(total, BF16)] * 4
        + [
            pltpu.SemaphoreType.DMA((3, pieces)),
            pltpu.SemaphoreType.DMA((3, per_device)),
            pltpu.SemaphoreType.DMA((7,)),
        ],
        compiler_params=pltpu.CompilerParams(vmem_limit_bytes=56 * 1024 * 1024),
        cost_estimate=pl.CostEstimate(
            flops=12 * rows * width * both,
            bytes_accessed=6 * width * both + 12 * rows * width,
            transcendentals=rows * both,
        ),
    )(facts, *blocks, *weights)


def grad_kernel(blocks, moved, sides, slot, tile, facts, *refs):
    pieces, refs = refs[:blocks], refs[blocks:]
    out_count = 2 * sides[0] + sides[1]
    outs, (x_all, cot_all, hidden, d_both, gate_v, up_v, down_v, gathered) = refs[-11 - out_count : -11], refs[-11:-3]
    fetched, taken, stored = refs[-3:]
    acts = refs[: -11 - out_count * (2 if moved else 1)]
    tok_count, (width, units) = pieces[0].shape[0], gate_v.shape

    def fetches(part):
        return [
            pltpu.make_async_copy(
                ref.at[:, pl.ds(part * width, width)],
                (x_all, cot_all)[part].at[pl.ds(piece * tok_count, tok_count), :],
                fetched.at[part, piece],
            )
            for piece, ref in enumerate(pieces)
        ]

    takes = []
    if not moved:
        third = len(acts) // 3
        for which in range(3):
            at = 0
            for group, ref in enumerate(acts[which * third : (which + 1) * third]):
                rows = pl.ds(at, ref.shape[0])
                target = hidden.at[rows, :] if which == 0 else d_both.at[rows, pl.ds((which - 1) * units, units)]
                source = ref.at[:, pl.ds(slot * units, units)]
                takes.append(pltpu.make_async_copy(source, target, taken.at[which, group]))
                at += ref.shape[0]
    for copy in takes + [copy for part in range(2) if sides[part] for copy in fetches(part)]:
        copy.start()
    if moved:
        groups = len(acts) // 3
        picks, own = acts[:groups], acts[groups : 2 * groups]
        block = 0
        for ref in acts[2 * groups :]:
            gathered[block : block + ref.shape[0]] = ref[...]
            block += ref.shape[0]
        block = 0
        for ref, mine in zip(picks, own):
            for piece in range(ref.shape[0]):
                packed = jnp.where(facts[0] == 1, gathered[facts[1 + block]], mine[piece])
                spread = dot(ref[piece][:, : mine.shape[1]], packed, 1, 0).astype(BF16)
                rows = slice(block * tok_count, (block + 1) * tok_count)
                hidden[rows] = spread[:, :units]
                d_both[rows] = spread[:, units:]
                block += 1
    for copy in takes + (fetches(0) if sides[0] else []):
        copy.wait()

    def each(body):
        lax.fori_loop(0, width // tile, lambda i, _: body(pl.ds(pl.multiple_of(i * tile, tile), tile)), None)

    def into_columns(features):
        pair = dot(x_all[:, features], d_both[...], 0, 0).astype(BF16)
        gate_v[features, :] = pair[:, :units]
        up_v[features, :] = pair[:, units:]

    def into_rows(features):
        down_v[:, features] = dot(hidden[...], cot_all[:, features], 0, 0).astype(BF16)

    sources = (gate_v, up_v) * sides[0] + (down_v,) * sides[1]
    stores = [
        pltpu.make_async_copy(source, target.at[slot], stored.at[i])
        for i, (source, target) in enumerate(zip(sources, outs))
    ]
    if sides[0]:
        each(into_columns)
        for store in stores[:2]:
            store.start()
    if sides[1]:
        for copy in fetches(1):
            copy.wait()
        each(into_rows)
        stores[-1].start()
    for store in stores:
        store.wait()


def grad_call(pieces, acts, facts, slot, units, per_device, width, sides=(1, 1), before=None):
    moved = before is not None
    tok_count = pieces[0].shape[0]
    total = len(pieces) * tok_count
    anywhere, vmem = pl.BlockSpec(memory_space=pl.ANY), pl.BlockSpec(memory_space=pltpu.VMEM)
    arrays = list(pieces) + list(acts) + list(before or ())
    shapes = [(per_device, width, units)] * (2 * sides[0]) + [(per_device, units, width)] * sides[1]
    row_blocks = (len(pieces),) + acts[-1].shape[1:] if moved else (1, 16, 128)
    return pl.pallas_call(
        functools.partial(grad_kernel, len(pieces), moved, sides, slot, 1024),
        in_specs=[pl.BlockSpec(memory_space=pltpu.SMEM)]
        + [anywhere] * len(pieces)
        + [vmem if moved else anywhere] * len(acts)
        + [anywhere] * len(before or ()),
        out_specs=[anywhere] * len(shapes),
        out_shape=[jax.ShapeDtypeStruct(shape, BF16) for shape in shapes],
        scratch_shapes=[pltpu.VMEM((total, width), BF16)] * 2
        + [pltpu.VMEM((total, units), BF16), pltpu.VMEM((total, 2 * units), BF16)]
        + [pltpu.VMEM((width, units), BF16)] * 2
        + [pltpu.VMEM((units, width), BF16), pltpu.VMEM(row_blocks, BF16)]
        + [
            pltpu.SemaphoreType.DMA((2, len(pieces))),
            pltpu.SemaphoreType.DMA((3, len(acts))),
            pltpu.SemaphoreType.DMA((3,)),
        ],
        input_output_aliases={1 + len(arrays) - len(shapes) + i: i for i in range(len(shapes))} if moved else {},
        compiler_params=pltpu.CompilerParams(vmem_limit_bytes=56 * 1024 * 1024),
        cost_estimate=pl.CostEstimate(
            flops=6 * total * width * units, bytes_accessed=4 * total * width, transcendentals=0
        ),
    )(facts, *arrays)


def gather_body(tokens, expert_ids, combine, cotangent, old_layout, pair_moves, gate_w, up_w, down_w):
    ep_count = lax.axis_size("ep")
    tp_count = lax.axis_size("tp")
    tok_count, top_k = expert_ids.shape
    expert_count = old_layout.shape[0]
    per_device, width, units = gate_w.shape
    share = width // tp_count
    capacity = 3 * tok_count * top_k // (2 * expert_count)
    chips = ep_count // 2
    half = chips // 2
    order = ring_order(chips)
    forward, backward = ring_pairs(order, 1), ring_pairs(order, -1)
    by_core = [(forward if pair[0] % 2 == 0 else backward)[i] for i, pair in enumerate(forward)]
    other_core = [(i, i ^ 1) for i in range(ep_count)]
    other_share = [(i, i ^ 1) for i in range(tp_count)]
    partners = [(i, i ^ (ep_count // 2)) for i in range(ep_count)]
    me = lax.axis_index("ep")
    my_share = lax.axis_index("tp")
    core = me % 2
    spot, from_partner = (jnp.asarray(table)[me] for table in block_tables(order)[1:])

    my_move = pair_moves[me] == 1
    last = per_device - 1
    experts = lax.dynamic_slice_in_dim(old_layout, me * per_device, per_device, 0)
    partner_last = old_layout[(me ^ (ep_count // 2)) * per_device + last]
    new_last = jnp.where(my_move, partner_last, experts[last])
    facts = jnp.concatenate([my_share[None], experts, new_last[None]]).astype(jnp.int32)
    weights = (gate_w, up_w, down_w.reshape(per_device * units, width))

    parts = [expert_ids.astype(F32)]
    rest = combine
    for _ in range(3):
        parts.append(lax.reduce_precision(rest, 8, 7))
        rest = rest - parts[-1]
    notes = jnp.concatenate(parts, axis=1)
    notes = jnp.pad(notes, ((0, 0), (0, -notes.shape[1] % 128))).astype(BF16)
    payload = jnp.concatenate([tokens, cotangent, notes], axis=1)

    def add(*values):
        return sum(value.astype(F32) for value in values).astype(BF16)

    def exchange(near_other, near_mine, far_other, far_mine):
        sent = add(near_other, lax.ppermute(far_other, "ep", other_core))
        return near_mine, lax.ppermute(far_mine, "ep", other_core), lax.ppermute(sent, "tp", other_share)

    move_facts = jnp.concatenate([my_move.astype(jnp.int32)[None], from_partner])
    kept_groups, totals, swapped = [], [], {}
    right = left = payload
    pending = crossing = None
    for step in range(half + 1):
        near = [payload] if step == 0 else [right, left] if step < half else [right]
        far = [lax.ppermute(piece, "ep", other_core) for piece in near]
        pieces = near + far
        if step < half - 1:
            right = lax.ppermute(right, "ep", forward)
            left = lax.ppermute(left, "ep", backward)
        elif step == half - 1:
            right = lax.ppermute(jnp.where(core == 0, right, left), "ep", by_core)
        if step > 1:
            crossing = exchange(*pending)
        result = group_call(pieces, facts, weights, top_k, capacity, share)
        acts, (near_other, far_other, near_mine, far_mine), rest = result[:3], result[3:7], result[7:]
        pending = (near_other, near_mine, far_other, far_mine)
        group = (acts, rest)
        if step == 0:
            early = exchange(*pending)
        elif step == 1:
            crossing = early
        if step == half - 1:
            swapped[1] = lax.ppermute(kept_groups[1][2][1], "ep", partners)
        right, left, pending, crossing, group, move_facts, swapped = lax.optimization_barrier(
            (right, left, pending, crossing, group, move_facts, swapped)
        )
        if crossing:
            totals.append(crossing)
        kept_groups.append((pieces, *group))
    near_other, near_mine, far_other, far_mine = pending
    sent = add(near_other, lax.ppermute(far_other, "ep", other_core))
    stay_facts = jnp.zeros((1,), jnp.int32)
    for number in (0, *range(2, half - 1)):
        swapped[number] = lax.ppermute(kept_groups[number][2][1], "ep", partners)
    sent, stay_facts, swapped = lax.optimization_barrier((sent, stay_facts, swapped))
    last_three = near_mine, lax.ppermute(far_mine, "ep", other_core), lax.ppermute(sent, "tp", other_share)

    for number in (half - 1, half):
        swapped[number] = lax.ppermute(kept_groups[number][2][1], "ep", partners)

    every = [piece for group in kept_groups for piece in group[0]]
    grads = None
    for slot in range(last):
        own_acts = [group[1][i] for i in range(3) for group in kept_groups]
        grads = grad_call(every, own_acts, stay_facts, slot, units, per_device, width)

    d_weights = jnp.concatenate([group[2][0] for group in kept_groups])[:, :top_k]
    d_weights = d_weights + lax.ppermute(d_weights, "tp", other_share)
    totals = [add(*parts) for parts in totals]
    last_three, grads, d_weights, swapped, totals = lax.optimization_barrier(
        (last_three, grads, d_weights, swapped, totals)
    )

    farthest = add(*last_three)
    met = [lax.ppermute(farthest[kind], "ep", by_core) for kind in range(2)]
    met, move_facts = lax.optimization_barrier((met, move_facts))
    by_hop = {0: totals[0]}
    for step in range(1, half):
        by_hop[-step], by_hop[step] = totals[step][:, :tok_count], totals[step][:, tok_count:]
    moved_acts = [group[2][2] for group in kept_groups] + [group[2][1] for group in kept_groups]
    moved_acts += [swapped[number] for number in range(half + 1)]

    def moved_grads(sides, before):
        return grad_call(every, moved_acts, move_facts, last, units, per_device, width, sides, before)

    (grad_down,) = moved_grads((0, 1), grads[2:])
    none = jnp.zeros_like(met[0])
    sums = [(jnp.where(core == 0, value, none), jnp.where(core == 0, none, value)) for value in met]
    for step in range(half - 1, 0, -1):
        sums = [
            (
                lax.ppermute(add(by_hop[step][kind], sums[kind][0]), "ep", forward),
                lax.ppermute(add(by_hop[-step][kind], sums[kind][1]), "ep", backward),
            )
            for kind in range(2)
        ]
        if step == half - 1:
            sums, grad_down, d_weights = lax.optimization_barrier((sums, grad_down, d_weights))
            d_weights = jnp.take(d_weights.reshape(ep_count, tok_count, top_k), spot, axis=0)
            d_weights = lax.all_to_all(d_weights.transpose(0, 2, 1), "ep", split_axis=0, concat_axis=0, tiled=True)
            d_combine = jnp.sum(d_weights, axis=0).T
        elif step == 2:
            sums, move_facts, d_combine = lax.optimization_barrier((sums, move_facts, d_combine))
    grad_gate, grad_up = moved_grads((1, 0), grads[:2])
    mixed, d_tokens = (add(by_hop[0][kind], *sums[kind]) for kind in range(2))

    return (mixed, d_tokens, d_combine, grad_gate, grad_up, grad_down)


def exchange_halves(value, axis, distance):
    mask = 2**distance
    pairs = [(source, source ^ mask) for source in range(lax.axis_size(axis))]
    return lax.ppermute(value, axis, pairs)


def dispatch_body(tokens, expert_ids, combine, cotangent, old_layout, pair_moves, gate_w, up_w, down_w):
    ep_count = lax.axis_size("ep")
    tp_count = lax.axis_size("tp")
    tok_count, top_k = expert_ids.shape
    expert_count = old_layout.shape[0]
    per_device = gate_w.shape[0]
    model_width = tokens.shape[1]
    share_width = model_width // tp_count
    capacity = 3 * tok_count * top_k // (2 * expert_count)
    pair_count = ep_count // 2
    swap_bit = ep_count.bit_length() - 2
    my_index = lax.axis_index("ep")
    my_share = lax.axis_index("tp")
    my_move = pair_moves[my_index] == 1
    slot_ids = jnp.arange(expert_count, dtype=jnp.int32)
    slot_device = slot_ids // per_device
    slot_local = slot_ids % per_device
    moved = (slot_local == per_device - 1) & (pair_moves[slot_device] == 1)
    source_slot = jnp.where(
        moved, (slot_device + pair_count) % ep_count * per_device + slot_local, slot_ids
    )
    new_layout = jnp.sum(
        jnp.where(source_slot[:, None] == slot_ids[None, :], old_layout[None, :], 0), axis=1
    )
    w_gate, w_up, w_down = (gate_w, up_w, down_w)
    arrived = exchange_halves(
        (gate_w[per_device - 1], up_w[per_device - 1], down_w[per_device - 1]), "ep", swap_bit
    )
    w_gate = jnp.concatenate(
        [gate_w[:-1], jnp.where(my_move, arrived[0], gate_w[-1])[None]], axis=0
    )
    w_up = jnp.concatenate([up_w[:-1], jnp.where(my_move, arrived[1], up_w[-1])[None]], axis=0)
    w_down = jnp.concatenate(
        [down_w[:-1], jnp.where(my_move, arrived[2], down_w[-1])[None]], axis=0
    )
    slot_of = jnp.sum(
        jnp.where(new_layout[None, :] == slot_ids[:, None], slot_ids[None, :], 0), axis=1
    )
    flat_ids = expert_ids.reshape(-1)
    onehot = (flat_ids[:, None] == slot_ids[None, :]).astype(jnp.int32)
    before = jnp.cumsum(onehot, axis=0) - onehot
    position = jnp.sum(before * onehot, axis=1)
    target_slot = jnp.sum(onehot * slot_of[None, :], axis=1)
    target_device = target_slot // per_device
    target_local = target_slot % per_device
    row_index = target_local * (ep_count * capacity) + target_device * capacity + position
    rows_total = expert_count * capacity
    matches = jnp.arange(rows_total, dtype=jnp.int32)[:, None] == row_index[None, :]
    select = jnp.sum(
        matches.reshape(rows_total, tok_count, top_k).astype(jnp.int32), axis=2
    ).astype(jnp.bfloat16)
    row_weight = jnp.sum(jnp.where(matches, combine.reshape(-1)[None, :], 0.0), axis=1)

    def dispatch(source, scaling):
        portion = lax.dynamic_slice_in_dim(source, my_share * share_width, share_width, 1)
        picked = jnp.dot(select, portion, preferred_element_type=jnp.float32)
        if scaling is not None:
            picked = picked * scaling[:, None]
        buffer = picked.astype(jnp.bfloat16).reshape(per_device, ep_count * capacity, share_width)
        landed = lax.all_to_all(buffer, "ep", split_axis=1, concat_axis=1, tiled=True)
        return lax.all_gather(landed, "tp", axis=2, tiled=True)

    def send_back(partial_value):
        shares = lax.psum_scatter(partial_value, "tp", scatter_dimension=2, tiled=True).astype(
            jnp.bfloat16
        )
        returned = lax.all_to_all(shares, "ep", split_axis=1, concat_axis=1, tiled=True)
        return returned.reshape(rows_total, share_width)[row_index].reshape(
            tok_count, top_k, share_width
        )

    rows_in = dispatch(tokens, None)
    gate = jnp.einsum("erd,edf->erf", rows_in, w_gate, preferred_element_type=jnp.float32)
    upper = jnp.einsum("erd,edf->erf", rows_in, w_up, preferred_element_type=jnp.float32)
    sigma = jax.nn.sigmoid(gate)
    active = gate * sigma
    hidden = (active * upper).astype(jnp.bfloat16)
    out_part = jnp.einsum("erf,efd->erd", hidden, w_down, preferred_element_type=jnp.float32)
    out_rows = send_back(out_part).astype(jnp.float32)
    mixed = jnp.einsum("tk,tkd->td", combine, out_rows).astype(jnp.bfloat16)
    cot_share = lax.dynamic_slice_in_dim(cotangent, my_share * share_width, share_width, 1).astype(
        jnp.float32
    )
    combine_part = jnp.einsum("td,tkd->tk", cot_share, out_rows)
    d_combine = lax.psum(combine_part, "tp")
    rows_grad = dispatch(cotangent, row_weight)
    d_hidden = jnp.einsum("erd,efd->erf", rows_grad, w_down, preferred_element_type=jnp.float32)
    d_gate = (d_hidden * upper * sigma * (1.0 + gate * (1.0 - sigma))).astype(jnp.bfloat16)
    d_up = (d_hidden * active).astype(jnp.bfloat16)
    back_part = jnp.einsum(
        "erf,edf->erd", d_gate, w_gate, preferred_element_type=jnp.float32
    ) + jnp.einsum("erf,edf->erd", d_up, w_up, preferred_element_type=jnp.float32)
    back_rows = send_back(back_part)
    d_tokens = jnp.sum(back_rows.astype(jnp.float32), axis=1).astype(jnp.bfloat16)
    grad_gate = jnp.einsum(
        "erd,erf->edf", rows_in, d_gate, preferred_element_type=jnp.float32
    ).astype(jnp.bfloat16)
    grad_up = jnp.einsum("erd,erf->edf", rows_in, d_up, preferred_element_type=jnp.float32).astype(
        jnp.bfloat16
    )
    grad_down = jnp.einsum(
        "erf,erd->efd", hidden, rows_grad, preferred_element_type=jnp.float32
    ).astype(jnp.bfloat16)
    return (mixed, d_tokens, d_combine, grad_gate, grad_up, grad_down)


def body(*operands):
    expert_ids, old_layout = operands[1], operands[4]
    tok_count, top_k = expert_ids.shape
    ep_count = lax.axis_size("ep")
    rows = 3 * tok_count * top_k * ep_count // (2 * old_layout.shape[0]) * operands[6].shape[0]
    gather = ep_count * tok_count <= 2 * rows and old_layout.shape[0] <= 256
    return (gather_body if gather else dispatch_body)(*operands)


def solution(mesh):
    return jax.shard_map(
        body,
        mesh=mesh,
        in_specs=(
            P("ep", None),
            P("ep", None),
            P("ep", None),
            P("ep", None),
            P(),
            P(),
            P("ep", None, "tp"),
            P("ep", None, "tp"),
            P("ep", "tp", None),
        ),
        out_specs=(
            P("ep", "tp"),
            P("ep", "tp"),
            P("ep", None),
            P("ep", None, "tp"),
            P("ep", None, "tp"),
            P("ep", "tp", None),
        ),
        check_vma=False,
    )
```

```python
import functools

import jax
import jax.numpy as jnp
import numpy as np
from jax import lax
from jax.experimental import pallas as pl
from jax.experimental.pallas import tpu as pltpu
from jax.sharding import PartitionSpec as P

F32 = jnp.float32
BF16 = jnp.bfloat16


def ring_order(chips):
    return list(range(0, chips, 2)) + list(range(chips - 1, 0, -2))


def ring_pairs(order, hop):
    chips = len(order)
    return [
        (chip * 2 + core, order[(place + hop) % chips] * 2 + core)
        for place, chip in enumerate(order)
        for core in range(2)
    ]


def block_tables(order):
    chips = len(order)
    half = chips // 2
    groups = [[0]] + [[-step, step] for step in range(1, half)] + [[half]]
    ep_count = 2 * chips
    arrival = np.zeros((ep_count, ep_count), np.int32)
    for place, chip in enumerate(order):
        for core in range(2):
            arrival[chip * 2 + core] = [
                order[(place + hop) % chips] * 2 + (core ^ side)
                for hops in groups
                for side in range(2)
                for hop in hops
            ]
    spot = np.argsort(arrival, axis=1).astype(np.int32)
    partner = np.arange(ep_count) ^ (ep_count // 2)
    from_partner = np.take_along_axis(spot[partner], arrival, axis=1).astype(np.int32)
    return arrival, spot, from_partner


def dot(a, b, ca, cb):
    return lax.dot_general(a, b, (((ca,), (cb,)), ((), ())), preferred_element_type=F32)


def group_kernel(pieces, top_k, capacity, tile, tile_out, facts, *refs):
    blocks, (gate_w, up_w, down_w) = refs[:pieces], refs[pieces : pieces + 3]
    act_outs, sum_outs, (d_weights, packed, picks) = refs[pieces + 3 : pieces + 6], refs[pieces + 6 : pieces + 10], refs[pieces + 10 : pieces + 13]
    x_all, cot_all, notes_all, gate_v, up_v, down_v, hidden_v, d_gate_v, d_up_v = refs[pieces + 13 : pieces + 22]
    sums, (fetched, loaded, stored) = refs[pieces + 22 : pieces + 26], refs[pieces + 26 :]
    per_device, width, units = gate_w.shape
    both = per_device * units
    tok_count, lanes = blocks[0].shape[0], notes_all.shape[1]
    share = sums[0].shape[2]

    def fetches(part):
        target = (x_all, cot_all, notes_all)[part]
        return [
            pltpu.make_async_copy(
                ref.at[:, pl.ds(part * width, target.shape[1])],
                target.at[pl.ds(piece * tok_count, tok_count), :],
                fetched.at[part, piece],
            )
            for piece, ref in enumerate(blocks)
        ]

    def load(which, slot):
        if which == 2:
            rows = pl.ds(slot * units, units)
            return pltpu.make_async_copy(down_w.at[rows, :], down_v.at[rows, :], loaded.at[which, slot])
        source, target = ((gate_w, gate_v), (up_w, up_v))[which]
        return pltpu.make_async_copy(
            source.at[slot], target.at[:, pl.ds(slot * units, units)], loaded.at[which, slot]
        )

    for fetch in fetches(2) + fetches(0):
        fetch.start()
    load(0, 0).start()
    load(1, 0).start()
    for fetch in fetches(1):
        fetch.start()
    load(2, 0).start()
    for slot in range(1, per_device):
        for which in range(3):
            load(which, slot).start()
    for fetch in fetches(2):
        fetch.wait()
    said = notes_all[...].astype(F32)
    lane = lax.broadcasted_iota(jnp.int32, said.shape, 1)
    ids = jnp.where(lane < top_k, said, -1.0).astype(jnp.int32)
    weight = pltpu.roll(said, lanes - top_k, 1) + (
        pltpu.roll(said, lanes - 2 * top_k, 1) + pltpu.roll(said, lanes - 3 * top_k, 1)
    )
    gains = [
        jnp.sum(jnp.where(ids == facts[1 + slot], weight, 0.0), axis=1, keepdims=True) for slot in range(per_device)
    ]
    traded_sums = [0.0] * per_device
    for fetch in fetches(0):
        fetch.wait()
    slots_in = 0
    for at in range(0, both, tile):
        columns = slice(at, at + tile)
        fresh = range(slots_in, (at + tile - 1) // units + 1)
        slots_in = (at + tile - 1) // units + 1
        for slot in fresh:
            load(0, slot).wait()
            load(1, slot).wait()
        gate = dot(x_all[...], gate_v[:, columns], 1, 0)
        upper = dot(x_all[...], up_v[:, columns], 1, 0)
        if at == 0:
            for fetch in fetches(1):
                fetch.wait()
        for slot in fresh:
            load(2, slot).wait()
        pulled = dot(cot_all[...], down_v[columns, :], 1, 1)
        sigma = jax.nn.sigmoid(gate)
        active = gate * sigma
        hidden = active * upper
        traded = hidden * pulled
        parts = [(part // units, part - at) for part in range(at, at + tile, lanes)]
        for slot, part in parts:
            traded_sums[slot] += jnp.sum(traded[:, part : part + lanes], axis=1, keepdims=True)
        gain = jnp.concatenate([jnp.broadcast_to(gains[slot], said.shape) for slot, _ in parts], axis=1)
        d_hidden = pulled * gain
        hidden_v[:, columns] = (hidden * gain).astype(BF16)
        d_gate_v[:, columns] = (d_hidden * upper * sigma * (1.0 + gate * (1.0 - sigma))).astype(BF16)
        d_up_v[:, columns] = (d_hidden * active).astype(BF16)

    stores = [
        pltpu.make_async_copy(source, target, stored.at[i])
        for i, (source, target) in enumerate(zip((hidden_v, d_gate_v, d_up_v, *sums), (*act_outs, *sum_outs)))
    ]
    for store in stores[:3]:
        store.start()
    d_weights[...] = sum(
        jnp.where(ids == facts[1 + slot], traded_sums[slot], 0.0) for slot in range(per_device)
    )

    near = pieces // 2 * tok_count
    for which in range(2):
        first = jnp.where(which == 0, 1 - facts[0], facts[0]) * share
        for at in range(0, share, tile_out):
            features = pl.ds(pl.multiple_of(first + at, tile_out), tile_out)
            out = dot(hidden_v[...], down_v[:, features], 1, 0).astype(BF16)
            back = dot(d_gate_v[...], gate_v[features, :], 1, 1) + dot(d_up_v[...], up_v[features, :], 1, 1)
            back = back.astype(BF16)
            columns = slice(at, at + tile_out)
            for kind, value in enumerate((out, back)):
                sums[2 * which][kind, :, columns] = value[:near]
                sums[2 * which + 1][kind, :, columns] = value[near:]
        for store in stores[3 + 2 * which : 5 + 2 * which]:
            store.start()

    row = lax.broadcasted_iota(jnp.int32, (tok_count, tok_count), 0)
    column = lax.broadcasted_iota(jnp.int32, (tok_count, tok_count), 1)
    earlier = jnp.where(column < row, 1.0, 0.0).astype(BF16)
    tail = slice((per_device - 1) * units, per_device * units)

    def pick_of(rows, expert):
        named = jnp.max(jnp.where(ids[rows] == expert, 1.0, 0.0), axis=1, keepdims=True)
        mask = jnp.broadcast_to(named, (tok_count, tok_count))
        position = dot(earlier, mask.astype(BF16), 1, 0).astype(jnp.int32)
        return jnp.where((position == column) & (mask > 0.0), 1.0, 0.0).astype(BF16)

    for piece in range(pieces):
        rows = slice(piece * tok_count, (piece + 1) * tok_count)
        pick = pick_of(rows, facts[per_device])
        for at, ref in enumerate((hidden_v, d_gate_v, d_up_v)):
            packed[piece, :, at * units : (at + 1) * units] = dot(pick, ref[rows, tail], 0, 0).astype(BF16)[:capacity]
        picks[piece] = pick_of(rows, facts[1 + per_device])
    for store in stores:
        store.wait()


def group_call(blocks, facts, weights, top_k, capacity, share):
    pieces = len(blocks)
    per_device, width, units = weights[0].shape
    both = per_device * units
    tok_count = blocks[0].shape[0]
    rows = pieces * tok_count
    lanes = 128
    anywhere, vmem = pl.BlockSpec(memory_space=pl.ANY), pl.BlockSpec(memory_space=pltpu.VMEM)
    act, total = (rows, both), (2, rows // 2, share)
    return pl.pallas_call(
        functools.partial(group_kernel, pieces, top_k, capacity, 256, 512),
        in_specs=[pl.BlockSpec(memory_space=pltpu.SMEM)] + [anywhere] * (pieces + 3),
        out_specs=[anywhere] * 7 + [vmem] * 3,
        out_shape=[jax.ShapeDtypeStruct(act, BF16)] * 3
        + [jax.ShapeDtypeStruct(total, BF16)] * 4
        + [
            jax.ShapeDtypeStruct((rows, lanes), F32),
            jax.ShapeDtypeStruct((pieces, capacity, 3 * units), BF16),
            jax.ShapeDtypeStruct((pieces, tok_count, tok_count), BF16),
        ],
        scratch_shapes=[pltpu.VMEM((rows, width), BF16)] * 2
        + [pltpu.VMEM((rows, lanes), BF16)]
        + [pltpu.VMEM((width, both), BF16)] * 2
        + [pltpu.VMEM((both, width), BF16)]
        + [pltpu.VMEM(act, BF16)] * 3
        + [pltpu.VMEM(total, BF16)] * 4
        + [
            pltpu.SemaphoreType.DMA((3, pieces)),
            pltpu.SemaphoreType.DMA((3, per_device)),
            pltpu.SemaphoreType.DMA((7,)),
        ],
        compiler_params=pltpu.CompilerParams(vmem_limit_bytes=56 * 1024 * 1024),
        cost_estimate=pl.CostEstimate(
            flops=12 * rows * width * both,
            bytes_accessed=6 * width * both + 12 * rows * width,
            transcendentals=rows * both,
        ),
    )(facts, *blocks, *weights)


def grad_kernel(blocks, moved, sides, slot, tile, facts, *refs):
    pieces, refs = refs[:blocks], refs[blocks:]
    out_count = 2 * sides[0] + sides[1]
    outs, (x_all, cot_all, hidden, d_both, gate_v, up_v, down_v, gathered) = refs[-11 - out_count : -11], refs[-11:-3]
    fetched, taken, stored = refs[-3:]
    acts = refs[: -11 - out_count * (2 if moved else 1)]
    tok_count, (width, units) = pieces[0].shape[0], gate_v.shape

    def fetches(part):
        return [
            pltpu.make_async_copy(
                ref.at[:, pl.ds(part * width, width)],
                (x_all, cot_all)[part].at[pl.ds(piece * tok_count, tok_count), :],
                fetched.at[part, piece],
            )
            for piece, ref in enumerate(pieces)
        ]

    takes = []
    if not moved:
        third = len(acts) // 3
        for which in range(3):
            at = 0
            for group, ref in enumerate(acts[which * third : (which + 1) * third]):
                rows = pl.ds(at, ref.shape[0])
                target = hidden.at[rows, :] if which == 0 else d_both.at[rows, pl.ds((which - 1) * units, units)]
                source = ref.at[:, pl.ds(slot * units, units)]
                takes.append(pltpu.make_async_copy(source, target, taken.at[which, group]))
                at += ref.shape[0]
    for copy in takes + [copy for part in range(2) if sides[part] for copy in fetches(part)]:
        copy.start()
    if moved:
        groups = len(acts) // 3
        picks, own = acts[:groups], acts[groups : 2 * groups]
        block = 0
        for ref in acts[2 * groups :]:
            gathered[block : block + ref.shape[0]] = ref[...]
            block += ref.shape[0]
        block = 0
        for ref, mine in zip(picks, own):
            for piece in range(ref.shape[0]):
                packed = jnp.where(facts[0] == 1, gathered[facts[1 + block]], mine[piece])
                spread = dot(ref[piece][:, : mine.shape[1]], packed, 1, 0).astype(BF16)
                rows = slice(block * tok_count, (block + 1) * tok_count)
                hidden[rows] = spread[:, :units]
                d_both[rows] = spread[:, units:]
                block += 1
    for copy in takes + (fetches(0) if sides[0] else []):
        copy.wait()

    def each(body):
        lax.fori_loop(0, width // tile, lambda i, _: body(pl.ds(pl.multiple_of(i * tile, tile), tile)), None)

    def into_columns(features):
        pair = dot(x_all[:, features], d_both[...], 0, 0).astype(BF16)
        gate_v[features, :] = pair[:, :units]
        up_v[features, :] = pair[:, units:]

    def into_rows(features):
        down_v[:, features] = dot(hidden[...], cot_all[:, features], 0, 0).astype(BF16)

    sources = (gate_v, up_v) * sides[0] + (down_v,) * sides[1]
    stores = [
        pltpu.make_async_copy(source, target.at[slot], stored.at[i])
        for i, (source, target) in enumerate(zip(sources, outs))
    ]
    if sides[0]:
        each(into_columns)
        for store in stores[:2]:
            store.start()
    if sides[1]:
        for copy in fetches(1):
            copy.wait()
        each(into_rows)
        stores[-1].start()
    for store in stores:
        store.wait()


def grad_call(pieces, acts, facts, slot, units, per_device, width, sides=(1, 1), before=None):
    moved = before is not None
    tok_count = pieces[0].shape[0]
    total = len(pieces) * tok_count
    anywhere, vmem = pl.BlockSpec(memory_space=pl.ANY), pl.BlockSpec(memory_space=pltpu.VMEM)
    arrays = list(pieces) + list(acts) + list(before or ())
    shapes = [(per_device, width, units)] * (2 * sides[0]) + [(per_device, units, width)] * sides[1]
    row_blocks = (len(pieces),) + acts[-1].shape[1:] if moved else (1, 16, 128)
    return pl.pallas_call(
        functools.partial(grad_kernel, len(pieces), moved, sides, slot, 1024),
        in_specs=[pl.BlockSpec(memory_space=pltpu.SMEM)]
        + [anywhere] * len(pieces)
        + [vmem if moved else anywhere] * len(acts)
        + [anywhere] * len(before or ()),
        out_specs=[anywhere] * len(shapes),
        out_shape=[jax.ShapeDtypeStruct(shape, BF16) for shape in shapes],
        scratch_shapes=[pltpu.VMEM((total, width), BF16)] * 2
        + [pltpu.VMEM((total, units), BF16), pltpu.VMEM((total, 2 * units), BF16)]
        + [pltpu.VMEM((width, units), BF16)] * 2
        + [pltpu.VMEM((units, width), BF16), pltpu.VMEM(row_blocks, BF16)]
        + [
            pltpu.SemaphoreType.DMA((2, len(pieces))),
            pltpu.SemaphoreType.DMA((3, len(acts))),
            pltpu.SemaphoreType.DMA((3,)),
        ],
        input_output_aliases={1 + len(arrays) - len(shapes) + i: i for i in range(len(shapes))} if moved else {},
        compiler_params=pltpu.CompilerParams(vmem_limit_bytes=56 * 1024 * 1024),
        cost_estimate=pl.CostEstimate(
            flops=6 * total * width * units, bytes_accessed=4 * total * width, transcendentals=0
        ),
    )(facts, *arrays)


def gather_body(tokens, expert_ids, combine, cotangent, old_layout, pair_moves, gate_w, up_w, down_w):
    ep_count = lax.axis_size("ep")
    tp_count = lax.axis_size("tp")
    tok_count, top_k = expert_ids.shape
    expert_count = old_layout.shape[0]
    per_device, width, units = gate_w.shape
    share = width // tp_count
    capacity = 3 * tok_count * top_k // (2 * expert_count)
    chips = ep_count // 2
    half = chips // 2
    order = ring_order(chips)
    forward, backward = ring_pairs(order, 1), ring_pairs(order, -1)
    by_core = [(forward if pair[0] % 2 == 0 else backward)[i] for i, pair in enumerate(forward)]
    other_core = [(i, i ^ 1) for i in range(ep_count)]
    other_share = [(i, i ^ 1) for i in range(tp_count)]
    partners = [(i, i ^ (ep_count // 2)) for i in range(ep_count)]
    me = lax.axis_index("ep")
    my_share = lax.axis_index("tp")
    core = me % 2
    spot, from_partner = (jnp.asarray(table)[me] for table in block_tables(order)[1:])

    my_move = pair_moves[me] == 1
    last = per_device - 1
    experts = lax.dynamic_slice_in_dim(old_layout, me * per_device, per_device, 0)
    partner_last = old_layout[(me ^ (ep_count // 2)) * per_device + last]
    new_last = jnp.where(my_move, partner_last, experts[last])
    facts = jnp.concatenate([my_share[None], experts, new_last[None]]).astype(jnp.int32)
    weights = (gate_w, up_w, down_w.reshape(per_device * units, width))

    parts = [expert_ids.astype(F32)]
    rest = combine
    for _ in range(3):
        parts.append(lax.reduce_precision(rest, 8, 7))
        rest = rest - parts[-1]
    notes = jnp.concatenate(parts, axis=1)
    notes = jnp.pad(notes, ((0, 0), (0, -notes.shape[1] % 128))).astype(BF16)
    payload = jnp.concatenate([tokens, cotangent, notes], axis=1)

    def add(*values):
        return sum(value.astype(F32) for value in values).astype(BF16)

    def exchange(near_other, near_mine, far_other, far_mine):
        sent = add(near_other, lax.ppermute(far_other, "ep", other_core))
        return near_mine, lax.ppermute(far_mine, "ep", other_core), lax.ppermute(sent, "tp", other_share)

    move_facts = jnp.concatenate([my_move.astype(jnp.int32)[None], from_partner])
    kept_groups, totals, swapped = [], [], {}
    right = left = payload
    pending = crossing = None
    for step in range(half + 1):
        near = [payload] if step == 0 else [right, left] if step < half else [right]
        far = [lax.ppermute(piece, "ep", other_core) for piece in near]
        pieces = near + far
        if step < half - 1:
            right = lax.ppermute(right, "ep", forward)
            left = lax.ppermute(left, "ep", backward)
        elif step == half - 1:
            right = lax.ppermute(jnp.where(core == 0, right, left), "ep", by_core)
        if step > 1:
            crossing = exchange(*pending)
        result = group_call(pieces, facts, weights, top_k, capacity, share)
        acts, (near_other, far_other, near_mine, far_mine), rest = result[:3], result[3:7], result[7:]
        pending = (near_other, near_mine, far_other, far_mine)
        group = (acts, rest)
        if step == 0:
            early = exchange(*pending)
        elif step == 1:
            crossing = early
        if step == half - 1:
            swapped[1] = lax.ppermute(kept_groups[1][2][1], "ep", partners)
        right, left, pending, crossing, group, move_facts, swapped = lax.optimization_barrier(
            (right, left, pending, crossing, group, move_facts, swapped)
        )
        if crossing:
            totals.append(crossing)
        kept_groups.append((pieces, *group))
    near_other, near_mine, far_other, far_mine = pending
    sent = add(near_other, lax.ppermute(far_other, "ep", other_core))
    stay_facts = jnp.zeros((1,), jnp.int32)
    for number in (0, *range(2, half - 1)):
        swapped[number] = lax.ppermute(kept_groups[number][2][1], "ep", partners)
    sent, stay_facts, swapped = lax.optimization_barrier((sent, stay_facts, swapped))
    last_three = near_mine, lax.ppermute(far_mine, "ep", other_core), lax.ppermute(sent, "tp", other_share)

    for number in (half - 1, half):
        swapped[number] = lax.ppermute(kept_groups[number][2][1], "ep", partners)

    every = [piece for group in kept_groups for piece in group[0]]
    grads = None
    for slot in range(last):
        own_acts = [group[1][i] for i in range(3) for group in kept_groups]
        grads = grad_call(every, own_acts, stay_facts, slot, units, per_device, width)

    d_weights = jnp.concatenate([group[2][0] for group in kept_groups])[:, :top_k]
    d_weights = d_weights + lax.ppermute(d_weights, "tp", other_share)
    totals = [add(*parts) for parts in totals]
    last_three, grads, d_weights, swapped, totals = lax.optimization_barrier(
        (last_three, grads, d_weights, swapped, totals)
    )

    farthest = add(*last_three)
    met = lax.ppermute(farthest, "ep", by_core)
    met, move_facts = lax.optimization_barrier((met, move_facts))
    by_hop = {0: totals[0]}
    for step in range(1, half):
        by_hop[-step], by_hop[step] = totals[step][:, :tok_count], totals[step][:, tok_count:]
    moved_acts = [group[2][2] for group in kept_groups] + [group[2][1] for group in kept_groups]
    moved_acts += [swapped[number] for number in range(half + 1)]

    def moved_grads(sides, before):
        return grad_call(every, moved_acts, move_facts, last, units, per_device, width, sides, before)

    (grad_down,) = moved_grads((0, 1), grads[2:])
    none = jnp.zeros_like(met)
    sums = (jnp.where(core == 0, met, none), jnp.where(core == 0, none, met))
    for step in range(half - 1, 0, -1):
        sums = (
            lax.ppermute(add(by_hop[step], sums[0]), "ep", forward),
            lax.ppermute(add(by_hop[-step], sums[1]), "ep", backward),
        )
        if step == half - 1:
            sums, grad_down, d_weights = lax.optimization_barrier((sums, grad_down, d_weights))
            d_weights = jnp.take(d_weights.reshape(ep_count, tok_count, top_k), spot, axis=0)
            d_weights = lax.all_to_all(d_weights.transpose(0, 2, 1), "ep", split_axis=0, concat_axis=0, tiled=True)
            d_combine = jnp.sum(d_weights, axis=0).T
        elif step == 2:
            sums, move_facts, d_combine = lax.optimization_barrier((sums, move_facts, d_combine))
    grad_gate, grad_up = moved_grads((1, 0), grads[:2])
    mixed, d_tokens = (add(by_hop[0][kind], sums[0][kind], sums[1][kind]) for kind in range(2))

    return (mixed, d_tokens, d_combine, grad_gate, grad_up, grad_down)


def exchange_halves(value, axis, distance):
    mask = 2**distance
    pairs = [(source, source ^ mask) for source in range(lax.axis_size(axis))]
    return lax.ppermute(value, axis, pairs)


def dispatch_body(tokens, expert_ids, combine, cotangent, old_layout, pair_moves, gate_w, up_w, down_w):
    ep_count = lax.axis_size("ep")
    tp_count = lax.axis_size("tp")
    tok_count, top_k = expert_ids.shape
    expert_count = old_layout.shape[0]
    per_device = gate_w.shape[0]
    model_width = tokens.shape[1]
    share_width = model_width // tp_count
    capacity = 3 * tok_count * top_k // (2 * expert_count)
    pair_count = ep_count // 2
    swap_bit = ep_count.bit_length() - 2
    my_index = lax.axis_index("ep")
    my_share = lax.axis_index("tp")
    my_move = pair_moves[my_index] == 1
    slot_ids = jnp.arange(expert_count, dtype=jnp.int32)
    slot_device = slot_ids // per_device
    slot_local = slot_ids % per_device
    moved = (slot_local == per_device - 1) & (pair_moves[slot_device] == 1)
    source_slot = jnp.where(
        moved, (slot_device + pair_count) % ep_count * per_device + slot_local, slot_ids
    )
    new_layout = jnp.sum(
        jnp.where(source_slot[:, None] == slot_ids[None, :], old_layout[None, :], 0), axis=1
    )
    w_gate, w_up, w_down = (gate_w, up_w, down_w)
    arrived = exchange_halves(
        (gate_w[per_device - 1], up_w[per_device - 1], down_w[per_device - 1]), "ep", swap_bit
    )
    w_gate = jnp.concatenate(
        [gate_w[:-1], jnp.where(my_move, arrived[0], gate_w[-1])[None]], axis=0
    )
    w_up = jnp.concatenate([up_w[:-1], jnp.where(my_move, arrived[1], up_w[-1])[None]], axis=0)
    w_down = jnp.concatenate(
        [down_w[:-1], jnp.where(my_move, arrived[2], down_w[-1])[None]], axis=0
    )
    slot_of = jnp.sum(
        jnp.where(new_layout[None, :] == slot_ids[:, None], slot_ids[None, :], 0), axis=1
    )
    flat_ids = expert_ids.reshape(-1)
    onehot = (flat_ids[:, None] == slot_ids[None, :]).astype(jnp.int32)
    before = jnp.cumsum(onehot, axis=0) - onehot
    position = jnp.sum(before * onehot, axis=1)
    target_slot = jnp.sum(onehot * slot_of[None, :], axis=1)
    target_device = target_slot // per_device
    target_local = target_slot % per_device
    row_index = target_local * (ep_count * capacity) + target_device * capacity + position
    rows_total = expert_count * capacity
    matches = jnp.arange(rows_total, dtype=jnp.int32)[:, None] == row_index[None, :]
    select = jnp.sum(
        matches.reshape(rows_total, tok_count, top_k).astype(jnp.int32), axis=2
    ).astype(jnp.bfloat16)
    row_weight = jnp.sum(jnp.where(matches, combine.reshape(-1)[None, :], 0.0), axis=1)

    def dispatch(source, scaling):
        portion = lax.dynamic_slice_in_dim(source, my_share * share_width, share_width, 1)
        picked = jnp.dot(select, portion, preferred_element_type=jnp.float32)
        if scaling is not None:
            picked = picked * scaling[:, None]
        buffer = picked.astype(jnp.bfloat16).reshape(per_device, ep_count * capacity, share_width)
        landed = lax.all_to_all(buffer, "ep", split_axis=1, concat_axis=1, tiled=True)
        return lax.all_gather(landed, "tp", axis=2, tiled=True)

    def send_back(partial_value):
        shares = lax.psum_scatter(partial_value, "tp", scatter_dimension=2, tiled=True).astype(
            jnp.bfloat16
        )
        returned = lax.all_to_all(shares, "ep", split_axis=1, concat_axis=1, tiled=True)
        return returned.reshape(rows_total, share_width)[row_index].reshape(
            tok_count, top_k, share_width
        )

    rows_in = dispatch(tokens, None)
    gate = jnp.einsum("erd,edf->erf", rows_in, w_gate, preferred_element_type=jnp.float32)
    upper = jnp.einsum("erd,edf->erf", rows_in, w_up, preferred_element_type=jnp.float32)
    sigma = jax.nn.sigmoid(gate)
    active = gate * sigma
    hidden = (active * upper).astype(jnp.bfloat16)
    out_part = jnp.einsum("erf,efd->erd", hidden, w_down, preferred_element_type=jnp.float32)
    out_rows = send_back(out_part).astype(jnp.float32)
    mixed = jnp.einsum("tk,tkd->td", combine, out_rows).astype(jnp.bfloat16)
    cot_share = lax.dynamic_slice_in_dim(cotangent, my_share * share_width, share_width, 1).astype(
        jnp.float32
    )
    combine_part = jnp.einsum("td,tkd->tk", cot_share, out_rows)
    d_combine = lax.psum(combine_part, "tp")
    rows_grad = dispatch(cotangent, row_weight)
    d_hidden = jnp.einsum("erd,efd->erf", rows_grad, w_down, preferred_element_type=jnp.float32)
    d_gate = (d_hidden * upper * sigma * (1.0 + gate * (1.0 - sigma))).astype(jnp.bfloat16)
    d_up = (d_hidden * active).astype(jnp.bfloat16)
    back_part = jnp.einsum(
        "erf,edf->erd", d_gate, w_gate, preferred_element_type=jnp.float32
    ) + jnp.einsum("erf,edf->erd", d_up, w_up, preferred_element_type=jnp.float32)
    back_rows = send_back(back_part)
    d_tokens = jnp.sum(back_rows.astype(jnp.float32), axis=1).astype(jnp.bfloat16)
    grad_gate = jnp.einsum(
        "erd,erf->edf", rows_in, d_gate, preferred_element_type=jnp.float32
    ).astype(jnp.bfloat16)
    grad_up = jnp.einsum("erd,erf->edf", rows_in, d_up, preferred_element_type=jnp.float32).astype(
        jnp.bfloat16
    )
    grad_down = jnp.einsum(
        "erf,erd->efd", hidden, rows_grad, preferred_element_type=jnp.float32
    ).astype(jnp.bfloat16)
    return (mixed, d_tokens, d_combine, grad_gate, grad_up, grad_down)


def body(*operands):
    expert_ids, old_layout = operands[1], operands[4]
    tok_count, top_k = expert_ids.shape
    ep_count = lax.axis_size("ep")
    rows = 3 * tok_count * top_k * ep_count // (2 * old_layout.shape[0]) * operands[6].shape[0]
    gather = ep_count * tok_count <= 2 * rows and old_layout.shape[0] <= 256
    return (gather_body if gather else dispatch_body)(*operands)


def solution(mesh):
    return jax.shard_map(
        body,
        mesh=mesh,
        in_specs=(
            P("ep", None),
            P("ep", None),
            P("ep", None),
            P("ep", None),
            P(),
            P(),
            P("ep", None, "tp"),
            P("ep", None, "tp"),
            P("ep", "tp", None),
        ),
        out_specs=(
            P("ep", "tp"),
            P("ep", "tp"),
            P("ep", None),
            P("ep", None, "tp"),
            P("ep", None, "tp"),
            P("ep", "tp", None),
        ),
        check_vma=False,
    )
```
